32 devices in a mesh: kv: 2 (over x), seq: 4 (over z), vocab: 4 (over y, core).
Axes of the slice: x: 2, y: 2, z: 4, core: 2. Of those that a mesh axis runs over, the one named last changes fastest.
Arguments:
- hidden_state: bfloat16 [48, 4, 3584], P('kv', 'vocab', 'seq'), may hold values from -6 to 6
- input_projection: bfloat16 [3584, 8, 1024], P('seq', 'kv'), may hold values from -0.09375 to 0.09375
- output_projection: bfloat16 [8, 512, 3584], P('kv', None, 'seq'), may hold values from -0.09375 to 0.09375
- norm_pre_attention: float32 [3584], P('seq'), may hold values from 0.1 to 1.9
- norm_post_attention: float32 [3584], P('seq'), may hold values from 0.1 to 1.9
- norm_pre_feedforward: float32 [3584], P('seq'), may hold values from 0.1 to 1.9
- norm_post_feedforward: float32 [3584], P('seq'), may hold values from 0.1 to 1.9
- norm_final: float32 [3584], P('seq'), may hold values from 0.1 to 1.9
- cache_keys: bfloat16 [4, 8192, 8, 256], P('vocab', 'seq', 'kv')
- cache_values: bfloat16 [4, 8192, 8, 256], P('vocab', 'seq', 'kv')
- cache_length: int32 [4], P('vocab'), may hold values from 1 to 8187, as said below
- ancestors: int32 [4, 48, 48], P('vocab'), may hold values from 0 to 1, as said below
- accepted_path: int32 [4, 5], P('vocab'), may hold values from 0 to 47, as said below
- gate_up_weight: bfloat16 [3584, 2, 14336], P('seq', None, ('kv', 'vocab')), may hold values from -0.09375 to 0.09375
- down_weight: bfloat16 [14336, 3584], P(('kv', 'vocab'), 'seq'), may hold values from -0.046875 to 0.046875
- draft_weight: bfloat16 [4, 3584, 3584], P(None, 'seq', ('kv', 'vocab')), may hold values from -0.09375 to 0.09375
- draft_bias: float32 [4, 3584], P(None, ('kv', 'vocab')), may hold values from -3 to 3
- vocab_weight: bfloat16 [16384, 3584], P(('kv', 'seq', 'vocab'))
- candidate_tokens: int32 [5, 48, 4, 8], replicated, may hold values from 0 to 16383
Outputs:
- keys_updated: bfloat16 [4, 8192, 8, 256], P('vocab', 'seq', 'kv')
- values_updated: bfloat16 [4, 8192, 8, 256], P('vocab', 'seq', 'kv')
- log_normalizer: float32 [5, 48, 4], replicated
- candidate_logits: float32 [5, 48, 4, 8], replicated
The draws below stay inside these ranges and needn't reach their ends.
Inputs may be any that keep to these rules, and one draw needn't show every extreme that they name: The first cache_length[k] slots of tenant k's cache are filled; in every draw some tenant holds exactly 8187. ancestors[k, t, u] is 1 exactly when u is t or an ancestor of t in tenant k's tree; node 0 is the root and every parent has a lower index than its child. accepted_path[k] lists 5 nodes of tenant k's tree from the root down, each the parent of the next; the last of them is node 47.
All inputs are finite; a program needn't handle non-finite values.
Results may differ from the reference program's by a relative error of at most 0.02.
Values may be sent and summed in bfloat16 or wider, within the bound.
No kernel may reach another device: no remote copies, remote signals or barrier semaphores. Data moves between devices by JAX's collectives and lax.ppermute only.
A program may use at most 128 MiB of HBM per device.

```python
import math
import jax
import jax.numpy as jnp
from jax import lax

MODEL_WIDTH = 3584
QUERY_HEADS = 16
KEY_VALUE_HEADS = 8
HEAD_SIZE = 256
FF = 14336
NDRAFT = 4
TREE_NODES = 48
ACCEPT = 5
CAND = 8
NHEAD = 5
TENANT_COUNT = 4
CACHE_SLOTS = 8192
V = 16384


def cache_field(key, salt):
    field_key = jax.random.fold_in(key, salt)
    noise_key, scale_random_key = jax.random.split(field_key, 2)
    array_shape = (TENANT_COUNT, CACHE_SLOTS, KEY_VALUE_HEADS, HEAD_SIZE)
    row_norm_scale = jnp.exp(jax.random.uniform(scale_random_key, (TENANT_COUNT, CACHE_SLOTS, KEY_VALUE_HEADS, 1), minval=-0.8, maxval=0.8))
    values = jax.random.normal(noise_key, array_shape) * row_norm_scale
    return jnp.clip(values, -8.0, 8.0).astype(jnp.bfloat16)


def draw_cache_keys(key, part):
    return cache_field(key, 101)


def draw_cache_values(key, part):
    return cache_field(key, 202)


def draw_vocab_weight(key, part):
    noise_key, scale_random_key = jax.random.split(jax.random.fold_in(key, 303), 2)
    row_norm_scale = 10.0 ** jax.random.uniform(scale_random_key, (V,))
    noise_part = jax.random.normal(noise_key, (V, MODEL_WIDTH))
    return (jnp.clip(noise_part * row_norm_scale[:, None], -30.0, 30.0) / math.sqrt(MODEL_WIDTH)).astype(jnp.bfloat16)


def draw_cache_length(key, part):
    first_key, second_key = jax.random.split(jax.random.fold_in(key, 404))
    lengths = jax.random.randint(first_key, (TENANT_COUNT,), 1, CACHE_SLOTS - ACCEPT + 1)
    longest = jax.random.randint(second_key, (), 0, TENANT_COUNT)
    return jnp.where(jnp.arange(TENANT_COUNT) == longest, CACHE_SLOTS - ACCEPT, lengths).astype(jnp.int32)


def tree_draw(key):
    backsteps = jax.random.randint(jax.random.fold_in(key, 505), (TENANT_COUNT, TREE_NODES), 0, 3)
    tree_nodes = jnp.arange(TREE_NODES, dtype=jnp.int32)
    parents = jnp.maximum(tree_nodes - 1 - jnp.minimum(backsteps, jnp.maximum(tree_nodes - 1, 0)), 0).astype(jnp.int32)
    parents = jnp.where(tree_nodes[None, :] <= ACCEPT - 2, jnp.maximum(tree_nodes - 1, 0)[None, :], parents).astype(jnp.int32)
    identity = (tree_nodes[:, None] == tree_nodes[None, :]).astype(jnp.int32)

    def build_tree(parent_row):

        def extend(node_index, ancestry):
            parent_line = lax.dynamic_index_in_dim(ancestry, parent_row[node_index], 0, True)
            self_line = lax.dynamic_index_in_dim(identity, node_index, 0, True)
            return lax.dynamic_update_slice(ancestry, jnp.maximum(parent_line, self_line), (node_index, jnp.int32(0)))
        ancestry = lax.fori_loop(1, TREE_NODES - 1, extend, identity)
        node_depth = jnp.sum(ancestry, axis=-1) - 1
        eligible = (node_depth == ACCEPT - 2) & (tree_nodes < TREE_NODES - 1)
        last_parent = jnp.max(jnp.where(eligible, tree_nodes, 0)).astype(jnp.int32)
        parent_line = lax.dynamic_index_in_dim(ancestry, last_parent, 0, True)
        self_line = identity[TREE_NODES - 1:TREE_NODES]
        return lax.dynamic_update_slice(ancestry, jnp.maximum(parent_line, self_line), (jnp.int32(TREE_NODES - 1), jnp.int32(0)))
    ancestry = jax.vmap(build_tree)(parents)
    deepest = ancestry[:, TREE_NODES - 1, :]
    ranking = jnp.argsort((1 - deepest) * TREE_NODES + tree_nodes[None, :], axis=-1, stable=True)
    return (ancestry.astype(jnp.int32), ranking[:, :ACCEPT].astype(jnp.int32))


def draw_ancestors(key, part):
    return tree_draw(key)[0]


def draw_accepted_path(key, part):
    return tree_draw(key)[1]


def plant(result, stream_key, smallest, largest):
    spot = [jax.random.randint(jax.random.fold_in(stream_key, axis), (), 0, length) for axis, length in enumerate(result.shape)]
    widest = result.shape.index(max(result.shape))
    neighbour = spot[:widest] + [(spot[widest] + 1) % result.shape[widest]] + spot[widest + 1:]
    return result.at[tuple(spot)].set(smallest).at[tuple(neighbour)].set(largest)


def steps_of(key, shape, cuts, low, high):
    loudness, own = 1.0, jax.random.fold_in(key, 6)
    for position, shards_of in cuts:
        heights = jnp.exp(jax.random.uniform(jax.random.fold_in(own, position), (shards_of,), jnp.float32, low / len(cuts), high / len(cuts)))
        loudness = loudness * jnp.repeat(heights, shape[position] // shards_of).reshape([-1 if axis == position else 1 for axis in range(len(shape))])
    return loudness


def scatter_about(key, dims, width, bound, cuts=(), kind=jnp.bfloat16):
    result = width * jax.random.normal(key, dims, jnp.float32)
    if cuts:
        result = result * steps_of(key, dims, cuts, -0.22, 0.18)
    return jnp.clip(result, -bound, bound).astype(kind)


def setup_inputs(seed: int = 0) -> dict:
    key_list = jax.random.split(jax.random.key(seed), 20)
    hidden_state = scatter_about(key_list[0], (TREE_NODES, TENANT_COUNT, MODEL_WIDTH), 1.0, 6.0, ((0, 2), (1, 4), (2, 4)))
    input_projection = scatter_about(key_list[1], (MODEL_WIDTH, KEY_VALUE_HEADS, 4 * HEAD_SIZE), MODEL_WIDTH ** -0.5, 0.09375, ((0, 4), (1, 2)))
    output_projection = scatter_about(key_list[2], (KEY_VALUE_HEADS, 2 * HEAD_SIZE, MODEL_WIDTH), (QUERY_HEADS * HEAD_SIZE) ** -0.5, 0.09375, ((0, 2), (2, 4)))
    norm_pre_attention = jnp.clip(1.0 + 0.18 * jax.random.normal(key_list[3], (MODEL_WIDTH,), jnp.float32), 0.1, 1.9)
    norm_post_attention = jnp.clip(1.0 + 0.18 * jax.random.normal(key_list[4], (MODEL_WIDTH,), jnp.float32), 0.1, 1.9)
    norm_pre_feedforward = jnp.clip(1.0 + 0.18 * jax.random.normal(key_list[5], (MODEL_WIDTH,), jnp.float32), 0.1, 1.9)
    norm_post_feedforward = jnp.clip(1.0 + 0.18 * jax.random.normal(key_list[6], (MODEL_WIDTH,), jnp.float32), 0.1, 1.9)
    norm_final = jnp.clip(1.0 + 0.18 * jax.random.normal(key_list[7], (MODEL_WIDTH,), jnp.float32), 0.1, 1.9)
    cache_keys = draw_cache_keys(jax.random.fold_in(key_list[19], 71), 0)
    cache_values = draw_cache_values(jax.random.fold_in(key_list[19], 71), 0)
    cache_length = draw_cache_length(jax.random.fold_in(key_list[19], 71), 0)
    ancestors = draw_ancestors(jax.random.fold_in(key_list[19], 71), 0)
    accepted_path = draw_accepted_path(jax.random.fold_in(key_list[19], 71), 0)
    gate_up_weight = scatter_about(key_list[13], (MODEL_WIDTH, 2, FF), MODEL_WIDTH ** -0.5, 0.09375, ((0, 4), (2, 8)))
    down_weight = scatter_about(key_list[14], (FF, MODEL_WIDTH), FF ** -0.5, 0.046875, ((0, 8), (1, 4)))
    draft_weight = scatter_about(key_list[15], (NDRAFT, MODEL_WIDTH, MODEL_WIDTH), MODEL_WIDTH ** -0.5, 0.09375, ((1, 4), (2, 8)))
    draft_bias = scatter_about(key_list[16], (NDRAFT, MODEL_WIDTH), 0.5, 3.0, ((1, 8),), jnp.float32)
    vocab_weight = draw_vocab_weight(jax.random.fold_in(key_list[19], 71), 0)
    candidate_tokens = plant(jax.random.randint(key_list[18], (NHEAD, TREE_NODES, TENANT_COUNT, CAND), 0, V), jax.random.fold_in(key_list[18], 1), 0, V - 1).astype(jnp.int32)
    return dict(hidden_state=hidden_state, input_projection=input_projection, output_projection=output_projection, norm_pre_attention=norm_pre_attention, norm_post_attention=norm_post_attention, norm_pre_feedforward=norm_pre_feedforward, norm_post_feedforward=norm_post_feedforward, norm_final=norm_final, cache_keys=cache_keys, cache_values=cache_values, cache_length=cache_length, ancestors=ancestors, accepted_path=accepted_path, gate_up_weight=gate_up_weight, down_weight=down_weight, draft_weight=draft_weight, draft_bias=draft_bias, vocab_weight=vocab_weight, candidate_tokens=candidate_tokens)


EPSILON = 1e-06
SCORE_CAP = 50.0
LOGIT_CAP = 30.0

def inverse_square_root(values):
    return lax.rsqrt(lax.optimization_barrier(jnp.mean(values * values, axis=-1, keepdims=True)) + EPSILON)

def apply_rotary(vectors, token_positions):
    half_dim = vectors.shape[-1] // 2
    frequency = 10000.0 ** (-2.0 * jnp.arange(half_dim, dtype=jnp.float32) / vectors.shape[-1])
    angles = token_positions.astype(jnp.float32)[..., None] * frequency
    cosine = jnp.cos(angles)
    sine_part = jnp.sin(angles)
    first_half = vectors[..., :half_dim]
    second_half = vectors[..., half_dim:]
    return jnp.concatenate([first_half * cosine - second_half * sine_part, second_half * cosine + first_half * sine_part], axis=-1)

def capped_weight(scores):
    return jnp.exp(SCORE_CAP * jnp.tanh(scores * 0.0625 / SCORE_CAP))

def attend_tenant(query_rows, keys_all, values_all, new_keys, new_values, length, ancestry):
    query_float = query_rows.astype(jnp.float32)
    scores = jnp.einsum('thgc,shc->thgs', query_float, keys_all.astype(jnp.float32))
    filled = jnp.arange(keys_all.shape[0], dtype=jnp.int32) < length
    weights = jnp.where(filled[None, None, None, :], capped_weight(scores), 0.0)
    tree_scores = jnp.einsum('thgc,uhc->thgu', query_float, new_keys.astype(jnp.float32))
    tree_weights = jnp.where(ancestry[:, None, None, :] > 0, capped_weight(tree_scores), 0.0)
    denominator = lax.optimization_barrier(jnp.sum(weights, axis=-1)) + lax.optimization_barrier(jnp.sum(tree_weights, axis=-1))
    rounded = lax.optimization_barrier(weights.astype(jnp.bfloat16)).astype(jnp.float32)
    tree_rounded = lax.optimization_barrier(tree_weights.astype(jnp.bfloat16)).astype(jnp.float32)
    numerator = jnp.einsum('thgs,shc->thgc', rounded, values_all.astype(jnp.float32))
    numerator = numerator + jnp.einsum('thgu,uhc->thgc', tree_rounded, new_values.astype(jnp.float32))
    return (numerator / denominator[..., None]).astype(jnp.bfloat16)

def reference(hidden_state, input_projection, output_projection, norm_pre_attention, norm_post_attention, norm_pre_feedforward, norm_post_feedforward, norm_final, cache_keys, cache_values, cache_length, ancestors, accepted_path, gate_up_weight, down_weight, draft_weight, draft_bias, vocab_weight, candidate_tokens):
    all_rows = TREE_NODES * TENANT_COUNT
    residual_stream = hidden_state.astype(jnp.float32)
    depths = lax.optimization_barrier(jnp.sum(ancestors, axis=-1)).astype(jnp.int32) - 1
    token_positions = jnp.transpose(cache_length[:, None] + depths)
    scaled_input = (residual_stream * norm_pre_attention).astype(jnp.bfloat16).reshape(all_rows, MODEL_WIDTH)
    projected_rows = jnp.dot(scaled_input, input_projection.reshape(MODEL_WIDTH, KEY_VALUE_HEADS * 4 * HEAD_SIZE), preferred_element_type=jnp.float32)
    projected_rows = projected_rows.reshape(TREE_NODES, TENANT_COUNT, KEY_VALUE_HEADS, 4 * HEAD_SIZE) * inverse_square_root(residual_stream)[..., None]
    query_rows = apply_rotary(projected_rows[..., :2 * HEAD_SIZE].reshape(TREE_NODES, TENANT_COUNT, KEY_VALUE_HEADS, 2, HEAD_SIZE), token_positions[:, :, None, None]).astype(jnp.bfloat16)
    new_keys = apply_rotary(projected_rows[..., 2 * HEAD_SIZE:3 * HEAD_SIZE], token_positions[:, :, None]).astype(jnp.bfloat16)
    new_values = projected_rows[..., 3 * HEAD_SIZE:].astype(jnp.bfloat16)
    outputs = []
    for tenant in range(TENANT_COUNT):
        outputs.append(attend_tenant(query_rows[:, tenant], cache_keys[tenant], cache_values[tenant], new_keys[:, tenant], new_values[:, tenant], cache_length[tenant], ancestors[tenant]))
    attended = jnp.stack(outputs, axis=1).reshape(all_rows, QUERY_HEADS * HEAD_SIZE)
    attention_out = jnp.dot(attended, output_projection.reshape(QUERY_HEADS * HEAD_SIZE, MODEL_WIDTH), preferred_element_type=jnp.float32)
    flat_residual = residual_stream.reshape(all_rows, MODEL_WIDTH)
    first_sum = (flat_residual + attention_out * inverse_square_root(attention_out) * norm_post_attention).astype(jnp.bfloat16)
    first_float = first_sum.astype(jnp.float32)
    scaled_ffn = (first_float * norm_pre_feedforward).astype(jnp.bfloat16)
    gate_up = jnp.dot(scaled_ffn, gate_up_weight.reshape(MODEL_WIDTH, 2 * FF), preferred_element_type=jnp.float32) * inverse_square_root(first_float)
    activated = (jax.nn.gelu(gate_up[:, :FF], approximate=True) * gate_up[:, FF:]).astype(jnp.bfloat16)
    ffn_out = jnp.dot(activated, down_weight, preferred_element_type=jnp.float32)
    second_sum = (first_float + ffn_out * inverse_square_root(ffn_out) * norm_post_feedforward).astype(jnp.bfloat16)
    second_float = second_sum.astype(jnp.float32)
    normed = (second_float * inverse_square_root(second_float) * norm_final).astype(jnp.bfloat16)
    branches = []
    for draft_index in range(NDRAFT):
        lifted = jnp.dot(normed, draft_weight[draft_index], preferred_element_type=jnp.float32) + draft_bias[draft_index]
        branches.append(jax.nn.silu(lifted).astype(jnp.bfloat16))
    branch = jnp.stack(branches, axis=0).reshape(NDRAFT * all_rows, MODEL_WIDTH)
    candidates = candidate_tokens.reshape(NHEAD, all_rows, CAND)
    piece_count = 64
    piece_rows = V // piece_count
    stacked = vocab_weight.reshape(piece_count, piece_rows, MODEL_WIDTH)
    offsets = jnp.arange(piece_count, dtype=jnp.int32) * piece_rows

    def scan_piece(running, inputs):
        totals, picked = running
        matrix, offset = inputs
        base_logits = lax.dot_general(normed, matrix, (((1,), (1,)), ((), ())), preferred_element_type=jnp.float32)
        draft_extra = lax.dot_general(branch, matrix, (((1,), (1,)), ((), ())), preferred_element_type=jnp.float32)
        draft_extra = draft_extra.reshape(NDRAFT, all_rows, piece_rows)
        raw_logits = jnp.concatenate([base_logits[None], base_logits[None] + draft_extra], axis=0)
        logits = LOGIT_CAP * jnp.tanh(raw_logits / LOGIT_CAP)
        totals = totals + lax.optimization_barrier(jnp.sum(jnp.exp(logits), axis=-1))
        columns = offset + jnp.arange(piece_rows, dtype=jnp.int32)
        matches = candidates[..., None] == columns
        picked = picked + lax.optimization_barrier(jnp.sum(jnp.where(matches, logits[:, :, None, :], 0.0), axis=-1))
        return ((totals, picked), None)
    start_state = (jnp.zeros((NHEAD, all_rows), jnp.float32), jnp.zeros((NHEAD, all_rows, CAND), jnp.float32))
    (totals, picked), _ = lax.scan(scan_piece, start_state, (stacked, offsets))
    log_normalizer = jnp.log(totals).reshape(NHEAD, TREE_NODES, TENANT_COUNT)
    candidate_logits = picked.reshape(NHEAD, TREE_NODES, TENANT_COUNT, CAND)
    tenant_index = jnp.arange(TENANT_COUNT, dtype=jnp.int32)[:, None]
    keys_tenant = jnp.transpose(new_keys, (1, 0, 2, 3))
    values_tenant = jnp.transpose(new_values, (1, 0, 2, 3))
    chosen_keys = keys_tenant[tenant_index, accepted_path]
    chosen_values = values_tenant[tenant_index, accepted_path]
    slot_rows = cache_length[:, None] + jnp.arange(ACCEPT, dtype=jnp.int32)
    keys_updated = cache_keys.at[tenant_index, slot_rows].set(chosen_keys)
    values_updated = cache_values.at[tenant_index, slot_rows].set(chosen_values)
    return (keys_updated, values_updated, log_normalizer, candidate_logits)
```

```python
import jax
import jax.numpy as jnp
from jax import lax
from jax.sharding import PartitionSpec as P

MODEL_WIDTH = 3584
HEAD_SIZE = 256
CAND = 8


EPSILON = 1e-06
SCORE_CAP = 50.0
LOGIT_CAP = 30.0


def apply_rotary(vectors, token_positions):
    half_dim = vectors.shape[-1] // 2
    frequency = 10000.0 ** (-2.0 * jnp.arange(half_dim, dtype=jnp.float32) / vectors.shape[-1])
    angles = token_positions.astype(jnp.float32)[..., None] * frequency
    cosine = jnp.cos(angles)
    sine_part = jnp.sin(angles)
    first_half = vectors[..., :half_dim]
    second_half = vectors[..., half_dim:]
    return jnp.concatenate(
        [
            first_half * cosine - second_half * sine_part,
            second_half * cosine + first_half * sine_part,
        ],
        axis=-1,
    )


def capped_weight(scores):
    return jnp.exp(SCORE_CAP * jnp.tanh(scores * 0.0625 / SCORE_CAP))


def row_inverse(values):
    totals = lax.psum(jnp.sum(values * values, axis=-1), "seq")
    return lax.rsqrt(totals / MODEL_WIDTH + EPSILON)[:, None]


def gated_units(gate_up, squares):
    inverse = lax.rsqrt(squares / MODEL_WIDTH + EPSILON)[:, None]
    return (
        jax.nn.gelu(gate_up[:, 0] * inverse, approximate=True) * (gate_up[:, 1] * inverse)
    ).astype(jnp.bfloat16)


def local_general(
    hidden_state,
    input_projection,
    output_projection,
    norm_pre_attention,
    norm_post_attention,
    norm_pre_feedforward,
    norm_post_feedforward,
    norm_final,
    cache_keys,
    cache_values,
    cache_length,
    ancestors,
    accepted_path,
    gate_up_weight,
    down_weight,
    draft_weight,
    draft_bias,
    vocab_weight,
    candidate_tokens,
):
    tok_block = hidden_state.shape[0]
    kv_count = lax.axis_size("kv")
    tenants = lax.axis_size("vocab")
    tree_size = tok_block * kv_count
    own_state = hidden_state[:, 0, :]
    tenant_state = lax.all_gather(own_state, "kv", axis=0, tiled=True)
    tenant_float = tenant_state.astype(jnp.float32)
    scaled_input = (tenant_float * norm_pre_attention).astype(jnp.bfloat16)
    projected_rows = jnp.einsum(
        "td,dhc->thc", scaled_input, input_projection, preferred_element_type=jnp.float32
    )
    projected_rows, squares = lax.psum(
        (projected_rows, jnp.sum(tenant_float * tenant_float, axis=-1)), "seq"
    )
    projected_rows = projected_rows * lax.rsqrt(squares / MODEL_WIDTH + EPSILON)[:, None, None]
    head_count = projected_rows.shape[1]
    depths = jnp.sum(ancestors[0], axis=-1) - 1
    length = cache_length[0]
    token_positions = length + depths
    query_rows = apply_rotary(
        projected_rows[:, :, : 2 * HEAD_SIZE].reshape(tree_size, head_count, 2, HEAD_SIZE),
        token_positions[:, None, None],
    ).astype(jnp.bfloat16)
    new_keys = apply_rotary(
        projected_rows[:, :, 2 * HEAD_SIZE : 3 * HEAD_SIZE], token_positions[:, None]
    ).astype(jnp.bfloat16)
    new_values = projected_rows[:, :, 3 * HEAD_SIZE :].astype(jnp.bfloat16)
    block_size = cache_keys.shape[1]
    block_start = lax.axis_index("seq") * block_size
    cache_cells = block_start + jnp.arange(block_size, dtype=jnp.int32)
    scores = jnp.einsum(
        "thgc,shc->thgs", query_rows, cache_keys[0], preferred_element_type=jnp.float32
    )
    weights = jnp.where((cache_cells < length)[None, None, None, :], capped_weight(scores), 0.0)
    numerator = jnp.einsum(
        "thgs,shc->thgc",
        weights.astype(jnp.bfloat16),
        cache_values[0],
        preferred_element_type=jnp.float32,
    )
    numerator, denominator = lax.psum((numerator, jnp.sum(weights, axis=-1)), "seq")
    tree_scores = jnp.einsum(
        "thgc,uhc->thgu", query_rows, new_keys, preferred_element_type=jnp.float32
    )
    tree_weights = jnp.where(ancestors[0][:, None, None, :] > 0, capped_weight(tree_scores), 0.0)
    numerator = numerator + jnp.einsum(
        "thgu,uhc->thgc",
        tree_weights.astype(jnp.bfloat16),
        new_values,
        preferred_element_type=jnp.float32,
    )
    denominator = denominator + jnp.sum(tree_weights, axis=-1)
    attended = (
        (numerator / denominator[..., None])
        .astype(jnp.bfloat16)
        .reshape(tree_size, head_count * 2 * HEAD_SIZE)
    )
    out_matrix = output_projection.reshape(head_count * 2 * HEAD_SIZE, output_projection.shape[2])
    attention_out = lax.psum_scatter(
        jnp.dot(attended, out_matrix, preferred_element_type=jnp.float32),
        "kv",
        scatter_dimension=0,
        tiled=True,
    )
    first_sum = (
        own_state.astype(jnp.float32)
        + attention_out * row_inverse(attention_out) * norm_post_attention
    ).astype(jnp.bfloat16)
    all_state = lax.all_gather(first_sum, ("kv", "vocab"), axis=0, tiled=True)
    all_float = all_state.astype(jnp.float32)
    scaled_ffn = (all_float * norm_pre_feedforward).astype(jnp.bfloat16)
    gate_up = jnp.einsum(
        "td,dcf->tcf", scaled_ffn, gate_up_weight, preferred_element_type=jnp.float32
    )
    ffn_squares = jnp.sum(all_float * all_float, axis=-1)
    gate_up, ffn_squares = lax.psum((gate_up, ffn_squares), "seq")
    activated = gated_units(gate_up, ffn_squares)
    ffn_out = lax.psum_scatter(
        jnp.dot(activated, down_weight, preferred_element_type=jnp.float32),
        ("kv", "vocab"),
        scatter_dimension=0,
        tiled=True,
    )
    first_float = first_sum.astype(jnp.float32)
    second_sum = (first_float + ffn_out * row_inverse(ffn_out) * norm_post_feedforward).astype(
        jnp.bfloat16
    )
    second_float = second_sum.astype(jnp.float32)
    normed = (second_float * row_inverse(second_float) * norm_final).astype(jnp.bfloat16)
    gathered = lax.all_gather(normed, ("kv", "vocab"), axis=0, tiled=True)
    lifted = jnp.einsum("td,ndc->tnc", gathered, draft_weight, preferred_element_type=jnp.float32)
    lifted = lax.psum(lifted.astype(jnp.bfloat16), "seq").astype(jnp.float32)
    branch = jax.nn.silu(lifted + draft_bias).astype(jnp.bfloat16)
    row_count = gathered.shape[0]
    vocab_rows = vocab_weight.shape[0]
    draft_count = branch.shape[1]
    columns = vocab_weight
    base_logits = lax.dot_general(
        lax.all_gather(gathered, "seq", axis=1, tiled=True),
        columns,
        (((1,), (1,)), ((), ())),
        preferred_element_type=jnp.float32,
    )
    columns = vocab_weight
    draft_extra = jnp.einsum(
        "tnc,vc->tnv",
        lax.all_gather(branch, ("kv", "vocab"), axis=2, tiled=True),
        columns,
        preferred_element_type=jnp.float32,
    )
    raw_logits = jnp.concatenate(
        [base_logits[:, None, :], base_logits[:, None, :] + draft_extra], axis=1
    )
    logits = LOGIT_CAP * jnp.tanh(raw_logits / LOGIT_CAP)
    totals = jnp.sum(jnp.exp(logits), axis=-1)
    head_total = draft_count + 1
    candidates = candidate_tokens.reshape(head_total, kv_count, tok_block, tenants, CAND)
    candidates = jnp.transpose(candidates, (0, 1, 3, 2, 4)).reshape(head_total, row_count, CAND)
    candidates = jnp.transpose(candidates, (1, 0, 2))
    vocab_start = lax.axis_index(("kv", "seq", "vocab")) * vocab_rows
    local_tokens = candidates - vocab_start
    entry_index = jnp.arange(vocab_rows, dtype=jnp.int32)
    picked = jnp.stack(
        [
            jnp.sum(
                jnp.where(entry_index == local_tokens[:, :, column : column + 1], logits, 0.0),
                axis=-1,
            )
            for column in range(CAND)
        ],
        axis=-1,
    )
    totals, picked = lax.psum((totals, picked), ("kv", "seq", "vocab"))
    log_totals = jnp.transpose(jnp.log(totals)).reshape(head_total, kv_count, tenants, tok_block)
    log_normalizer = jnp.transpose(log_totals, (0, 1, 3, 2)).reshape(head_total, tree_size, tenants)
    picked = jnp.transpose(picked, (1, 0, 2)).reshape(
        head_total, kv_count, tenants, tok_block, CAND
    )
    candidate_logits = jnp.transpose(picked, (0, 1, 3, 2, 4)).reshape(
        head_total, tree_size, tenants, CAND
    )
    accept_count = accepted_path.shape[1]
    slot_rows = length + jnp.arange(accept_count, dtype=jnp.int32)
    tree_nodes = jnp.arange(tree_size, dtype=jnp.int32)
    matches = (cache_cells[:, None, None] == slot_rows[None, :, None]) & (
        accepted_path[0][None, :, None] == tree_nodes[None, None, :]
    )
    selector = jnp.sum(matches.astype(jnp.float32), axis=1)
    written = jnp.sum(selector, axis=-1) > 0.0
    selector = selector.astype(jnp.bfloat16)

    def write_path(old_block, fresh_rows):
        moved_rows = jnp.dot(
            selector, fresh_rows.reshape(tree_size, -1), preferred_element_type=jnp.float32
        ).astype(jnp.bfloat16)
        return jnp.where(
            written[:, None], moved_rows, old_block[0].reshape(block_size, -1)
        ).reshape(old_block.shape)

    keys_updated = write_path(cache_keys, new_keys)
    values_updated = write_path(cache_values, new_values)
    return (keys_updated, values_updated, log_normalizer, candidate_logits)


def split_pair(values):
    high = values.astype(jnp.bfloat16)
    low = (values - high.astype(jnp.float32)).astype(jnp.bfloat16)
    return high, low


def send_back(blocks):
    count = lax.axis_size("seq")
    return [
        lax.ppermute(blocks[j], "seq", [(i, (i - j) % count) for i in range(count)])
        for j in range(1, count)
    ]


def collect(block):
    count = lax.axis_size("seq")
    return [block] + [
        lax.ppermute(block, "seq", [(i, (i + j) % count) for i in range(count)])
        for j in range(1, count)
    ]


def token_totals(values):
    parts = collect(values)
    total = parts[0]
    for j in range(1, len(parts)):
        total = total + jnp.roll(parts[j], j, axis=0)
    return total


def kv_swap(values):
    return lax.ppermute(values, "kv", [(0, 1), (1, 0)])


def inverse_of(totals):
    return lax.rsqrt(totals / MODEL_WIDTH + EPSILON)


def local(
    hidden_state,
    input_projection,
    output_projection,
    norm_pre_attention,
    norm_post_attention,
    norm_pre_feedforward,
    norm_post_feedforward,
    norm_final,
    cache_keys,
    cache_values,
    cache_length,
    ancestors,
    accepted_path,
    gate_up_weight,
    down_weight,
    draft_weight,
    draft_bias,
    vocab_weight,
    candidate_tokens,
):
    f32, bf16 = jnp.float32, jnp.bfloat16
    tok_block = hidden_state.shape[0]
    seq_count = lax.axis_size("seq")
    kv_count = lax.axis_size("kv")
    tenants = lax.axis_size("vocab")
    groups = kv_count * tenants
    sub = tok_block // seq_count
    tree_size = tok_block * kv_count
    chunk = kv_count * sub
    width = hidden_state.shape[2]
    head_count = input_projection.shape[1]
    seq_at = lax.axis_index("seq")
    kv_at = lax.axis_index("kv")
    back = (seq_at - jnp.arange(seq_count, dtype=jnp.int32)) % seq_count
    own_state = jnp.stack(
        [
            lax.dynamic_slice_in_dim(hidden_state[:, 0, :], back[j] * sub, sub, 0)
            for j in range(seq_count)
        ]
    )
    other_state = kv_swap(own_state)
    tenant_state = jnp.stack([own_state, other_state], axis=1).reshape(tree_size, width)
    tenant_float = tenant_state.astype(f32)
    scaled_input = (tenant_float * norm_pre_attention).astype(bf16)
    projected = jnp.einsum(
        "td,dhc->thc", scaled_input, input_projection, preferred_element_type=f32
    ).reshape(seq_count, chunk, head_count * 4 * HEAD_SIZE)
    square_high, square_low = split_pair(
        jnp.sum(tenant_float * tenant_float, axis=-1).reshape(seq_count, chunk, 1)
    )
    packed = jnp.concatenate(
        [
            projected.astype(bf16),
            jnp.broadcast_to(square_high, (seq_count, chunk, 64)),
            jnp.broadcast_to(square_low, (seq_count, chunk, 64)),
        ],
        axis=-1,
    )
    arrived = send_back(packed)
    columns = head_count * 4 * HEAD_SIZE
    summed = packed[0].astype(f32)
    for part in arrived:
        summed = summed + part.astype(f32)
    squares = summed[:, columns : columns + 1] + summed[:, columns + 64 : columns + 65]
    rows = (summed[:, :columns] * inverse_of(squares)).reshape(chunk, head_count, 4 * HEAD_SIZE)
    kv_order = kv_at ^ jnp.arange(kv_count, dtype=jnp.int32)
    node_of = (
        kv_order[None, :, None] * tok_block
        + back[:, None, None] * sub
        + jnp.arange(sub, dtype=jnp.int32)[None, None, :]
    ).reshape(tree_size)
    node_pick = (node_of[:, None] == jnp.arange(tree_size, dtype=jnp.int32)[None, :]).astype(f32)
    tree_mask = jnp.einsum(
        "tu,uv,wv->tw",
        node_pick[:chunk],
        ancestors[0].astype(f32),
        node_pick,
    )
    depths = jnp.sum(tree_mask, axis=-1).astype(jnp.int32) - 1
    length = cache_length[0]
    token_positions = length + depths
    queries = apply_rotary(
        rows[:, :, : 2 * HEAD_SIZE].reshape(chunk, head_count, 2, HEAD_SIZE),
        token_positions[:, None, None],
    ).astype(bf16)
    own_keys = apply_rotary(
        rows[:, :, 2 * HEAD_SIZE : 3 * HEAD_SIZE], token_positions[:, None]
    ).astype(bf16)
    own_values = rows[:, :, 3 * HEAD_SIZE :].astype(bf16)
    query_rows = jnp.concatenate(
        collect(queries.reshape(chunk, head_count * 2 * HEAD_SIZE)), axis=0
    ).reshape(tree_size, head_count, 2, HEAD_SIZE)
    fresh = jnp.concatenate(
        collect(
            jnp.concatenate(
                [
                    own_keys.reshape(chunk, head_count * HEAD_SIZE),
                    own_values.reshape(chunk, head_count * HEAD_SIZE),
                ],
                axis=1,
            )
        ),
        axis=0,
    )
    new_keys = fresh[:, : head_count * HEAD_SIZE].reshape(tree_size, head_count, HEAD_SIZE)
    new_values = fresh[:, head_count * HEAD_SIZE :].reshape(tree_size, head_count, HEAD_SIZE)
    block_size = cache_keys.shape[1]
    block_start = seq_at * block_size
    cache_cells = block_start + jnp.arange(block_size, dtype=jnp.int32)
    scores = jnp.einsum(
        "thgc,shc->thgs", query_rows, cache_keys[0], preferred_element_type=f32
    )
    weights = jnp.where((cache_cells < length)[None, None, None, :], capped_weight(scores), 0.0)
    numerator = jnp.einsum(
        "thgs,shc->thgc",
        weights.astype(bf16),
        cache_values[0],
        preferred_element_type=f32,
    ).reshape(seq_count, chunk, head_count * 2 * HEAD_SIZE)
    pairs = head_count * 2
    sum_high, sum_low = split_pair(
        jnp.sum(weights, axis=-1).reshape(seq_count, chunk, pairs)
    )
    packed = jnp.concatenate(
        [
            numerator.astype(bf16),
            sum_high,
            sum_low,
            jnp.zeros((seq_count, chunk, 128 - 2 * pairs), bf16),
        ],
        axis=-1,
    )
    arrived = send_back(packed)
    tree_scores = jnp.einsum("thgc,uhc->thgu", queries, new_keys, preferred_element_type=f32)
    tree_weights = jnp.where(tree_mask[:, None, None, :] > 0, capped_weight(tree_scores), 0.0)
    tree_numerator = jnp.einsum(
        "thgu,uhc->thgc", tree_weights.astype(bf16), new_values, preferred_element_type=f32
    )
    summed = packed[0].astype(f32)
    for part in arrived:
        summed = summed + part.astype(f32)
    columns = pairs * HEAD_SIZE
    denominator = (
        summed[:, columns : columns + pairs] + summed[:, columns + pairs : columns + 2 * pairs]
    ).reshape(chunk, head_count, 2) + jnp.sum(tree_weights, axis=-1)
    numerator = summed[:, :columns].reshape(chunk, head_count, 2, HEAD_SIZE) + tree_numerator
    attended = (numerator / denominator[..., None]).astype(bf16).reshape(chunk, columns)
    attended = jnp.concatenate(collect(attended), axis=0)
    out_matrix = output_projection.reshape(columns, width)
    attention_out = jnp.dot(attended, out_matrix, preferred_element_type=f32).reshape(
        seq_count, kv_count, sub, width
    )
    attention_out = attention_out[:, 0] + kv_swap(attention_out[:, 1].astype(bf16)).astype(f32)
    totals = token_totals(jnp.sum(attention_out * attention_out, axis=-1))
    first_sum = (
        own_state.astype(f32) + attention_out * inverse_of(totals)[..., None] * norm_post_attention
    ).astype(bf16)

    def gather_tokens(values):
        everyone = lax.all_gather(
            values.reshape(tok_block, width), ("kv", "vocab"), axis=0, tiled=True
        )
        return (
            everyone.reshape(groups, seq_count, sub, width)
            .transpose(1, 0, 2, 3)
            .reshape(groups * tok_block, width)
        )

    all_state = gather_tokens(first_sum)
    all_float = all_state.astype(f32)
    share = groups * sub
    scaled_ffn = (all_float * norm_pre_feedforward).astype(bf16)
    ffn_squares = jnp.sum(all_float * all_float, axis=-1).reshape(seq_count, share)
    squares = ffn_squares[0]
    for part in send_back(ffn_squares):
        squares = squares + part
    units = down_weight.shape[0]
    pieces = 2
    piece = units // pieces
    inverse = inverse_of(squares)[:, None]
    ffn_out = 0.0
    for p in range(pieces):
        window = slice(p * piece, (p + 1) * piece)
        partial = jnp.einsum(
            "td,dcf->ctf", scaled_ffn, gate_up_weight[:, :, window], preferred_element_type=f32
        )
        partial = partial.astype(bf16).reshape(2, seq_count, share, piece).transpose(1, 0, 2, 3)
        summed = partial[0].astype(f32)
        for part in send_back(partial):
            summed = summed + part.astype(f32)
        activated = (
            jax.nn.gelu(summed[0] * inverse, approximate=True) * (summed[1] * inverse)
        ).astype(bf16)
        activated = jnp.concatenate(collect(activated), axis=0)
        ffn_out = ffn_out + jnp.dot(
            activated, down_weight[window], preferred_element_type=f32
        )
    ffn_out = (
        ffn_out.astype(bf16)
        .reshape(seq_count, groups, sub, width)
        .transpose(1, 0, 2, 3)
    )
    ffn_out = lax.all_to_all(ffn_out, ("kv", "vocab"), 0, 0)
    ffn_out = jnp.sum(ffn_out.astype(f32), axis=0)
    totals = token_totals(jnp.sum(ffn_out * ffn_out, axis=-1))
    second_sum = (
        first_sum.astype(f32) + ffn_out * inverse_of(totals)[..., None] * norm_post_feedforward
    ).astype(bf16)
    second_float = second_sum.astype(f32)
    totals = token_totals(jnp.sum(second_float * second_float, axis=-1))
    normed = (second_float * inverse_of(totals)[..., None] * norm_final).astype(bf16)
    gathered = gather_tokens(normed)
    draft_count = draft_weight.shape[0]
    draft_columns = draft_weight.shape[2]
    lifted = jnp.einsum("td,ndc->tnc", gathered, draft_weight, preferred_element_type=f32)
    lifted = lifted.astype(bf16).reshape(seq_count, share, draft_count, draft_columns)
    summed = lifted[0].astype(f32)
    for part in send_back(lifted):
        summed = summed + part.astype(f32)
    branch = jax.nn.silu(summed + draft_bias).astype(bf16)
    row_count = groups * tok_block
    branch = jnp.concatenate(collect(branch), axis=0)
    vocab_rows = vocab_weight.shape[0]
    straight = jnp.concatenate(
        [
            lax.dynamic_slice_in_dim(gathered, back[j] * share, share, 0)
            for j in range(seq_count)
        ],
        axis=0,
    )
    whole = lax.all_gather(straight, "seq", axis=1, tiled=True)
    whole = jnp.concatenate(
        [
            lax.dynamic_slice_in_dim(whole, back[j] * share, share, 0)
            for j in range(seq_count)
        ],
        axis=0,
    )
    base_logits = lax.dot_general(
        whole, vocab_weight, (((1,), (1,)), ((), ())), preferred_element_type=f32
    )
    draft_extra = jnp.einsum(
        "tnc,vc->tnv",
        lax.all_gather(branch, ("kv", "vocab"), axis=2, tiled=True),
        vocab_weight,
        preferred_element_type=f32,
    )
    raw_logits = jnp.concatenate(
        [base_logits[:, None, :], base_logits[:, None, :] + draft_extra], axis=1
    )
    logits = LOGIT_CAP * jnp.tanh(raw_logits / LOGIT_CAP)
    totals = jnp.sum(jnp.exp(logits), axis=-1)
    head_total = draft_count + 1
    candidates = candidate_tokens.reshape(head_total, kv_count, seq_count, sub, tenants, CAND)
    candidates = jnp.transpose(candidates, (2, 1, 4, 3, 0, 5)).reshape(
        seq_count, share, head_total, CAND
    )
    candidates = jnp.concatenate(
        [lax.dynamic_slice_in_dim(candidates, back[j], 1, 0) for j in range(seq_count)], axis=0
    ).reshape(row_count, head_total, CAND)
    vocab_start = lax.axis_index(("kv", "seq", "vocab")) * vocab_rows
    local_tokens = candidates - vocab_start
    entry_index = jnp.arange(vocab_rows, dtype=jnp.int32)
    picked = jnp.stack(
        [
            jnp.sum(
                jnp.where(entry_index == local_tokens[:, :, column : column + 1], logits, 0.0),
                axis=-1,
            )
            for column in range(CAND)
        ],
        axis=-1,
    )
    tally = jnp.concatenate([totals[..., None], picked], axis=-1).reshape(
        seq_count, share * head_total * (CAND + 1)
    )
    tally = token_totals(tally)
    group_at = lax.axis_index(("kv", "vocab"))
    step = 1
    while step < groups:
        tally = tally + lax.ppermute(
            tally, ("kv", "vocab"), [(i, i ^ step) for i in range(groups)]
        )
        step *= 2
    tally = jnp.concatenate(
        [lax.dynamic_slice_in_dim(tally, back[j], 1, 0) for j in range(seq_count)], axis=0
    ).reshape(seq_count, kv_count, tenants, sub, head_total, CAND + 1)
    tally = jnp.transpose(tally, (4, 1, 0, 3, 2, 5)).reshape(
        head_total, tree_size, tenants, CAND + 1
    )
    log_normalizer = jnp.log(tally[..., 0])
    candidate_logits = tally[..., 1:]
    accept_pick = (accepted_path[0][:, None] == node_of[None, :]).astype(bf16)

    def write_path(old_block, fresh_rows):
        chosen = jnp.einsum(
            "au,uhc->ahc", accept_pick, fresh_rows, preferred_element_type=f32
        ).astype(bf16)
        result = old_block[0]
        for a in range(accept_pick.shape[0]):
            result = jnp.where((cache_cells == length + a)[:, None, None], chosen[a][None], result)
        return result[None]

    keys_updated = write_path(cache_keys, new_keys)
    values_updated = write_path(cache_values, new_values)
    return (keys_updated, values_updated, log_normalizer, candidate_logits)


def solution(mesh):
    placed = (
        P("kv", "vocab", "seq"),
        P("seq", "kv", None),
        P("kv", None, "seq"),
        P("seq"),
        P("seq"),
        P("seq"),
        P("seq"),
        P("seq"),
        P("vocab", "seq", "kv", None),
        P("vocab", "seq", "kv", None),
        P("vocab"),
        P("vocab", None, None),
        P("vocab", None),
        P("seq", None, ("kv", "vocab")),
        P(("kv", "vocab"), "seq"),
        P(None, "seq", ("kv", "vocab")),
        P(None, ("kv", "vocab")),
        P(("kv", "seq", "vocab"), None),
        P(),
    )
    tokens = 48 // mesh.shape["kv"]
    fits = mesh.shape["kv"] == 2 and tokens % mesh.shape["seq"] == 0
    body = local if fits else local_general
    return jax.shard_map(
        body,
        mesh=mesh,
        in_specs=placed,
        out_specs=(P("vocab", "seq", "kv", None), P("vocab", "seq", "kv", None), P(), P()),
        check_vma=False,
    )
```

```python
import jax
import jax.numpy as jnp
from jax import lax
from jax.experimental import pallas as pl
from jax.experimental.pallas import tpu as pltpu
from jax.sharding import PartitionSpec as P

MODEL_WIDTH = 3584
HEAD_SIZE = 256
CAND = 8


EPSILON = 1e-06
SCORE_CAP = 50.0
LOGIT_CAP = 30.0


def apply_rotary(vectors, token_positions):
    half_dim = vectors.shape[-1] // 2
    frequency = 10000.0 ** (-2.0 * jnp.arange(half_dim, dtype=jnp.float32) / vectors.shape[-1])
    angles = token_positions.astype(jnp.float32)[..., None] * frequency
    cosine = jnp.cos(angles)
    sine_part = jnp.sin(angles)
    first_half = vectors[..., :half_dim]
    second_half = vectors[..., half_dim:]
    return jnp.concatenate(
        [
            first_half * cosine - second_half * sine_part,
            second_half * cosine + first_half * sine_part,
        ],
        axis=-1,
    )


def capped_weight(scores):
    return jnp.exp(SCORE_CAP * jnp.tanh(scores * 0.0625 / SCORE_CAP))


def row_inverse(values):
    totals = lax.psum(jnp.sum(values * values, axis=-1), "seq")
    return lax.rsqrt(totals / MODEL_WIDTH + EPSILON)[:, None]


def gated_units(gate_up, squares):
    inverse = lax.rsqrt(squares / MODEL_WIDTH + EPSILON)[:, None]
    return (
        jax.nn.gelu(gate_up[:, 0] * inverse, approximate=True) * (gate_up[:, 1] * inverse)
    ).astype(jnp.bfloat16)


def local_general(
    hidden_state,
    input_projection,
    output_projection,
    norm_pre_attention,
    norm_post_attention,
    norm_pre_feedforward,
    norm_post_feedforward,
    norm_final,
    cache_keys,
    cache_values,
    cache_length,
    ancestors,
    accepted_path,
    gate_up_weight,
    down_weight,
    draft_weight,
    draft_bias,
    vocab_weight,
    candidate_tokens,
):
    tok_block = hidden_state.shape[0]
    kv_count = lax.axis_size("kv")
    tenants = lax.axis_size("vocab")
    tree_size = tok_block * kv_count
    own_state = hidden_state[:, 0, :]
    tenant_state = lax.all_gather(own_state, "kv", axis=0, tiled=True)
    tenant_float = tenant_state.astype(jnp.float32)
    scaled_input = (tenant_float * norm_pre_attention).astype(jnp.bfloat16)
    projected_rows = jnp.einsum(
        "td,dhc->thc", scaled_input, input_projection, preferred_element_type=jnp.float32
    )
    projected_rows, squares = lax.psum(
        (projected_rows, jnp.sum(tenant_float * tenant_float, axis=-1)), "seq"
    )
    projected_rows = projected_rows * lax.rsqrt(squares / MODEL_WIDTH + EPSILON)[:, None, None]
    head_count = projected_rows.shape[1]
    depths = jnp.sum(ancestors[0], axis=-1) - 1
    length = cache_length[0]
    token_positions = length + depths
    query_rows = apply_rotary(
        projected_rows[:, :, : 2 * HEAD_SIZE].reshape(tree_size, head_count, 2, HEAD_SIZE),
        token_positions[:, None, None],
    ).astype(jnp.bfloat16)
    new_keys = apply_rotary(
        projected_rows[:, :, 2 * HEAD_SIZE : 3 * HEAD_SIZE], token_positions[:, None]
    ).astype(jnp.bfloat16)
    new_values = projected_rows[:, :, 3 * HEAD_SIZE :].astype(jnp.bfloat16)
    block_size = cache_keys.shape[1]
    block_start = lax.axis_index("seq") * block_size
    cache_cells = block_start + jnp.arange(block_size, dtype=jnp.int32)
    scores = jnp.einsum(
        "thgc,shc->thgs", query_rows, cache_keys[0], preferred_element_type=jnp.float32
    )
    weights = jnp.where((cache_cells < length)[None, None, None, :], capped_weight(scores), 0.0)
    numerator = jnp.einsum(
        "thgs,shc->thgc",
        weights.astype(jnp.bfloat16),
        cache_values[0],
        preferred_element_type=jnp.float32,
    )
    numerator, denominator = lax.psum((numerator, jnp.sum(weights, axis=-1)), "seq")
    tree_scores = jnp.einsum(
        "thgc,uhc->thgu", query_rows, new_keys, preferred_element_type=jnp.float32
    )
    tree_weights = jnp.where(ancestors[0][:, None, None, :] > 0, capped_weight(tree_scores), 0.0)
    numerator = numerator + jnp.einsum(
        "thgu,uhc->thgc",
        tree_weights.astype(jnp.bfloat16),
        new_values,
        preferred_element_type=jnp.float32,
    )
    denominator = denominator + jnp.sum(tree_weights, axis=-1)
    attended = (
        (numerator / denominator[..., None])
        .astype(jnp.bfloat16)
        .reshape(tree_size, head_count * 2 * HEAD_SIZE)
    )
    out_matrix = output_projection.reshape(head_count * 2 * HEAD_SIZE, output_projection.shape[2])
    attention_out = lax.psum_scatter(
        jnp.dot(attended, out_matrix, preferred_element_type=jnp.float32),
        "kv",
        scatter_dimension=0,
        tiled=True,
    )
    first_sum = (
        own_state.astype(jnp.float32)
        + attention_out * row_inverse(attention_out) * norm_post_attention
    ).astype(jnp.bfloat16)
    all_state = lax.all_gather(first_sum, ("kv", "vocab"), axis=0, tiled=True)
    all_float = all_state.astype(jnp.float32)
    scaled_ffn = (all_float * norm_pre_feedforward).astype(jnp.bfloat16)
    gate_up = jnp.einsum(
        "td,dcf->tcf", scaled_ffn, gate_up_weight, preferred_element_type=jnp.float32
    )
    ffn_squares = jnp.sum(all_float * all_float, axis=-1)
    gate_up, ffn_squares = lax.psum((gate_up, ffn_squares), "seq")
    activated = gated_units(gate_up, ffn_squares)
    ffn_out = lax.psum_scatter(
        jnp.dot(activated, down_weight, preferred_element_type=jnp.float32),
        ("kv", "vocab"),
        scatter_dimension=0,
        tiled=True,
    )
    first_float = first_sum.astype(jnp.float32)
    second_sum = (first_float + ffn_out * row_inverse(ffn_out) * norm_post_feedforward).astype(
        jnp.bfloat16
    )
    second_float = second_sum.astype(jnp.float32)
    normed = (second_float * row_inverse(second_float) * norm_final).astype(jnp.bfloat16)
    gathered = lax.all_gather(normed, ("kv", "vocab"), axis=0, tiled=True)
    lifted = jnp.einsum("td,ndc->tnc", gathered, draft_weight, preferred_element_type=jnp.float32)
    lifted = lax.psum(lifted.astype(jnp.bfloat16), "seq").astype(jnp.float32)
    branch = jax.nn.silu(lifted + draft_bias).astype(jnp.bfloat16)
    row_count = gathered.shape[0]
    vocab_rows = vocab_weight.shape[0]
    draft_count = branch.shape[1]
    columns = vocab_weight
    base_logits = lax.dot_general(
        lax.all_gather(gathered, "seq", axis=1, tiled=True),
        columns,
        (((1,), (1,)), ((), ())),
        preferred_element_type=jnp.float32,
    )
    columns = vocab_weight
    draft_extra = jnp.einsum(
        "tnc,vc->tnv",
        lax.all_gather(branch, ("kv", "vocab"), axis=2, tiled=True),
        columns,
        preferred_element_type=jnp.float32,
    )
    raw_logits = jnp.concatenate(
        [base_logits[:, None, :], base_logits[:, None, :] + draft_extra], axis=1
    )
    logits = LOGIT_CAP * jnp.tanh(raw_logits / LOGIT_CAP)
    totals = jnp.sum(jnp.exp(logits), axis=-1)
    head_total = draft_count + 1
    candidates = candidate_tokens.reshape(head_total, kv_count, tok_block, tenants, CAND)
    candidates = jnp.transpose(candidates, (0, 1, 3, 2, 4)).reshape(head_total, row_count, CAND)
    candidates = jnp.transpose(candidates, (1, 0, 2))
    vocab_start = lax.axis_index(("kv", "seq", "vocab")) * vocab_rows
    local_tokens = candidates - vocab_start
    entry_index = jnp.arange(vocab_rows, dtype=jnp.int32)
    picked = jnp.stack(
        [
            jnp.sum(
                jnp.where(entry_index == local_tokens[:, :, column : column + 1], logits, 0.0),
                axis=-1,
            )
            for column in range(CAND)
        ],
        axis=-1,
    )
    totals, picked = lax.psum((totals, picked), ("kv", "seq", "vocab"))
    log_totals = jnp.transpose(jnp.log(totals)).reshape(head_total, kv_count, tenants, tok_block)
    log_normalizer = jnp.transpose(log_totals, (0, 1, 3, 2)).reshape(head_total, tree_size, tenants)
    picked = jnp.transpose(picked, (1, 0, 2)).reshape(
        head_total, kv_count, tenants, tok_block, CAND
    )
    candidate_logits = jnp.transpose(picked, (0, 1, 3, 2, 4)).reshape(
        head_total, tree_size, tenants, CAND
    )
    accept_count = accepted_path.shape[1]
    slot_rows = length + jnp.arange(accept_count, dtype=jnp.int32)
    tree_nodes = jnp.arange(tree_size, dtype=jnp.int32)
    matches = (cache_cells[:, None, None] == slot_rows[None, :, None]) & (
        accepted_path[0][None, :, None] == tree_nodes[None, None, :]
    )
    selector = jnp.sum(matches.astype(jnp.float32), axis=1)
    written = jnp.sum(selector, axis=-1) > 0.0
    selector = selector.astype(jnp.bfloat16)

    def write_path(old_block, fresh_rows):
        moved_rows = jnp.dot(
            selector, fresh_rows.reshape(tree_size, -1), preferred_element_type=jnp.float32
        ).astype(jnp.bfloat16)
        return jnp.where(
            written[:, None], moved_rows, old_block[0].reshape(block_size, -1)
        ).reshape(old_block.shape)

    keys_updated = write_path(cache_keys, new_keys)
    values_updated = write_path(cache_values, new_values)
    return (keys_updated, values_updated, log_normalizer, candidate_logits)


def fits(sizes):
    return sizes["kv"] == 2 and sizes["vocab"] == 4 and sizes["seq"] == 4


def send_ahead(pick):
    count = lax.axis_size("seq")
    return [
        lax.ppermute(pick(j), "seq", [(i, (i + j) % count) for i in range(count)])
        for j in range(1, count)
    ]


def collect(block):
    count = lax.axis_size("seq")
    return [block] + [
        lax.ppermute(block, "seq", [(i, (i - j) % count) for i in range(count)])
        for j in range(1, count)
    ]


def in_order(blocks, ahead):
    result = jnp.zeros((len(blocks),) + blocks[0].shape, blocks[0].dtype)
    for j, block in enumerate(blocks):
        result = lax.dynamic_update_index_in_dim(result, block, ahead[j], 0)
    return result


def add_up(blocks):
    total = blocks[0].astype(jnp.float32)
    for block in blocks[1:]:
        total = total + block.astype(jnp.float32)
    return total


def swap(values, axis, bit):
    count = lax.axis_size(axis)
    return lax.ppermute(values, axis, [(i, i ^ bit) for i in range(count)])


def split_lanes(values):
    high = values.astype(jnp.bfloat16)
    low = (values - high.astype(jnp.float32)).astype(jnp.bfloat16)
    shape = values.shape[:-1] + (64,)
    return jnp.concatenate([jnp.broadcast_to(high, shape), jnp.broadcast_to(low, shape)], axis=-1)


def inverse_of(totals):
    return lax.rsqrt(totals / MODEL_WIDTH + EPSILON)


def rotate(vectors, cosine, sine):
    half = vectors.shape[-1] // 2
    first, second = vectors[..., :half], vectors[..., half:]
    return jnp.concatenate(
        [first * cosine - second * sine, second * cosine + first * sine], axis=-1
    )


def update_caches(cache_keys, cache_values, rows, offset):
    slots = cache_keys.shape[0]
    accept = rows.shape[1]
    parts = 4
    piece = slots // parts

    def kernel(offset_ref, rows_ref, keys_in, values_in, keys_out, values_out, flag, sems):
        flag[...] = jnp.zeros_like(flag)
        copies = []
        for which, (source, target) in enumerate(((keys_in, keys_out), (values_in, values_out))):
            for p in range(parts):
                window = pl.ds(p * piece, piece)
                copies.append(
                    pltpu.make_async_copy(
                        source.at[window], target.at[window], sems.at[which * parts + p]
                    )
                )
        for copy in copies:
            copy.start()
        for copy in copies:
            copy.wait()
        for which, target in enumerate((keys_out, values_out)):
            for a in range(accept):
                slot = offset_ref[0] + a

                @pl.when((slot >= 0) & (slot < slots))
                def _():
                    copy = pltpu.make_async_copy(
                        rows_ref.at[which, pl.ds(a, 1)], target.at[pl.ds(slot, 1)], sems.at[0]
                    )
                    copy.start()
                    copy.wait()

    like = jax.ShapeDtypeStruct(cache_keys.shape, cache_keys.dtype)
    return pl.pallas_call(
        kernel,
        out_shape=(like, like, jax.ShapeDtypeStruct((8, 128), jnp.float32)),
        in_specs=[
            pl.BlockSpec(memory_space=pltpu.SMEM),
            pl.BlockSpec(memory_space=pltpu.VMEM),
            pl.BlockSpec(memory_space=pl.ANY),
            pl.BlockSpec(memory_space=pl.ANY),
        ],
        out_specs=(
            pl.BlockSpec(memory_space=pl.ANY),
            pl.BlockSpec(memory_space=pl.ANY),
            pl.BlockSpec(memory_space=pltpu.VMEM),
        ),
        scratch_shapes=[pltpu.SemaphoreType.DMA((2 * parts,))],
        cost_estimate=pl.CostEstimate(
            flops=0, bytes_accessed=4 * cache_keys.size * 2, transcendentals=0
        ),
    )(offset, rows, cache_keys, cache_values)


def local(
    hidden_state,
    input_projection,
    output_projection,
    norm_pre_attention,
    norm_post_attention,
    norm_pre_feedforward,
    norm_post_feedforward,
    norm_final,
    cache_keys,
    cache_values,
    cache_length,
    ancestors,
    accepted_path,
    gate_up_weight,
    down_weight,
    draft_weight,
    draft_bias,
    vocab_weight,
    candidate_tokens,
):
    f32, bf16 = jnp.float32, jnp.bfloat16
    plane = ("kv", "vocab")
    tok_block, _, width = hidden_state.shape
    seq_count = lax.axis_size("seq")
    kv_count = lax.axis_size("kv")
    tenants = lax.axis_size("vocab")
    groups = kv_count * tenants
    tree_size = tok_block * kv_count
    row_count = tok_block * groups
    seq_at = lax.axis_index("seq")
    kv_at = lax.axis_index("kv")
    vocab_at = lax.axis_index("vocab")
    ahead = [(seq_at + j) % seq_count for j in range(seq_count)]
    own_state = hidden_state[:, 0, :]

    half = vocab_weight.shape[0] // 2
    over_kv = swap(vocab_weight, "kv", 1)
    over_y = swap(vocab_weight, "vocab", 2)
    far_top = swap(over_kv[:half], "vocab", 2)
    far_bottom = swap(over_y[half:], "kv", 1)
    near = [vocab_weight, over_kv, over_y, far_top, far_bottom]
    vocab_blocks = near + [swap(block, "vocab", 1) for block in near]

    tenant_state = jnp.concatenate([own_state, swap(own_state, "kv", 1)], axis=0)
    tenant_float = tenant_state.astype(f32)
    scaled_input = (tenant_float * norm_pre_attention).astype(bf16)
    projected = jnp.einsum(
        "td,dhc->htc", scaled_input, input_projection, preferred_element_type=f32
    ).astype(bf16)
    square_lanes = split_lanes(jnp.sum(tenant_float * tenant_float, axis=-1, keepdims=True))
    head_count = projected.shape[0]
    pair = 2 * HEAD_SIZE
    packed = jnp.concatenate(
        [
            projected[:, :, :pair],
            jnp.broadcast_to(square_lanes, (head_count,) + square_lanes.shape),
        ],
        axis=-1,
    )
    summed = add_up(
        [lax.dynamic_index_in_dim(packed, seq_at, 0, False)]
        + send_ahead(lambda j: lax.dynamic_index_in_dim(packed, ahead[j], 0, False))
    )
    inverse = inverse_of(summed[:, pair : pair + 1] + summed[:, pair + 64 : pair + 65])
    tree_mask = ancestors[0]
    tree_mask = jnp.where(
        kv_at == 0, tree_mask, jnp.roll(tree_mask, (tok_block, tok_block), (0, 1))
    )
    length = cache_length[0]
    depths = jnp.sum(tree_mask, axis=-1, keepdims=True) - 1
    frequency = 10000.0 ** (
        -2.0 * jnp.arange(HEAD_SIZE // 2, dtype=f32) / HEAD_SIZE
    )
    angles = (length + depths).astype(f32) * frequency
    cosine, sine = jnp.cos(angles), jnp.sin(angles)
    query_rows = jnp.concatenate(
        [
            rotate(summed[:, :HEAD_SIZE] * inverse, cosine, sine),
            rotate(summed[:, HEAD_SIZE:pair] * inverse, cosine, sine),
        ],
        axis=0,
    ).astype(bf16)
    all_queries = in_order(collect(query_rows), ahead)
    fresh = projected[:, :, pair:]
    fresh = add_up(
        [lax.dynamic_index_in_dim(fresh, seq_at, 0, False)]
        + send_ahead(lambda j: lax.dynamic_index_in_dim(fresh, ahead[j], 0, False))
    )
    new_keys = rotate(fresh[:, :HEAD_SIZE] * inverse, cosine, sine).astype(bf16)
    new_values = (fresh[:, HEAD_SIZE:] * inverse).astype(bf16)

    block_size = cache_keys.shape[1]
    block_start = seq_at * block_size
    cache_cells = block_start + jnp.arange(block_size, dtype=jnp.int32)
    scores = jnp.einsum("hrc,shc->hrs", all_queries, cache_keys[0], preferred_element_type=f32)
    weights = jnp.where((cache_cells < length)[None, None, :], capped_weight(scores), 0.0)
    numerator = jnp.einsum(
        "hrs,shc->hrc", weights.astype(bf16), cache_values[0], preferred_element_type=f32
    )
    rows = 2 * tree_size
    sums = jnp.sum(weights, axis=-1)
    sums_high = sums.astype(bf16)
    sums_low = (sums - sums_high.astype(f32)).astype(bf16)
    sums = jnp.concatenate(
        [sums_high, sums_low, jnp.zeros((head_count, HEAD_SIZE - 2 * rows), bf16)], axis=-1
    )
    packed = jnp.concatenate(
        [
            numerator.astype(bf16),
            jnp.broadcast_to(sums[:, None, :], (head_count, 16, HEAD_SIZE)),
        ],
        axis=1,
    )
    arrived = send_ahead(lambda j: lax.dynamic_index_in_dim(packed, ahead[j], 0, False))
    tree_scores = lax.dot_general(
        query_rows, new_keys, (((1,), (1,)), ((), ())), preferred_element_type=f32
    )
    seen = jnp.concatenate([tree_mask, tree_mask], axis=0) > 0
    tree_weights = jnp.where(seen, capped_weight(tree_scores), 0.0)
    tree_numerator = jnp.dot(tree_weights.astype(bf16), new_values, preferred_element_type=f32)
    tree_sums = jnp.sum(tree_weights, axis=-1, keepdims=True)
    summed = add_up([lax.dynamic_index_in_dim(packed, seq_at, 0, False)] + arrived)
    denominator = (summed[rows, :rows] + summed[rows, rows : 2 * rows])[:, None] + tree_sums
    attended = ((summed[:rows] + tree_numerator) / denominator).astype(bf16)
    attended = in_order(collect(attended), ahead).reshape(head_count, 2, tree_size, HEAD_SIZE)
    attention_out = jnp.einsum(
        "hgtc,hgcd->td",
        attended,
        output_projection.reshape(head_count, 2, HEAD_SIZE, width),
        preferred_element_type=f32,
    )
    attention_out = attention_out[:tok_block] + swap(
        attention_out[tok_block:].astype(bf16), "kv", 1
    ).astype(f32)

    def token_totals(*values):
        lanes = 128 // len(values)
        columns = [jnp.sum(value, axis=-1, keepdims=True) for value in values]
        columns = jnp.concatenate(
            [jnp.broadcast_to(column, (tok_block, lanes)) for column in columns], axis=-1
        )
        columns = add_up(collect(columns))
        return [columns[:, k * lanes : k * lanes + 1] for k in range(len(values))]

    (totals,) = token_totals(attention_out * attention_out)
    first_sum = (
        own_state.astype(f32) + attention_out * inverse_of(totals) * norm_post_attention
    ).astype(bf16)

    all_state = lax.all_gather(first_sum, plane, axis=0, tiled=True)
    all_float = all_state.astype(f32)
    scaled_ffn = (all_float * norm_pre_feedforward).astype(bf16)
    square_lanes = split_lanes(jnp.sum(all_float * all_float, axis=-1, keepdims=True))
    share = row_count // seq_count
    units = down_weight.shape[0]
    partial = jnp.einsum(
        "td,dcf->ctf", scaled_ffn, gate_up_weight, preferred_element_type=f32
    ).astype(bf16)

    node_at = jnp.arange(tree_size, dtype=jnp.int32)
    node_at = jnp.where(kv_at == 0, node_at, (node_at + tok_block) % tree_size)
    accept_pick = (accepted_path[0][:, None] == node_at[None, :]).astype(bf16)
    chosen = jnp.dot(
        accept_pick,
        jnp.concatenate([new_keys, new_values], axis=1),
        preferred_element_type=f32,
    ).astype(bf16)
    chosen = in_order(collect(chosen), ahead)
    accept_count = chosen.shape[1]
    chosen = chosen.reshape(head_count, accept_count, 2, HEAD_SIZE).transpose(2, 1, 0, 3)
    chosen, partial = lax.optimization_barrier((chosen, partial))
    keys_updated, values_updated, flag = update_caches(
        cache_keys[0], cache_values[0], chosen, (length - block_start).reshape(1)
    )

    pieces = 2
    piece = units // pieces
    ffn_out = 0.0
    for p in range(pieces):
        window = slice(p * piece, (p + 1) * piece)
        gate = partial[0, :, window]
        up = partial[1, :, window]
        if p == 0:
            gate = jnp.concatenate([gate, square_lanes], axis=-1)
        lanes = gate.shape[1]
        both = jnp.concatenate([gate, up], axis=-1).reshape(seq_count, share, lanes + piece)
        summed = add_up(
            [lax.dynamic_index_in_dim(both, seq_at, 0, False)]
            + send_ahead(lambda j: lax.dynamic_index_in_dim(both, ahead[j], 0, False))
        )
        if p == 0:
            inverse = inverse_of(summed[:, piece : piece + 1] + summed[:, piece + 64 : piece + 65])
            flag, summed = lax.optimization_barrier((flag, summed))
        activated = (
            jax.nn.gelu(summed[:, :piece] * inverse, approximate=True)
            * (summed[:, lanes:] * inverse)
        ).astype(bf16)
        activated = in_order(collect(activated), ahead).reshape(row_count, piece)
        ffn_out = ffn_out + jnp.dot(activated, down_weight[window], preferred_element_type=f32)
    ffn_out = ffn_out.astype(bf16).reshape(groups, tok_block, width)
    ffn_out = add_up(list(lax.all_to_all(ffn_out, plane, 0, 0)))
    first_float = first_sum.astype(f32)
    scaled_out = ffn_out * norm_post_feedforward
    out_total, first_total, cross_total, scaled_total = token_totals(
        ffn_out * ffn_out, first_float * first_float, first_float * scaled_out, scaled_out * scaled_out
    )
    inverse = inverse_of(out_total)
    second_sum = (first_float + scaled_out * inverse).astype(bf16)
    second_total = first_total + inverse * (2.0 * cross_total + inverse * scaled_total)
    normed = (
        second_sum.astype(f32) * inverse_of(jnp.maximum(second_total, 0.0)) * norm_final
    ).astype(bf16)

    gathered = lax.all_gather(normed, plane, axis=0, tiled=True)
    lifted = jnp.einsum(
        "td,ndc->ntc", gathered, draft_weight, preferred_element_type=f32
    ).astype(bf16)
    summed = add_up(
        [lax.dynamic_index_in_dim(lifted, seq_at, 0, False)]
        + send_ahead(lambda j: lax.dynamic_index_in_dim(lifted, ahead[j], 0, False))
    )
    bias = lax.dynamic_index_in_dim(draft_bias, seq_at, 0, True)
    branch = jax.nn.silu(summed + bias).astype(bf16)
    branch = lax.all_to_all(branch.reshape(groups, tok_block, -1), plane, 0, 0)
    branch = branch.transpose(1, 0, 2).reshape(tok_block, MODEL_WIDTH)
    base = in_order(collect(normed), ahead)
    base = jnp.concatenate([base[s] for s in range(seq_count)], axis=-1)
    token_rows = jnp.concatenate([base] + collect(branch), axis=0)
    raw = jnp.concatenate(
        [
            lax.dot_general(
                token_rows, block, (((1,), (1,)), ((), ())), preferred_element_type=f32
            )
            for block in vocab_blocks
        ],
        axis=1,
    ).reshape(seq_count + 1, tok_block, -1)
    raw = jnp.concatenate([raw[:1], raw[:1] + raw[1:]], axis=0)
    logits = LOGIT_CAP * jnp.tanh(raw / LOGIT_CAP)
    totals = jnp.sum(jnp.exp(logits), axis=-1)

    vocab_rows = vocab_weight.shape[0]

    def first_entry(kv_bit, vocab_bits):
        place = ((kv_at ^ kv_bit) * seq_count + seq_at) * tenants + (vocab_at ^ vocab_bits)
        return place * vocab_rows

    entries = []
    for core in (0, 1):
        for kv_bit, vocab_bits in ((0, 0), (1, 0), (0, 2), (1, 2)):
            entries.append(
                first_entry(kv_bit, vocab_bits ^ core) + jnp.arange(vocab_rows, dtype=jnp.int32)
            )
    entries = jnp.concatenate(entries)
    candidates = lax.dynamic_slice(
        candidate_tokens,
        (0, kv_at * tok_block, vocab_at, 0),
        (seq_count + 1, tok_block, 1, CAND),
    )[:, :, 0]
    candidates = jnp.concatenate(
        [candidates[:1]]
        + [lax.dynamic_slice_in_dim(candidates, 1 + ahead[j], 1, 0) for j in range(seq_count)],
        axis=0,
    )
    picked = [
        jnp.sum(
            jnp.where(entries == candidates[:, :, column : column + 1], logits, 0.0), axis=-1
        )
        for column in range(CAND)
    ]
    tally = jnp.stack([totals] + picked)
    draft_tally = in_order([tally[:, 1 + j] for j in range(seq_count)], ahead)
    tally = jnp.concatenate([tally[:, 0][None], draft_tally], axis=0)
    head_total = seq_count + 1
    tally = add_up(collect(tally.reshape(head_total * (CAND + 1), tok_block)))
    tally = lax.all_gather(tally, plane, axis=0)
    tally = tally.reshape(kv_count, tenants, head_total, CAND + 1, tok_block)
    log_normalizer = jnp.log(
        tally[:, :, :, 0].transpose(2, 0, 3, 1).reshape(head_total, tree_size, tenants)
    )
    candidate_logits = (
        tally[:, :, :, 1:]
        .transpose(2, 0, 4, 1, 3)
        .reshape(head_total, tree_size, tenants, CAND)
    )
    return (keys_updated[None], values_updated[None], log_normalizer, candidate_logits)


def solution(mesh):
    placed = (
        P("kv", "vocab", "seq"),
        P("seq", "kv", None),
        P("kv", None, "seq"),
        P("seq"),
        P("seq"),
        P("seq"),
        P("seq"),
        P("seq"),
        P("vocab", "seq", "kv", None),
        P("vocab", "seq", "kv", None),
        P("vocab"),
        P("vocab", None, None),
        P("vocab", None),
        P("seq", None, ("kv", "vocab")),
        P(("kv", "vocab"), "seq"),
        P(None, "seq", ("kv", "vocab")),
        P(None, ("kv", "vocab")),
        P(("kv", "seq", "vocab"), None),
        P(),
    )
    body = local if fits(mesh.shape) else local_general
    return jax.shard_map(
        body,
        mesh=mesh,
        in_specs=placed,
        out_specs=(P("vocab", "seq", "kv", None), P("vocab", "seq", "kv", None), P(), P()),
        check_vma=False,
    )
```

```python
import jax
import jax.numpy as jnp
from jax import lax
from jax.experimental import pallas as pl
from jax.experimental.pallas import tpu as pltpu
from jax.sharding import PartitionSpec as P

MODEL_WIDTH = 3584
HEAD_SIZE = 256
CAND = 8


EPSILON = 1e-06
SCORE_CAP = 50.0
LOGIT_CAP = 30.0


def apply_rotary(vectors, token_positions):
    half_dim = vectors.shape[-1] // 2
    frequency = 10000.0 ** (-2.0 * jnp.arange(half_dim, dtype=jnp.float32) / vectors.shape[-1])
    angles = token_positions.astype(jnp.float32)[..., None] * frequency
    cosine = jnp.cos(angles)
    sine_part = jnp.sin(angles)
    first_half = vectors[..., :half_dim]
    second_half = vectors[..., half_dim:]
    return jnp.concatenate(
        [
            first_half * cosine - second_half * sine_part,
            second_half * cosine + first_half * sine_part,
        ],
        axis=-1,
    )


def capped_weight(scores):
    return jnp.exp(SCORE_CAP * jnp.tanh(scores * 0.0625 / SCORE_CAP))


def row_inverse(values):
    totals = lax.psum(jnp.sum(values * values, axis=-1), "seq")
    return lax.rsqrt(totals / MODEL_WIDTH + EPSILON)[:, None]


def gated_units(gate_up, squares):
    inverse = lax.rsqrt(squares / MODEL_WIDTH + EPSILON)[:, None]
    return (
        jax.nn.gelu(gate_up[:, 0] * inverse, approximate=True) * (gate_up[:, 1] * inverse)
    ).astype(jnp.bfloat16)


def local_general(
    hidden_state,
    input_projection,
    output_projection,
    norm_pre_attention,
    norm_post_attention,
    norm_pre_feedforward,
    norm_post_feedforward,
    norm_final,
    cache_keys,
    cache_values,
    cache_length,
    ancestors,
    accepted_path,
    gate_up_weight,
    down_weight,
    draft_weight,
    draft_bias,
    vocab_weight,
    candidate_tokens,
):
    tok_block = hidden_state.shape[0]
    kv_count = lax.axis_size("kv")
    tenants = lax.axis_size("vocab")
    tree_size = tok_block * kv_count
    own_state = hidden_state[:, 0, :]
    tenant_state = lax.all_gather(own_state, "kv", axis=0, tiled=True)
    tenant_float = tenant_state.astype(jnp.float32)
    scaled_input = (tenant_float * norm_pre_attention).astype(jnp.bfloat16)
    projected_rows = jnp.einsum(
        "td,dhc->thc", scaled_input, input_projection, preferred_element_type=jnp.float32
    )
    projected_rows, squares = lax.psum(
        (projected_rows, jnp.sum(tenant_float * tenant_float, axis=-1)), "seq"
    )
    projected_rows = projected_rows * lax.rsqrt(squares / MODEL_WIDTH + EPSILON)[:, None, None]
    head_count = projected_rows.shape[1]
    depths = jnp.sum(ancestors[0], axis=-1) - 1
    length = cache_length[0]
    token_positions = length + depths
    query_rows = apply_rotary(
        projected_rows[:, :, : 2 * HEAD_SIZE].reshape(tree_size, head_count, 2, HEAD_SIZE),
        token_positions[:, None, None],
    ).astype(jnp.bfloat16)
    new_keys = apply_rotary(
        projected_rows[:, :, 2 * HEAD_SIZE : 3 * HEAD_SIZE], token_positions[:, None]
    ).astype(jnp.bfloat16)
    new_values = projected_rows[:, :, 3 * HEAD_SIZE :].astype(jnp.bfloat16)
    block_size = cache_keys.shape[1]
    block_start = lax.axis_index("seq") * block_size
    cache_cells = block_start + jnp.arange(block_size, dtype=jnp.int32)
    scores = jnp.einsum(
        "thgc,shc->thgs", query_rows, cache_keys[0], preferred_element_type=jnp.float32
    )
    weights = jnp.where((cache_cells < length)[None, None, None, :], capped_weight(scores), 0.0)
    numerator = jnp.einsum(
        "thgs,shc->thgc",
        weights.astype(jnp.bfloat16),
        cache_values[0],
        preferred_element_type=jnp.float32,
    )
    numerator, denominator = lax.psum((numerator, jnp.sum(weights, axis=-1)), "seq")
    tree_scores = jnp.einsum(
        "thgc,uhc->thgu", query_rows, new_keys, preferred_element_type=jnp.float32
    )
    tree_weights = jnp.where(ancestors[0][:, None, None, :] > 0, capped_weight(tree_scores), 0.0)
    numerator = numerator + jnp.einsum(
        "thgu,uhc->thgc",
        tree_weights.astype(jnp.bfloat16),
        new_values,
        preferred_element_type=jnp.float32,
    )
    denominator = denominator + jnp.sum(tree_weights, axis=-1)
    attended = (
        (numerator / denominator[..., None])
        .astype(jnp.bfloat16)
        .reshape(tree_size, head_count * 2 * HEAD_SIZE)
    )
    out_matrix = output_projection.reshape(head_count * 2 * HEAD_SIZE, output_projection.shape[2])
    attention_out = lax.psum_scatter(
        jnp.dot(attended, out_matrix, preferred_element_type=jnp.float32),
        "kv",
        scatter_dimension=0,
        tiled=True,
    )
    first_sum = (
        own_state.astype(jnp.float32)
        + attention_out * row_inverse(attention_out) * norm_post_attention
    ).astype(jnp.bfloat16)
    all_state = lax.all_gather(first_sum, ("kv", "vocab"), axis=0, tiled=True)
    all_float = all_state.astype(jnp.float32)
    scaled_ffn = (all_float * norm_pre_feedforward).astype(jnp.bfloat16)
    gate_up = jnp.einsum(
        "td,dcf->tcf", scaled_ffn, gate_up_weight, preferred_element_type=jnp.float32
    )
    ffn_squares = jnp.sum(all_float * all_float, axis=-1)
    gate_up, ffn_squares = lax.psum((gate_up, ffn_squares), "seq")
    activated = gated_units(gate_up, ffn_squares)
    ffn_out = lax.psum_scatter(
        jnp.dot(activated, down_weight, preferred_element_type=jnp.float32),
        ("kv", "vocab"),
        scatter_dimension=0,
        tiled=True,
    )
    first_float = first_sum.astype(jnp.float32)
    second_sum = (first_float + ffn_out * row_inverse(ffn_out) * norm_post_feedforward).astype(
        jnp.bfloat16
    )
    second_float = second_sum.astype(jnp.float32)
    normed = (second_float * row_inverse(second_float) * norm_final).astype(jnp.bfloat16)
    gathered = lax.all_gather(normed, ("kv", "vocab"), axis=0, tiled=True)
    lifted = jnp.einsum("td,ndc->tnc", gathered, draft_weight, preferred_element_type=jnp.float32)
    lifted = lax.psum(lifted.astype(jnp.bfloat16), "seq").astype(jnp.float32)
    branch = jax.nn.silu(lifted + draft_bias).astype(jnp.bfloat16)
    row_count = gathered.shape[0]
    vocab_rows = vocab_weight.shape[0]
    draft_count = branch.shape[1]
    columns = vocab_weight
    base_logits = lax.dot_general(
        lax.all_gather(gathered, "seq", axis=1, tiled=True),
        columns,
        (((1,), (1,)), ((), ())),
        preferred_element_type=jnp.float32,
    )
    columns = vocab_weight
    draft_extra = jnp.einsum(
        "tnc,vc->tnv",
        lax.all_gather(branch, ("kv", "vocab"), axis=2, tiled=True),
        columns,
        preferred_element_type=jnp.float32,
    )
    raw_logits = jnp.concatenate(
        [base_logits[:, None, :], base_logits[:, None, :] + draft_extra], axis=1
    )
    logits = LOGIT_CAP * jnp.tanh(raw_logits / LOGIT_CAP)
    totals = jnp.sum(jnp.exp(logits), axis=-1)
    head_total = draft_count + 1
    candidates = candidate_tokens.reshape(head_total, kv_count, tok_block, tenants, CAND)
    candidates = jnp.transpose(candidates, (0, 1, 3, 2, 4)).reshape(head_total, row_count, CAND)
    candidates = jnp.transpose(candidates, (1, 0, 2))
    vocab_start = lax.axis_index(("kv", "seq", "vocab")) * vocab_rows
    local_tokens = candidates - vocab_start
    entry_index = jnp.arange(vocab_rows, dtype=jnp.int32)
    picked = jnp.stack(
        [
            jnp.sum(
                jnp.where(entry_index == local_tokens[:, :, column : column + 1], logits, 0.0),
                axis=-1,
            )
            for column in range(CAND)
        ],
        axis=-1,
    )
    totals, picked = lax.psum((totals, picked), ("kv", "seq", "vocab"))
    log_totals = jnp.transpose(jnp.log(totals)).reshape(head_total, kv_count, tenants, tok_block)
    log_normalizer = jnp.transpose(log_totals, (0, 1, 3, 2)).reshape(head_total, tree_size, tenants)
    picked = jnp.transpose(picked, (1, 0, 2)).reshape(
        head_total, kv_count, tenants, tok_block, CAND
    )
    candidate_logits = jnp.transpose(picked, (0, 1, 3, 2, 4)).reshape(
        head_total, tree_size, tenants, CAND
    )
    accept_count = accepted_path.shape[1]
    slot_rows = length + jnp.arange(accept_count, dtype=jnp.int32)
    tree_nodes = jnp.arange(tree_size, dtype=jnp.int32)
    matches = (cache_cells[:, None, None] == slot_rows[None, :, None]) & (
        accepted_path[0][None, :, None] == tree_nodes[None, None, :]
    )
    selector = jnp.sum(matches.astype(jnp.float32), axis=1)
    written = jnp.sum(selector, axis=-1) > 0.0
    selector = selector.astype(jnp.bfloat16)

    def write_path(old_block, fresh_rows):
        moved_rows = jnp.dot(
            selector, fresh_rows.reshape(tree_size, -1), preferred_element_type=jnp.float32
        ).astype(jnp.bfloat16)
        return jnp.where(
            written[:, None], moved_rows, old_block[0].reshape(block_size, -1)
        ).reshape(old_block.shape)

    keys_updated = write_path(cache_keys, new_keys)
    values_updated = write_path(cache_values, new_values)
    return (keys_updated, values_updated, log_normalizer, candidate_logits)


def fits(sizes):
    return sizes["kv"] == 2 and sizes["vocab"] == 4 and sizes["seq"] == 4


def send_ahead(pick):
    count = lax.axis_size("seq")
    return [
        lax.ppermute(pick(j), "seq", [(i, (i + j) % count) for i in range(count)])
        for j in range(1, count)
    ]


def collect(block):
    count = lax.axis_size("seq")
    return [block] + [
        lax.ppermute(block, "seq", [(i, (i - j) % count) for i in range(count)])
        for j in range(1, count)
    ]


def in_order(blocks, ahead):
    result = jnp.zeros((len(blocks),) + blocks[0].shape, blocks[0].dtype)
    for j, block in enumerate(blocks):
        result = lax.dynamic_update_index_in_dim(result, block, ahead[j], 0)
    return result


def add_up(blocks):
    total = blocks[0].astype(jnp.float32)
    for block in blocks[1:]:
        total = total + block.astype(jnp.float32)
    return total


def swap(values, axis, bit):
    count = lax.axis_size(axis)
    return lax.ppermute(values, axis, [(i, i ^ bit) for i in range(count)])


def split_lanes(values):
    high = values.astype(jnp.bfloat16)
    low = (values - high.astype(jnp.float32)).astype(jnp.bfloat16)
    shape = values.shape[:-1] + (64,)
    return jnp.concatenate([jnp.broadcast_to(high, shape), jnp.broadcast_to(low, shape)], axis=-1)


def zero_at(event):
    corner = event.reshape(-1)[0] if event.ndim < 2 else event[(0,) * event.ndim]
    return (jnp.abs(corner.astype(jnp.float32)) > 3e38).astype(jnp.int32)


def still(*values):
    return sum(value[(0,) * value.ndim].astype(jnp.float32) * 0.0 for value in values)


def rows_after(values, first, count, event):
    return lax.dynamic_slice_in_dim(values, first + zero_at(event), count, 0)


def inverse_of(totals):
    return lax.rsqrt(totals / MODEL_WIDTH + EPSILON)


def rotate(vectors, cosine, sine):
    half = vectors.shape[-1] // 2
    first, second = vectors[..., :half], vectors[..., half:]
    return jnp.concatenate(
        [first * cosine - second * sine, second * cosine + first * sine], axis=-1
    )


def update_caches(cache_keys, cache_values, rows, offset):
    slots, heads, size = cache_keys.shape
    accept = rows.shape[1]
    piece = 256
    parts = slots // piece

    def kernel(
        offset_ref, rows_ref, keys_in, values_in, keys_out, values_out, flag, held, get, put, sem
    ):
        flag[...] = jnp.zeros_like(flag)

        def copies(number):
            source, target = ((keys_in, keys_out), (values_in, values_out))[number // parts]
            window = pl.ds(number % parts * piece, piece)
            return (
                pltpu.make_async_copy(source.at[window], held.at[number], get.at[number]),
                pltpu.make_async_copy(held.at[number], target.at[window], put.at[number]),
            )

        pairs = [copies(number) for number in range(2 * parts)]
        for inward, _ in pairs:
            inward.start()
        for inward, outward in pairs:
            inward.wait()
            outward.start()
        for _, outward in pairs:
            outward.wait()
        for which, target in enumerate((keys_out, values_out)):
            for a in range(accept):
                slot = offset_ref[0] + a

                @pl.when((slot >= 0) & (slot < slots))
                def _():
                    copy = pltpu.make_async_copy(
                        rows_ref.at[which, pl.ds(a, 1)], target.at[pl.ds(slot, 1)], sem.at[0]
                    )
                    copy.start()
                    copy.wait()

    like = jax.ShapeDtypeStruct(cache_keys.shape, cache_keys.dtype)
    return pl.pallas_call(
        kernel,
        out_shape=(like, like, jax.ShapeDtypeStruct((8, 128), jnp.float32)),
        in_specs=[
            pl.BlockSpec(memory_space=pltpu.SMEM),
            pl.BlockSpec(memory_space=pltpu.VMEM),
            pl.BlockSpec(memory_space=pltpu.HBM),
            pl.BlockSpec(memory_space=pltpu.HBM),
        ],
        out_specs=(
            pl.BlockSpec(memory_space=pltpu.HBM),
            pl.BlockSpec(memory_space=pltpu.HBM),
            pl.BlockSpec(memory_space=pltpu.VMEM),
        ),
        scratch_shapes=[
            pltpu.VMEM((2 * parts, piece, heads, size), cache_keys.dtype),
            pltpu.SemaphoreType.DMA((2 * parts,)),
            pltpu.SemaphoreType.DMA((2 * parts,)),
            pltpu.SemaphoreType.DMA((1,)),
        ],
        compiler_params=pltpu.CompilerParams(vmem_limit_bytes=24 * 2**20),
        cost_estimate=pl.CostEstimate(
            flops=0, bytes_accessed=4 * cache_keys.size * 2, transcendentals=0
        ),
    )(offset, rows, cache_keys, cache_values)


def score_vocabulary(numbers, candidates, base, own, other, blocks, lanes):
    tokens, width = own[0].shape
    share = base[0].shape[1]
    count = len(own)
    extent = sum(part.shape[0] for part in blocks[0])
    parts = [part for block in blocks for part in block]
    inputs = base + own + other

    def kernel(numbers_ref, candidates_ref, *rest):
        vectors, rest = rest[: len(inputs)], rest[len(inputs) :]
        sources, (out_ref, held, wide, narrow, sems) = rest[: len(parts)], rest[len(parts) :]
        number = 0
        for b, block in enumerate(blocks):
            first = 0
            for part in block:
                rows = part.shape[0]
                pltpu.make_async_copy(
                    sources[number], held.at[b, pl.ds(first, rows)], sems.at[b]
                ).start()
                number += 1
                first += rows
        for core in range(2):
            wide[pl.ds(core * lanes + (count + 1) * tokens, lanes - (count + 1) * tokens), :] = (
                jnp.zeros((lanes - (count + 1) * tokens, width), jnp.float32)
            )
        for j in range(count):
            place = numbers_ref[len(blocks) + j]
            columns = pl.ds(pl.multiple_of(place * share, 128), share)
            block = vectors[j][...].astype(jnp.float32)
            for core in range(2):
                wide[pl.ds(core * lanes, tokens), columns] = block[
                    core * tokens : (core + 1) * tokens
                ]
                first = pl.multiple_of(core * lanes + (place + 1) * tokens, 8)
                wide[pl.ds(first, tokens), :] = vectors[count * (core + 1) + j][...].astype(
                    jnp.float32
                )
        narrow[...] = wide[...].astype(narrow.dtype)
        lane = lax.broadcasted_iota(jnp.int32, (extent, lanes), 1)
        row = lax.broadcasted_iota(jnp.int32, (extent, lanes), 0)
        out_ref[...] = jnp.zeros_like(out_ref)

        def step(b, carry):
            pltpu.make_async_copy(held.at[b], held.at[b], sems.at[b]).wait()
            entry = row + numbers_ref[b]
            both = lax.dot_general(
                held[b],
                narrow[...],
                (((1,), (1,)), ((), ())),
                preferred_element_type=jnp.float32,
            )
            for core in range(2):
                group = slice(core * lanes, (core + 1) * lanes)
                raw = both[:, group]
                first = jnp.where(lane < tokens, raw, 0.0)
                for head in range(1, count + 1):
                    raw = raw + pltpu.roll(first, head * tokens, 1)
                logits = LOGIT_CAP * jnp.tanh(raw / LOGIT_CAP)
                tally = [jnp.sum(jnp.exp(logits), axis=0, keepdims=True)]
                for c in range(CAND):
                    match = entry == candidates_ref[c : c + 1, group]
                    tally.append(jnp.sum(jnp.where(match, logits, 0.0), axis=0, keepdims=True))
                out_ref[0 : CAND + 1, group] += jnp.concatenate(tally, axis=0)
            return carry

        lax.fori_loop(0, len(blocks), step, 0)

    return pl.pallas_call(
        kernel,
        out_shape=jax.ShapeDtypeStruct((16, 2 * lanes), jnp.float32),
        in_specs=[pl.BlockSpec(memory_space=pltpu.SMEM)]
        + [pl.BlockSpec(memory_space=pltpu.VMEM)] * (1 + len(inputs))
        + [pl.BlockSpec(memory_space=pltpu.HBM)] * len(parts),
        out_specs=pl.BlockSpec(memory_space=pltpu.VMEM),
        scratch_shapes=[
            pltpu.VMEM((len(blocks), extent, width), own[0].dtype),
            pltpu.VMEM((2 * lanes, width), jnp.float32),
            pltpu.VMEM((2 * lanes, width), own[0].dtype),
            pltpu.SemaphoreType.DMA((len(blocks),)),
        ],
        compiler_params=pltpu.CompilerParams(vmem_limit_bytes=40 * 2**20),
        cost_estimate=pl.CostEstimate(
            flops=4 * len(blocks) * extent * width * lanes,
            bytes_accessed=2 * len(blocks) * extent * width,
            transcendentals=4 * len(blocks) * extent * lanes,
        ),
    )(numbers, candidates, *inputs, *parts)


def local(
    hidden_state,
    input_projection,
    output_projection,
    norm_pre_attention,
    norm_post_attention,
    norm_pre_feedforward,
    norm_post_feedforward,
    norm_final,
    cache_keys,
    cache_values,
    cache_length,
    ancestors,
    accepted_path,
    gate_up_weight,
    down_weight,
    draft_weight,
    draft_bias,
    vocab_weight,
    candidate_tokens,
):
    f32, bf16 = jnp.float32, jnp.bfloat16
    plane = ("kv", "vocab")
    tok_block, _, width = hidden_state.shape
    seq_count = lax.axis_size("seq")
    kv_count = lax.axis_size("kv")
    tenants = lax.axis_size("vocab")
    groups = kv_count * tenants
    tree_size = tok_block * kv_count
    row_count = tok_block * groups
    seq_at = lax.axis_index("seq")
    kv_at = lax.axis_index("kv")
    vocab_at = lax.axis_index("vocab")
    ahead = [(seq_at + j) % seq_count for j in range(seq_count)]
    own_state = hidden_state[:, 0, :]

    tenant_state = jnp.concatenate([own_state, swap(own_state, "kv", 1)], axis=0)
    vocab_rows = vocab_weight.shape[0]
    quarter = vocab_rows // 4

    def exchange(first, count, event):
        rows = rows_after(vocab_weight, first, count, event)
        return swap(rows, "kv", 1), swap(rows, "vocab", 2)

    kv_0, row_0 = exchange(0, quarter, tenant_state)
    tenant_float = tenant_state.astype(f32)
    scaled_input = (tenant_float * norm_pre_attention).astype(bf16)
    projected = jnp.einsum(
        "td,dhc->htc", scaled_input, input_projection, preferred_element_type=f32
    ).astype(bf16)
    square_lanes = split_lanes(jnp.sum(tenant_float * tenant_float, axis=-1, keepdims=True))
    head_count = projected.shape[0]
    pair = 2 * HEAD_SIZE
    packed = jnp.concatenate(
        [
            projected[:, :, :pair],
            jnp.broadcast_to(square_lanes, (head_count,) + square_lanes.shape),
        ],
        axis=-1,
    )
    summed = add_up(
        [lax.dynamic_index_in_dim(packed, seq_at, 0, False)]
        + send_ahead(lambda j: lax.dynamic_index_in_dim(packed, ahead[j], 0, False))
    )
    inverse = inverse_of(summed[:, pair : pair + 1] + summed[:, pair + 64 : pair + 65] + still(kv_0, row_0))
    tree_mask = ancestors[0]
    tree_mask = jnp.where(
        kv_at == 0, tree_mask, jnp.roll(tree_mask, (tok_block, tok_block), (0, 1))
    )
    length = cache_length[0]
    depths = jnp.sum(tree_mask, axis=-1, keepdims=True) - 1
    frequency = 10000.0 ** (
        -2.0 * jnp.arange(HEAD_SIZE // 2, dtype=f32) / HEAD_SIZE
    )
    angles = (length + depths).astype(f32) * frequency
    cosine, sine = jnp.cos(angles), jnp.sin(angles)
    query_rows = jnp.concatenate(
        [
            rotate(summed[:, :HEAD_SIZE] * inverse, cosine, sine),
            rotate(summed[:, HEAD_SIZE:pair] * inverse, cosine, sine),
        ],
        axis=0,
    ).astype(bf16)
    kv_1, row_1 = exchange(quarter, quarter, query_rows)
    all_queries = in_order(collect(query_rows), ahead)
    fresh = projected[:, :, pair:]
    fresh = add_up(
        [lax.dynamic_index_in_dim(fresh, seq_at, 0, False)]
        + send_ahead(lambda j: lax.dynamic_index_in_dim(fresh, ahead[j], 0, False))
    )
    new_keys = rotate(fresh[:, :HEAD_SIZE] * inverse, cosine, sine).astype(bf16)
    new_values = (fresh[:, HEAD_SIZE:] * inverse).astype(bf16)

    block_size = cache_keys.shape[1]
    block_start = seq_at * block_size
    cache_cells = block_start + jnp.arange(block_size, dtype=jnp.int32)
    scores = jnp.einsum("hrc,shc->hrs", all_queries, cache_keys[0], preferred_element_type=f32)
    weights = jnp.where((cache_cells < length)[None, None, :], capped_weight(scores), 0.0)
    numerator = jnp.einsum(
        "hrs,shc->hrc", weights.astype(bf16), cache_values[0], preferred_element_type=f32
    )
    rows = 2 * tree_size
    sums = jnp.sum(weights, axis=-1)
    sums_high = sums.astype(bf16)
    sums_low = (sums - sums_high.astype(f32)).astype(bf16)
    sums = jnp.concatenate(
        [sums_high, sums_low, jnp.zeros((head_count, HEAD_SIZE - 2 * rows), bf16)], axis=-1
    )
    node_at = jnp.arange(tree_size, dtype=jnp.int32)
    node_at = jnp.where(kv_at == 0, node_at, (node_at + tok_block) % tree_size)
    accept_pick = (accepted_path[0][:, None] == node_at[None, :]).astype(bf16)
    accept_count = accept_pick.shape[0]
    chosen = jnp.concatenate(
        [
            jnp.dot(accept_pick, fresh_part, preferred_element_type=f32).astype(bf16)
            for fresh_part in (new_keys, new_values)
        ],
        axis=0,
    )
    packed = jnp.concatenate(
        [
            numerator.astype(bf16),
            sums[:, None, :],
            jnp.broadcast_to(chosen, (head_count,) + chosen.shape),
            jnp.zeros((head_count, 15 - 2 * accept_count, HEAD_SIZE), bf16),
        ],
        axis=1,
    )
    arrived = send_ahead(lambda j: lax.dynamic_index_in_dim(packed, ahead[j], 0, False))
    tree_scores = lax.dot_general(
        query_rows, new_keys, (((1,), (1,)), ((), ())), preferred_element_type=f32
    )
    seen = jnp.concatenate([tree_mask, tree_mask], axis=0) > 0
    tree_weights = jnp.where(seen, capped_weight(tree_scores), 0.0)
    tree_numerator = jnp.dot(tree_weights.astype(bf16), new_values, preferred_element_type=f32)
    tree_sums = jnp.sum(tree_weights, axis=-1, keepdims=True)
    behind = [(seq_at - j) % seq_count for j in range(seq_count)]
    tail = slice(rows + 1, rows + 1 + 2 * accept_count)
    accepted = in_order([chosen] + [block[tail] for block in arrived], behind)
    accepted = accepted.reshape(head_count, 2, accept_count, HEAD_SIZE).transpose(1, 2, 0, 3)
    summed = add_up([lax.dynamic_index_in_dim(packed, seq_at, 0, False)] + arrived)
    denominator = (summed[rows, :rows] + summed[rows, rows : 2 * rows])[:, None] + tree_sums
    attended = ((summed[:rows] + tree_numerator) / denominator).astype(bf16)
    attended = in_order(collect(attended), ahead).reshape(head_count, 2, tree_size, HEAD_SIZE)
    attention_out = jnp.einsum(
        "hgtc,hgcd->td",
        attended,
        output_projection.reshape(head_count, 2, HEAD_SIZE, width),
        preferred_element_type=f32,
    )
    theirs = (attention_out[tok_block:] + still(kv_1, row_1)).astype(bf16)
    attention_out = attention_out[:tok_block] + swap(theirs, "kv", 1).astype(f32)

    def token_totals(*values):
        lanes = 128 // len(values)
        columns = [jnp.sum(value, axis=-1, keepdims=True) for value in values]
        columns = jnp.concatenate(
            [jnp.broadcast_to(column, (tok_block, lanes)) for column in columns], axis=-1
        )
        columns = add_up(collect(columns))
        return [columns[:, k * lanes : k * lanes + 1] for k in range(len(values))]

    (totals,) = token_totals(attention_out * attention_out)
    first_sum = (
        own_state.astype(f32) + attention_out * inverse_of(totals) * norm_post_attention
    ).astype(bf16)

    all_state = lax.all_gather(first_sum, plane, axis=0, tiled=True)
    kv_2, row_2 = exchange(2 * quarter, 2 * quarter, all_state)
    all_float = all_state.astype(f32)
    scaled_ffn = (all_float * norm_pre_feedforward).astype(bf16)
    square_lanes = split_lanes(jnp.sum(all_float * all_float, axis=-1, keepdims=True))
    share = row_count // seq_count
    units = down_weight.shape[0]
    partial = jnp.einsum(
        "td,dcf->ctf", scaled_ffn, gate_up_weight, preferred_element_type=f32
    ).astype(bf16)

    keys_updated, values_updated, flag = update_caches(
        cache_keys[0],
        cache_values[0],
        accepted,
        (length - block_start + zero_at(partial)).reshape(1),
    )

    def rows_of(place):
        def window(values):
            return lax.dynamic_slice_in_dim(values, place * share, share, 0)

        return jnp.concatenate(
            [window(partial[0]), window(square_lanes), window(partial[1])], axis=-1
        )

    summed = add_up([rows_of(seq_at)] + send_ahead(lambda j: rows_of(ahead[j])))
    summed = summed + (flag[0, 0] + still(kv_2, row_2))
    far_0 = swap(rows_after(kv_0, 0, quarter, summed), "vocab", 2)
    far_2 = swap(rows_after(row_2, 0, quarter, summed), "kv", 1)
    inverse = inverse_of(summed[:, units : units + 1] + summed[:, units + 64 : units + 65])
    activated = (
        jax.nn.gelu(summed[:, :units] * inverse, approximate=True)
        * (summed[:, units + 128 :] * inverse)
    ).astype(bf16)
    activated = in_order(collect(activated), ahead).reshape(row_count, units)
    ffn_out = jnp.dot(activated, down_weight, preferred_element_type=f32)
    ffn_out = (ffn_out + still(far_0, far_2)).astype(bf16).reshape(groups, tok_block, width)
    ffn_out = add_up(list(lax.all_to_all(ffn_out, plane, 0, 0)))
    first_float = first_sum.astype(f32)
    scaled_out = ffn_out * norm_post_feedforward
    out_total, first_total, cross_total, scaled_total = token_totals(
        ffn_out * ffn_out, first_float * first_float, first_float * scaled_out, scaled_out * scaled_out
    )
    inverse = inverse_of(out_total)
    second_sum = (first_float + scaled_out * inverse).astype(bf16)
    second_total = first_total + inverse * (2.0 * cross_total + inverse * scaled_total)
    normed = (
        second_sum.astype(f32) * inverse_of(jnp.maximum(second_total, 0.0)) * norm_final
    ).astype(bf16)

    gathered = lax.all_gather(normed, plane, axis=0, tiled=True)
    lifted = jnp.einsum(
        "td,ndc->ntc", gathered, draft_weight, preferred_element_type=f32
    ).astype(bf16)
    summed = add_up(
        [lax.dynamic_index_in_dim(lifted, seq_at, 0, False)]
        + send_ahead(lambda j: lax.dynamic_index_in_dim(lifted, ahead[j], 0, False))
    )
    bias = lax.dynamic_index_in_dim(draft_bias, seq_at, 0, True)
    branch = jax.nn.silu(summed + bias).astype(bf16)
    branch = lax.all_to_all(branch, plane, 0, 1, tiled=True)
    far_1 = swap(rows_after(kv_1, 0, quarter, branch), "vocab", 2)
    far_3 = swap(rows_after(row_2, quarter, quarter, branch), "kv", 1)
    head_total = seq_count + 1
    lanes = 128
    base = collect(jnp.concatenate([normed, swap(normed, "vocab", 1)], axis=0))
    heads = collect(branch)
    other_heads = [swap(head, "vocab", 1) for head in heads]
    vocab_blocks = [
        [vocab_weight],
        [kv_0, kv_1, kv_2],
        [row_0, row_1, row_2],
        [far_0, far_1, far_2, far_3],
    ]
    starts = [
        (((kv_at ^ kv_bit) * seq_count + seq_at) * tenants + (vocab_at ^ vocab_bit)) * vocab_rows
        for kv_bit, vocab_bit in ((0, 0), (1, 0), (0, 2), (1, 2))
    ]
    spare = lanes - head_total * tok_block

    def candidates_of(tenant):
        tokens = lax.dynamic_slice(
            candidate_tokens,
            (0, kv_at * tok_block, tenant, 0),
            (head_total, tok_block, 1, CAND),
        )
        tokens = tokens.reshape(head_total * tok_block, CAND).T
        return jnp.pad(tokens, ((0, 0), (0, spare)), constant_values=-1)

    candidates = jnp.concatenate(
        [candidates_of(vocab_at), candidates_of(vocab_at ^ 1)], axis=1
    )
    tally = score_vocabulary(
        jnp.stack(starts + ahead).astype(jnp.int32),
        candidates,
        base,
        heads,
        other_heads,
        vocab_blocks,
        lanes,
    )
    tally = tally[:, :lanes] + swap(tally[:, lanes:], "vocab", 1)
    tally = add_up(collect(tally))
    tally = lax.all_gather(tally, plane, axis=0)
    tally = tally[:, : CAND + 1, : head_total * tok_block]
    tally = tally.reshape(kv_count, tenants, CAND + 1, head_total, tok_block)
    log_normalizer = jnp.log(tally[:, :, 0].transpose(2, 0, 3, 1)).reshape(
        head_total, tree_size, tenants
    )
    candidate_logits = (
        tally[:, :, 1:]
        .transpose(3, 0, 4, 1, 2)
        .reshape(head_total, tree_size, tenants, CAND)
    )
    return (keys_updated[None], values_updated[None], log_normalizer, candidate_logits)


def solution(mesh):
    placed = (
        P("kv", "vocab", "seq"),
        P("seq", "kv", None),
        P("kv", None, "seq"),
        P("seq"),
        P("seq"),
        P("seq"),
        P("seq"),
        P("seq"),
        P("vocab", "seq", "kv", None),
        P("vocab", "seq", "kv", None),
        P("vocab"),
        P("vocab", None, None),
        P("vocab", None),
        P("seq", None, ("kv", "vocab")),
        P(("kv", "vocab"), "seq"),
        P(None, "seq", ("kv", "vocab")),
        P(None, ("kv", "vocab")),
        P(("kv", "seq", "vocab"), None),
        P(),
    )
    body = local if fits(mesh.shape) else local_general
    return jax.shard_map(
        body,
        mesh=mesh,
        in_specs=placed,
        out_specs=(P("vocab", "seq", "kv", None), P("vocab", "seq", "kv", None), P(), P()),
        check_vma=False,
    )
```

```python
import jax
import jax.numpy as jnp
from jax import lax
from jax.experimental import pallas as pl
from jax.experimental.pallas import tpu as pltpu
from jax.sharding import PartitionSpec as P

MODEL_WIDTH = 3584
HEAD_SIZE = 256
CAND = 8


EPSILON = 1e-06
SCORE_CAP = 50.0
LOGIT_CAP = 30.0


def apply_rotary(vectors, token_positions):
    half_dim = vectors.shape[-1] // 2
    frequency = 10000.0 ** (-2.0 * jnp.arange(half_dim, dtype=jnp.float32) / vectors.shape[-1])
    angles = token_positions.astype(jnp.float32)[..., None] * frequency
    cosine = jnp.cos(angles)
    sine_part = jnp.sin(angles)
    first_half = vectors[..., :half_dim]
    second_half = vectors[..., half_dim:]
    return jnp.concatenate(
        [
            first_half * cosine - second_half * sine_part,
            second_half * cosine + first_half * sine_part,
        ],
        axis=-1,
    )


def capped_weight(scores):
    return jnp.exp(SCORE_CAP * jnp.tanh(scores * 0.0625 / SCORE_CAP))


def row_inverse(values):
    totals = lax.psum(jnp.sum(values * values, axis=-1), "seq")
    return lax.rsqrt(totals / MODEL_WIDTH + EPSILON)[:, None]


def gated_units(gate_up, squares):
    inverse = lax.rsqrt(squares / MODEL_WIDTH + EPSILON)[:, None]
    return (
        jax.nn.gelu(gate_up[:, 0] * inverse, approximate=True) * (gate_up[:, 1] * inverse)
    ).astype(jnp.bfloat16)


def local_general(
    hidden_state,
    input_projection,
    output_projection,
    norm_pre_attention,
    norm_post_attention,
    norm_pre_feedforward,
    norm_post_feedforward,
    norm_final,
    cache_keys,
    cache_values,
    cache_length,
    ancestors,
    accepted_path,
    gate_up_weight,
    down_weight,
    draft_weight,
    draft_bias,
    vocab_weight,
    candidate_tokens,
):
    tok_block = hidden_state.shape[0]
    kv_count = lax.axis_size("kv")
    tenants = lax.axis_size("vocab")
    tree_size = tok_block * kv_count
    own_state = hidden_state[:, 0, :]
    tenant_state = lax.all_gather(own_state, "kv", axis=0, tiled=True)
    tenant_float = tenant_state.astype(jnp.float32)
    scaled_input = (tenant_float * norm_pre_attention).astype(jnp.bfloat16)
    projected_rows = jnp.einsum(
        "td,dhc->thc", scaled_input, input_projection, preferred_element_type=jnp.float32
    )
    projected_rows, squares = lax.psum(
        (projected_rows, jnp.sum(tenant_float * tenant_float, axis=-1)), "seq"
    )
    projected_rows = projected_rows * lax.rsqrt(squares / MODEL_WIDTH + EPSILON)[:, None, None]
    head_count = projected_rows.shape[1]
    depths = jnp.sum(ancestors[0], axis=-1) - 1
    length = cache_length[0]
    token_positions = length + depths
    query_rows = apply_rotary(
        projected_rows[:, :, : 2 * HEAD_SIZE].reshape(tree_size, head_count, 2, HEAD_SIZE),
        token_positions[:, None, None],
    ).astype(jnp.bfloat16)
    new_keys = apply_rotary(
        projected_rows[:, :, 2 * HEAD_SIZE : 3 * HEAD_SIZE], token_positions[:, None]
    ).astype(jnp.bfloat16)
    new_values = projected_rows[:, :, 3 * HEAD_SIZE :].astype(jnp.bfloat16)
    block_size = cache_keys.shape[1]
    block_start = lax.axis_index("seq") * block_size
    cache_cells = block_start + jnp.arange(block_size, dtype=jnp.int32)
    scores = jnp.einsum(
        "thgc,shc->thgs", query_rows, cache_keys[0], preferred_element_type=jnp.float32
    )
    weights = jnp.where((cache_cells < length)[None, None, None, :], capped_weight(scores), 0.0)
    numerator = jnp.einsum(
        "thgs,shc->thgc",
        weights.astype(jnp.bfloat16),
        cache_values[0],
        preferred_element_type=jnp.float32,
    )
    numerator, denominator = lax.psum((numerator, jnp.sum(weights, axis=-1)), "seq")
    tree_scores = jnp.einsum(
        "thgc,uhc->thgu", query_rows, new_keys, preferred_element_type=jnp.float32
    )
    tree_weights = jnp.where(ancestors[0][:, None, None, :] > 0, capped_weight(tree_scores), 0.0)
    numerator = numerator + jnp.einsum(
        "thgu,uhc->thgc",
        tree_weights.astype(jnp.bfloat16),
        new_values,
        preferred_element_type=jnp.float32,
    )
    denominator = denominator + jnp.sum(tree_weights, axis=-1)
    attended = (
        (numerator / denominator[..., None])
        .astype(jnp.bfloat16)
        .reshape(tree_size, head_count * 2 * HEAD_SIZE)
    )
    out_matrix = output_projection.reshape(head_count * 2 * HEAD_SIZE, output_projection.shape[2])
    attention_out = lax.psum_scatter(
        jnp.dot(attended, out_matrix, preferred_element_type=jnp.float32),
        "kv",
        scatter_dimension=0,
        tiled=True,
    )
    first_sum = (
        own_state.astype(jnp.float32)
        + attention_out * row_inverse(attention_out) * norm_post_attention
    ).astype(jnp.bfloat16)
    all_state = lax.all_gather(first_sum, ("kv", "vocab"), axis=0, tiled=True)
    all_float = all_state.astype(jnp.float32)
    scaled_ffn = (all_float * norm_pre_feedforward).astype(jnp.bfloat16)
    gate_up = jnp.einsum(
        "td,dcf->tcf", scaled_ffn, gate_up_weight, preferred_element_type=jnp.float32
    )
    ffn_squares = jnp.sum(all_float * all_float, axis=-1)
    gate_up, ffn_squares = lax.psum((gate_up, ffn_squares), "seq")
    activated = gated_units(gate_up, ffn_squares)
    ffn_out = lax.psum_scatter(
        jnp.dot(activated, down_weight, preferred_element_type=jnp.float32),
        ("kv", "vocab"),
        scatter_dimension=0,
        tiled=True,
    )
    first_float = first_sum.astype(jnp.float32)
    second_sum = (first_float + ffn_out * row_inverse(ffn_out) * norm_post_feedforward).astype(
        jnp.bfloat16
    )
    second_float = second_sum.astype(jnp.float32)
    normed = (second_float * row_inverse(second_float) * norm_final).astype(jnp.bfloat16)
    gathered = lax.all_gather(normed, ("kv", "vocab"), axis=0, tiled=True)
    lifted = jnp.einsum("td,ndc->tnc", gathered, draft_weight, preferred_element_type=jnp.float32)
    lifted = lax.psum(lifted.astype(jnp.bfloat16), "seq").astype(jnp.float32)
    branch = jax.nn.silu(lifted + draft_bias).astype(jnp.bfloat16)
    row_count = gathered.shape[0]
    vocab_rows = vocab_weight.shape[0]
    draft_count = branch.shape[1]
    columns = vocab_weight
    base_logits = lax.dot_general(
        lax.all_gather(gathered, "seq", axis=1, tiled=True),
        columns,
        (((1,), (1,)), ((), ())),
        preferred_element_type=jnp.float32,
    )
    columns = vocab_weight
    draft_extra = jnp.einsum(
        "tnc,vc->tnv",
        lax.all_gather(branch, ("kv", "vocab"), axis=2, tiled=True),
        columns,
        preferred_element_type=jnp.float32,
    )
    raw_logits = jnp.concatenate(
        [base_logits[:, None, :], base_logits[:, None, :] + draft_extra], axis=1
    )
    logits = LOGIT_CAP * jnp.tanh(raw_logits / LOGIT_CAP)
    totals = jnp.sum(jnp.exp(logits), axis=-1)
    head_total = draft_count + 1
    candidates = candidate_tokens.reshape(head_total, kv_count, tok_block, tenants, CAND)
    candidates = jnp.transpose(candidates, (0, 1, 3, 2, 4)).reshape(head_total, row_count, CAND)
    candidates = jnp.transpose(candidates, (1, 0, 2))
    vocab_start = lax.axis_index(("kv", "seq", "vocab")) * vocab_rows
    local_tokens = candidates - vocab_start
    entry_index = jnp.arange(vocab_rows, dtype=jnp.int32)
    picked = jnp.stack(
        [
            jnp.sum(
                jnp.where(entry_index == local_tokens[:, :, column : column + 1], logits, 0.0),
                axis=-1,
            )
            for column in range(CAND)
        ],
        axis=-1,
    )
    totals, picked = lax.psum((totals, picked), ("kv", "seq", "vocab"))
    log_totals = jnp.transpose(jnp.log(totals)).reshape(head_total, kv_count, tenants, tok_block)
    log_normalizer = jnp.transpose(log_totals, (0, 1, 3, 2)).reshape(head_total, tree_size, tenants)
    picked = jnp.transpose(picked, (1, 0, 2)).reshape(
        head_total, kv_count, tenants, tok_block, CAND
    )
    candidate_logits = jnp.transpose(picked, (0, 1, 3, 2, 4)).reshape(
        head_total, tree_size, tenants, CAND
    )
    accept_count = accepted_path.shape[1]
    slot_rows = length + jnp.arange(accept_count, dtype=jnp.int32)
    tree_nodes = jnp.arange(tree_size, dtype=jnp.int32)
    matches = (cache_cells[:, None, None] == slot_rows[None, :, None]) & (
        accepted_path[0][None, :, None] == tree_nodes[None, None, :]
    )
    selector = jnp.sum(matches.astype(jnp.float32), axis=1)
    written = jnp.sum(selector, axis=-1) > 0.0
    selector = selector.astype(jnp.bfloat16)

    def write_path(old_block, fresh_rows):
        moved_rows = jnp.dot(
            selector, fresh_rows.reshape(tree_size, -1), preferred_element_type=jnp.float32
        ).astype(jnp.bfloat16)
        return jnp.where(
            written[:, None], moved_rows, old_block[0].reshape(block_size, -1)
        ).reshape(old_block.shape)

    keys_updated = write_path(cache_keys, new_keys)
    values_updated = write_path(cache_values, new_values)
    return (keys_updated, values_updated, log_normalizer, candidate_logits)


def fits(sizes):
    return sizes["kv"] == 2 and sizes["vocab"] == 4 and sizes["seq"] == 4


def send_ahead(pick):
    count = lax.axis_size("seq")
    return [
        lax.ppermute(pick(j), "seq", [(i, (i + j) % count) for i in range(count)])
        for j in range(1, count)
    ]


def collect(block):
    count = lax.axis_size("seq")
    return [block] + [
        lax.ppermute(block, "seq", [(i, (i - j) % count) for i in range(count)])
        for j in range(1, count)
    ]


def in_order(blocks, ahead):
    result = jnp.zeros((len(blocks),) + blocks[0].shape, blocks[0].dtype)
    for j, block in enumerate(blocks):
        result = lax.dynamic_update_index_in_dim(result, block, ahead[j], 0)
    return result


def add_up(blocks):
    total = blocks[0].astype(jnp.float32)
    for block in blocks[1:]:
        total = total + block.astype(jnp.float32)
    return total


def swap(values, axis, bit):
    count = lax.axis_size(axis)
    return lax.ppermute(values, axis, [(i, i ^ bit) for i in range(count)])


def split_lanes(values):
    high = values.astype(jnp.bfloat16)
    low = (values - high.astype(jnp.float32)).astype(jnp.bfloat16)
    shape = values.shape[:-1] + (64,)
    return jnp.concatenate([jnp.broadcast_to(high, shape), jnp.broadcast_to(low, shape)], axis=-1)


def hold(values, *events):
    count = len(values)
    anywhere = pl.BlockSpec(memory_space=pl.ANY)
    return pl.pallas_call(
        lambda *refs: None,
        out_shape=[jax.ShapeDtypeStruct(value.shape, value.dtype) for value in values],
        in_specs=[anywhere] * (count + len(events)),
        out_specs=[anywhere] * count,
        input_output_aliases={k: k for k in range(count)},
    )(*values, *events)


def inverse_of(totals):
    return lax.rsqrt(totals / MODEL_WIDTH + EPSILON)


def rotate(vectors, cosine, sine):
    half = vectors.shape[-1] // 2
    first, second = vectors[..., :half], vectors[..., half:]
    return jnp.concatenate(
        [first * cosine - second * sine, second * cosine + first * sine], axis=-1
    )


def copy_rows(sources, targets, *events):
    unit = 64
    number = len(sources)
    shapes = [
        (sum(rows for _, _, rows in parts),) + sources[0].shape[1:] for parts in targets
    ]
    moves = []
    for t, parts in enumerate(targets):
        filled = 0
        for source, first, rows in parts:
            for p in range(0, rows, unit):
                size = min(unit, rows - p)
                moves.append((source, first + p, t, filled + p, size))
            filled += rows

    def kernel(*refs):
        inputs, rest = refs[:number], refs[number + len(events) :]
        outputs, (held, get, put) = rest[: len(shapes)], rest[len(shapes) :]
        pairs = []
        for k, (source, first, target, place, size) in enumerate(moves):
            slot = held.at[k, pl.ds(0, size)]
            pairs.append(
                (
                    pltpu.make_async_copy(
                        inputs[source].at[pl.ds(first, size)], slot, get.at[k]
                    ),
                    pltpu.make_async_copy(
                        slot, outputs[target].at[pl.ds(place, size)], put.at[k]
                    ),
                )
            )
        for k, (inward, _) in enumerate(pairs):
            inward.start(priority=k % 2)
        for k, (inward, outward) in enumerate(pairs):
            inward.wait()
            outward.start(priority=k % 2)
        for _, outward in pairs:
            outward.wait()

    row = sources[0].shape[1:]
    dtype = sources[0].dtype
    return pl.pallas_call(
        kernel,
        out_shape=[jax.ShapeDtypeStruct(shape, dtype) for shape in shapes],
        in_specs=[pl.BlockSpec(memory_space=pl.ANY)] * (number + len(events)),
        out_specs=[pl.BlockSpec(memory_space=pltpu.HBM)] * len(shapes),
        scratch_shapes=[
            pltpu.VMEM((len(moves), unit) + row, dtype),
            pltpu.SemaphoreType.DMA((len(moves),)),
            pltpu.SemaphoreType.DMA((len(moves),)),
        ],
        compiler_params=pltpu.CompilerParams(vmem_limit_bytes=58 * 2**20),
        cost_estimate=pl.CostEstimate(
            flops=0,
            bytes_accessed=sum(4 * shape[0] * shape[1] for shape in shapes),
            transcendentals=0,
        ),
    )(*sources, *events)


def update_cache(cache, numbers, packed, arrived, first_row, accept, event):
    slots, heads, size = cache.shape
    count = 1 + len(arrived)
    tail = pl.ds(packed.shape[1] - 16, 16)
    first_row = first_row - (packed.shape[1] - 16)
    piece = 256
    parts = slots // piece

    def kernel(numbers_ref, source, _, packed_ref, *rest):
        arrived_refs, rest = rest[: count - 1], rest[count - 1 :]
        target, flag, held, tails, stage, ready, get, put, sem = rest
        flag[...] = jnp.zeros_like(flag)

        tail_copies = []
        for j in range(count):
            head = lax.rem(numbers_ref[1] + (count - j), count)
            block = packed_ref.at[0, tail] if j == 0 else arrived_refs[j - 1].at[tail]
            tail_copies.append(pltpu.make_async_copy(block, tails.at[head], sem.at[j]))
            tail_copies[j].start()
        pairs = []
        for k in range(parts):
            window = pl.ds(k * piece, piece)
            pairs.append(
                (
                    pltpu.make_async_copy(source.at[window], held.at[k], get.at[k]),
                    pltpu.make_async_copy(held.at[k], target.at[window], put.at[k]),
                )
            )
        for k, (inward, _) in enumerate(pairs):
            inward.start(priority=k % 2)
        for k, (inward, outward) in enumerate(pairs):
            inward.wait()
            outward.start(priority=k % 2)
        for copy in tail_copies:
            copy.wait()
        for head in range(count):
            rows = tails[head].astype(jnp.float32)
            for r in range(accept):
                stage[r, head : head + 1, :] = rows[first_row + r : first_row + r + 1]
        ready[...] = stage[...].astype(ready.dtype)
        for _, outward in pairs:
            outward.wait()
        for a in range(accept):
            slot = numbers_ref[0] + a

            @pl.when((slot >= 0) & (slot < slots))
            def _():
                copy = pltpu.make_async_copy(
                    ready.at[pl.ds(a, 1)], target.at[pl.ds(slot, 1)], sem.at[0]
                )
                copy.start()
                copy.wait()

    return pl.pallas_call(
        kernel,
        out_shape=(
            jax.ShapeDtypeStruct(cache.shape, cache.dtype),
            jax.ShapeDtypeStruct((8, 128), jnp.float32),
        ),
        in_specs=[
            pl.BlockSpec(memory_space=pltpu.SMEM),
            pl.BlockSpec(memory_space=pltpu.HBM),
        ]
        + [pl.BlockSpec(memory_space=pl.ANY)] * (1 + count),
        out_specs=(
            pl.BlockSpec(memory_space=pltpu.HBM),
            pl.BlockSpec(memory_space=pltpu.VMEM),
        ),
        scratch_shapes=[
            pltpu.VMEM((parts, piece, heads, size), cache.dtype),
            pltpu.VMEM((count, 16, size), cache.dtype),
            pltpu.VMEM((accept, heads, size), jnp.float32),
            pltpu.VMEM((accept, heads, size), cache.dtype),
            pltpu.SemaphoreType.DMA((parts,)),
            pltpu.SemaphoreType.DMA((parts,)),
            pltpu.SemaphoreType.DMA((count,)),
        ],
        compiler_params=pltpu.CompilerParams(vmem_limit_bytes=56 * 2**20),
        cost_estimate=pl.CostEstimate(
            flops=0, bytes_accessed=0, transcendentals=0
        ),
    )(numbers, cache, event, packed, *arrived)


def score_vocabulary(numbers, candidates, heads, vocab_blocks, half, lanes):
    tokens = heads[0][0].shape[0]
    count = len(heads[0])
    groups = len(heads)
    parts = [part for block in vocab_blocks for part in block]
    arrays = []
    for array, _ in parts:
        if not any(array is known for known in arrays):
            arrays.append(array)
    blocks, extent, width = len(vocab_blocks), 2 * half, arrays[0].shape[1]
    share = width // count
    unit = 64
    inputs = [head for group in heads for head in group]

    def kernel(numbers_ref, *rest):
        candidate_refs, rest = rest[:groups], rest[groups:]
        vectors, rest = rest[: len(inputs)], rest[len(inputs) :]
        sources, rest = rest[: len(arrays)], rest[len(arrays) :]
        *out_refs, held, arrived, wide, narrow, square, row_sems, sems = rest
        arrivals = []
        for k, vector in enumerate(vectors):
            arrivals.append(pltpu.make_async_copy(vector, arrived.at[k], sems.at[k]))
            arrivals[k].start(priority=k % 2)
        for k, (array, first) in enumerate(parts):
            source = sources[[array is known for known in arrays].index(True)]
            for q, p in enumerate(range(0, half, unit)):
                pltpu.make_async_copy(
                    source.at[pl.ds(first + p, unit)],
                    held.at[k // 2, pl.ds(k % 2 * half + p, unit)],
                    row_sems.at[k // 2],
                ).start(priority=q % 2)
        spare = lanes - (count + 1) * tokens
        wanted = []
        for group, ref in enumerate(candidate_refs):
            wide[pl.ds((group + 1) * lanes - spare, spare), :] = jnp.zeros(
                (spare, width), jnp.float32
            )
            square[...] = jnp.full((lanes, 128), -1, jnp.int32)
            for head in range(count + 1):
                square[head * tokens : (head + 1) * tokens, 0:CAND] = ref[head]
            wanted.append(square[...].T[0:CAND])
        for k, arrival in enumerate(arrivals):
            arrival.wait()
            group, j = k // count, k % count
            place = numbers_ref[2 * blocks + j]
            columns = pl.ds(pl.multiple_of(place * share, 128), share)
            wide[pl.ds(group * lanes, tokens), columns] = arrived[k, :, width:].astype(
                jnp.float32
            )
            first = pl.multiple_of(group * lanes + (place + 1) * tokens, 8)
            wide[pl.ds(first, tokens), :] = arrived[k, :, :width].astype(jnp.float32)
        narrow[...] = wide[...].astype(narrow.dtype)
        lane = lax.broadcasted_iota(jnp.int32, (half, lanes), 1)
        row = lax.broadcasted_iota(jnp.int32, (half, lanes), 0)
        for out_ref in out_refs:
            out_ref[...] = jnp.zeros_like(out_ref)

        def step(b, low):
            pltpu.make_async_copy(held.at[b], held.at[b], row_sems.at[b]).wait()
            both = lax.dot_general(
                held[b],
                narrow[low * lanes : (low + 2) * lanes, :],
                (((1,), (1,)), ((), ())),
                preferred_element_type=jnp.float32,
            )
            for group in (low, low + 1):
                place = slice((group - low) * lanes, (group - low + 1) * lanes)
                for part in range(2):
                    raw = both[part * half : (part + 1) * half, place]
                    entry = row + numbers_ref[2 * b + part]
                    first = jnp.where(lane < tokens, raw, 0.0)
                    for head in range(1, count + 1):
                        raw = raw + pltpu.roll(first, head * tokens, 1)
                    logits = LOGIT_CAP * jnp.tanh(raw / LOGIT_CAP)
                    tally = [jnp.sum(jnp.exp(logits), axis=0, keepdims=True)]
                    for c in range(CAND):
                        match = entry == wanted[group][c : c + 1]
                        tally.append(
                            jnp.sum(jnp.where(match, logits, 0.0), axis=0, keepdims=True)
                        )
                    out_refs[group][0 : CAND + 1, :] += jnp.concatenate(tally, axis=0)

        for low in range(2):

            def run(b, carry, low=low):
                step(b, low)
                return carry

            middle = blocks // 2
            lax.fori_loop(low * middle, (low + 1) * middle, run, 0)

    return pl.pallas_call(
        kernel,
        out_shape=[jax.ShapeDtypeStruct((16, lanes), jnp.float32)] * groups,
        in_specs=[pl.BlockSpec(memory_space=pltpu.SMEM)]
        + [pl.BlockSpec(memory_space=pltpu.VMEM)] * groups
        + [pl.BlockSpec(memory_space=pl.ANY)] * (len(inputs) + len(arrays)),
        out_specs=[pl.BlockSpec(memory_space=pltpu.VMEM)] * groups,
        scratch_shapes=[
            pltpu.VMEM((blocks, extent, width), inputs[0].dtype),
            pltpu.VMEM((len(inputs),) + inputs[0].shape, inputs[0].dtype),
            pltpu.VMEM((groups * lanes, width), jnp.float32),
            pltpu.VMEM((groups * lanes, width), inputs[0].dtype),
            pltpu.VMEM((lanes, 128), jnp.int32),
            pltpu.SemaphoreType.DMA((blocks,)),
            pltpu.SemaphoreType.DMA((len(inputs),)),
        ],
        compiler_params=pltpu.CompilerParams(vmem_limit_bytes=58 * 2**20),
        cost_estimate=pl.CostEstimate(
            flops=4 * blocks * extent * width * lanes,
            bytes_accessed=2 * blocks * extent * width,
            transcendentals=4 * blocks * extent * lanes,
        ),
    )(numbers, *candidates, *inputs, *arrays)


def project_out(places, attended, weight, own_rows):
    rows = attended[0].shape[0] // 2
    size = attended[0].shape[1]
    count, _, width = weight.shape

    def kernel(places_ref, *refs):
        blocks, (weight_ref, theirs_ref, own_ref) = refs[:count], refs[count:]
        total = jnp.zeros((rows, width), jnp.float32)
        for j, block in enumerate(blocks):
            for g in range(2):
                total = total + jnp.dot(
                    block[g * rows : (g + 1) * rows, :],
                    weight_ref[places_ref[j], g * size : (g + 1) * size, :],
                    preferred_element_type=jnp.float32,
                )
        own_ref[...] = total[:own_rows]
        theirs_ref[...] = total[own_rows:].astype(theirs_ref.dtype)

    vmem = pl.BlockSpec(memory_space=pltpu.VMEM)
    return pl.pallas_call(
        kernel,
        out_shape=[
            jax.ShapeDtypeStruct((rows - own_rows, width), attended[0].dtype),
            jax.ShapeDtypeStruct((own_rows, width), jnp.float32),
        ],
        in_specs=[pl.BlockSpec(memory_space=pltpu.SMEM)] + [vmem] * (count + 1),
        out_specs=[vmem] * 2,
        compiler_params=pltpu.CompilerParams(vmem_limit_bytes=16 * 2**20),
        cost_estimate=pl.CostEstimate(
            flops=2 * rows * weight.size, bytes_accessed=2 * weight.size, transcendentals=0
        ),
    )(places, *attended, weight)


def local(
    hidden_state,
    input_projection,
    output_projection,
    norm_pre_attention,
    norm_post_attention,
    norm_pre_feedforward,
    norm_post_feedforward,
    norm_final,
    cache_keys,
    cache_values,
    cache_length,
    ancestors,
    accepted_path,
    gate_up_weight,
    down_weight,
    draft_weight,
    draft_bias,
    vocab_weight,
    candidate_tokens,
):
    f32, bf16 = jnp.float32, jnp.bfloat16
    plane = ("kv", "vocab")
    tok_block, _, width = hidden_state.shape
    seq_count = lax.axis_size("seq")
    kv_count = lax.axis_size("kv")
    tenants = lax.axis_size("vocab")
    groups = kv_count * tenants
    tree_size = tok_block * kv_count
    row_count = tok_block * groups
    seq_at = lax.axis_index("seq")
    kv_at = lax.axis_index("kv")
    vocab_at = lax.axis_index("vocab")
    ahead = [(seq_at + j) % seq_count for j in range(seq_count)]
    own_state = hidden_state[:, 0, :]

    tenant_state = jnp.concatenate([own_state, swap(own_state, "kv", 1)], axis=0)
    vocab_rows = vocab_weight.shape[0]
    half = vocab_rows // 2

    tenant_float = tenant_state.astype(f32)
    scaled_input = (tenant_float * norm_pre_attention).astype(bf16)
    projected = jnp.einsum(
        "td,dhc->htc", scaled_input, input_projection, preferred_element_type=f32
    ).astype(bf16)
    square_lanes = split_lanes(jnp.sum(tenant_float * tenant_float, axis=-1, keepdims=True))
    head_count = projected.shape[0]
    pair = 2 * HEAD_SIZE
    packed = jnp.concatenate(
        [
            projected,
            jnp.broadcast_to(square_lanes, (head_count,) + square_lanes.shape),
        ],
        axis=-1,
    )
    arrived = send_ahead(lambda j: lax.dynamic_index_in_dim(packed, ahead[j], 0, False))
    summed = add_up([lax.dynamic_index_in_dim(packed, seq_at, 0, False)] + arrived)
    whole = 2 * pair
    inverse = inverse_of(summed[:, whole : whole + 1] + summed[:, whole + 64 : whole + 65])
    tree_mask = ancestors[0]
    tree_mask = jnp.where(
        kv_at == 0, tree_mask, jnp.roll(tree_mask, (tok_block, tok_block), (0, 1))
    )
    length = cache_length[0]
    depths = jnp.sum(tree_mask, axis=-1, keepdims=True) - 1
    frequency = 10000.0 ** (
        -2.0 * jnp.arange(HEAD_SIZE // 2, dtype=f32) / HEAD_SIZE
    )
    angles = (length + depths).astype(f32) * frequency
    cosine, sine = jnp.cos(angles), jnp.sin(angles)
    query_rows = jnp.concatenate(
        [
            rotate(summed[:, :HEAD_SIZE] * inverse, cosine, sine),
            rotate(summed[:, HEAD_SIZE:pair] * inverse, cosine, sine),
        ],
        axis=0,
    ).astype(bf16)
    all_queries = in_order(collect(query_rows), ahead)
    new_keys = rotate(summed[:, pair : pair + HEAD_SIZE] * inverse, cosine, sine).astype(bf16)
    new_values = (summed[:, pair + HEAD_SIZE : whole] * inverse).astype(bf16)

    block_size = cache_keys.shape[1]
    block_start = seq_at * block_size
    cache_cells = block_start + jnp.arange(block_size, dtype=jnp.int32)
    scores = jnp.einsum("hrc,shc->hrs", all_queries, cache_keys[0], preferred_element_type=f32)
    weights = jnp.where((cache_cells < length)[None, None, :], capped_weight(scores), 0.0)
    numerator = jnp.einsum(
        "hrs,shc->hrc", weights.astype(bf16), cache_values[0], preferred_element_type=f32
    )
    rows = 2 * tree_size
    sums = jnp.sum(weights, axis=-1)
    sums_high = sums.astype(bf16)
    sums_low = (sums - sums_high.astype(f32)).astype(bf16)
    sums = jnp.concatenate(
        [sums_high, sums_low, jnp.zeros((head_count, HEAD_SIZE - 2 * rows), bf16)], axis=-1
    )
    node_at = jnp.arange(tree_size, dtype=jnp.int32)
    node_at = jnp.where(kv_at == 0, node_at, (node_at + tok_block) % tree_size)
    accept_pick = (accepted_path[0][:, None] == node_at[None, :]).astype(bf16)
    accept_count = accept_pick.shape[0]
    chosen = jnp.concatenate(
        [
            jnp.dot(accept_pick, fresh_part, preferred_element_type=f32).astype(bf16)
            for fresh_part in (new_keys, new_values)
        ],
        axis=0,
    )
    packed = jnp.concatenate(
        [
            numerator.astype(bf16),
            sums[:, None, :],
            jnp.broadcast_to(chosen, (head_count,) + chosen.shape),
            jnp.zeros((head_count, 15 - 2 * accept_count, HEAD_SIZE), bf16),
        ],
        axis=1,
    )
    arrived = send_ahead(lambda j: lax.dynamic_index_in_dim(packed, ahead[j], 0, False))
    tree_scores = lax.dot_general(
        query_rows, new_keys, (((1,), (1,)), ((), ())), preferred_element_type=f32
    )
    seen = jnp.concatenate([tree_mask, tree_mask], axis=0) > 0
    tree_weights = jnp.where(seen, capped_weight(tree_scores), 0.0)
    tree_numerator = jnp.dot(tree_weights.astype(bf16), new_values, preferred_element_type=f32)
    tree_sums = jnp.sum(tree_weights, axis=-1, keepdims=True)
    head_blocks = (packed, arrived)
    summed = add_up([lax.dynamic_index_in_dim(packed, seq_at, 0, False)] + arrived)
    denominator = (summed[rows, :rows] + summed[rows, rows : 2 * rows])[:, None] + tree_sums
    attended = ((summed[:rows] + tree_numerator) / denominator).astype(bf16)
    core_rows = swap(vocab_weight, "vocab", 1)
    theirs, attention_out = project_out(
        jnp.stack(ahead).astype(jnp.int32),
        list(hold([attended], core_rows)) + collect(attended)[1:],
        output_projection,
        tok_block,
    )
    first_part, second_part = copy_rows(
        [vocab_weight],
        [[(0, 0, half)], [(0, half, vocab_rows - half)]],
        theirs,
    )
    (theirs,) = hold([swap(theirs, "kv", 1)], first_part, second_part)
    attention_out = attention_out + theirs.astype(f32)

    def token_totals(*values):
        lanes = 128 // len(values)
        columns = [jnp.sum(value, axis=-1, keepdims=True) for value in values]
        columns = jnp.concatenate(
            [jnp.broadcast_to(column, (tok_block, lanes)) for column in columns], axis=-1
        )
        columns = add_up(collect(columns))
        return [columns[:, k * lanes : k * lanes + 1] for k in range(len(values))]

    own_float = own_state.astype(f32)

    def add_normed(state, update, gain):
        scaled = update * gain
        update_total, state_total, cross_total, scaled_total = token_totals(
            update * update, state * state, state * scaled, scaled * scaled
        )
        inverse = inverse_of(update_total)
        total = state_total + inverse * (2.0 * cross_total + inverse * scaled_total)
        return state + scaled * inverse, inverse_of(jnp.maximum(total, 0.0))

    first_sum, inverse = add_normed(own_float, attention_out, norm_post_attention)
    scaled_ffn = (first_sum * inverse * norm_pre_feedforward).astype(bf16)

    scaled_ffn = lax.all_gather(scaled_ffn, plane, axis=0, tiled=True)
    share = row_count // seq_count
    units = down_weight.shape[0]
    partial = jnp.einsum(
        "td,dcf->ctf", scaled_ffn, gate_up_weight, preferred_element_type=f32
    ).astype(bf16)

    first_part, second_part = hold([first_part, second_part], partial)
    first_part, second_part = swap(first_part, "kv", 1), swap(second_part, "vocab", 2)
    slot_numbers = jnp.stack([length - block_start, seq_at])
    keys_updated, flag = update_cache(
        cache_keys[0], slot_numbers, *head_blocks, rows + 1, accept_count, partial
    )

    head_total = seq_count + 1
    lanes = 128
    starts = [
        (((kv_at ^ kv_bit) * seq_count + seq_at) * tenants + (vocab_at ^ vocab_bit)) * vocab_rows
        + first
        for kv_bit, vocab_bit, first in (
            (0, 0, 0),
            (0, 1, 0),
            (1, 0, 0),
            (1, 1, 0),
            (0, 0, half),
            (0, 1, half),
            (0, 2, half),
            (0, 3, half),
        )
    ]
    later = (flag[0, 0] != 0.0).astype(jnp.int32)
    candidates = [
        lax.dynamic_slice(
            candidate_tokens,
            (0, block * tok_block + later, tenant, 0),
            (head_total, tok_block, 1, CAND),
        )[:, :, 0]
        for block, tenant in (
            (kv_at, vocab_at ^ 2),
            (kv_at, vocab_at),
            (kv_at ^ 1, vocab_at),
        )
    ]
    numbers = jnp.stack(starts + ahead).astype(jnp.int32) + later

    def rows_of(place):
        return lax.dynamic_slice_in_dim(partial, place * share, share, 1)

    summed = add_up([rows_of(seq_at)] + send_ahead(lambda j: rows_of(ahead[j])))
    activated = (jax.nn.gelu(summed[0], approximate=True) * summed[1]).astype(bf16)
    (activated,) = hold([activated], flag)
    values_updated, value_flag = update_cache(
        cache_values[0],
        slot_numbers,
        *head_blocks,
        rows + 1 + accept_count,
        accept_count,
        activated,
    )
    ffn_out = in_order(
        [
            jnp.dot(block, down_weight, preferred_element_type=f32).astype(bf16)
            for block in collect(activated)
        ],
        ahead,
    ).reshape(groups, tok_block, width)
    ffn_out, numbers, *candidates = hold(
        [ffn_out, numbers, *candidates], first_part, second_part, value_flag
    )
    ffn_out = add_up(list(lax.all_to_all(ffn_out, plane, 0, 0)))
    second_sum, inverse = add_normed(first_sum, ffn_out, norm_post_feedforward)
    normed = (second_sum * inverse * norm_final).astype(bf16)

    gathered = lax.all_gather(normed, plane, axis=0, tiled=True)
    lifted = jnp.einsum(
        "td,ndc->ntc", gathered, draft_weight, preferred_element_type=f32
    ).astype(bf16)
    places = [("vocab", 2), (None, 0), ("kv", 1)]

    def around(values):
        return [values if axis is None else swap(values, axis, bit) for axis, bit in places]

    first_part, second_part = hold([first_part, second_part], lifted)
    core_first, core_second = swap(first_part, "vocab", 1), swap(second_part, "vocab", 1)
    summed = add_up(
        [lax.dynamic_index_in_dim(lifted, seq_at, 0, False)]
        + send_ahead(lambda j: lax.dynamic_index_in_dim(lifted, ahead[j], 0, False))
    )
    bias = lax.dynamic_index_in_dim(draft_bias, seq_at, 0, True)
    branch = jax.nn.silu(summed + bias).astype(bf16)
    vocab_blocks = [
        [(vocab_weight, 0), (core_rows, 0)],
        [(first_part, 0), (core_first, 0)],
        [(vocab_weight, half), (core_rows, half)],
        [(second_part, 0), (core_second, 0)],
    ]
    (branch,) = hold([branch], core_first, core_second)
    branch = lax.all_to_all(branch, plane, 0, 1, tiled=True)
    heads = collect(jnp.concatenate([branch, normed], axis=1))
    heads = [list(group) for group in zip(*[around(head) for head in heads])]
    tally = score_vocabulary(
        numbers, candidates, heads, vocab_blocks, half, lanes
    )
    tally = tally[1] + (swap(tally[0], "vocab", 2) + swap(tally[2], "kv", 1))
    tally = add_up(collect(tally))
    tally = lax.all_gather(tally, plane, axis=0)
    tally = tally[:, : CAND + 1, : head_total * tok_block]
    tally = tally.reshape(kv_count, tenants, CAND + 1, head_total, tok_block)
    log_normalizer = jnp.log(tally[:, :, 0].transpose(2, 0, 3, 1)).reshape(
        head_total, tree_size, tenants
    )
    candidate_logits = (
        tally[:, :, 1:]
        .transpose(3, 0, 4, 1, 2)
        .reshape(head_total, tree_size, tenants, CAND)
    )
    return (keys_updated[None], values_updated[None], log_normalizer, candidate_logits)


def solution(mesh):
    placed = (
        P("kv", "vocab", "seq"),
        P("seq", "kv", None),
        P("kv", None, "seq"),
        P("seq"),
        P("seq"),
        P("seq"),
        P("seq"),
        P("seq"),
        P("vocab", "seq", "kv", None),
        P("vocab", "seq", "kv", None),
        P("vocab"),
        P("vocab", None, None),
        P("vocab", None),
        P("seq", None, ("kv", "vocab")),
        P(("kv", "vocab"), "seq"),
        P(None, "seq", ("kv", "vocab")),
        P(None, ("kv", "vocab")),
        P(("kv", "seq", "vocab"), None),
        P(),
    )
    body = local if fits(mesh.shape) else local_general
    return jax.shard_map(
        body,
        mesh=mesh,
        in_specs=placed,
        out_specs=(P("vocab", "seq", "kv", None), P("vocab", "seq", "kv", None), P(), P()),
        check_vma=False,
    )
```

```python
import jax
import jax.numpy as jnp
from jax import lax
from jax.experimental import pallas as pl
from jax.experimental.pallas import tpu as pltpu
from jax.sharding import PartitionSpec as P

MODEL_WIDTH = 3584
HEAD_SIZE = 256
CAND = 8


EPSILON = 1e-06
SCORE_CAP = 50.0
LOGIT_CAP = 30.0


def apply_rotary(vectors, token_positions):
    half_dim = vectors.shape[-1] // 2
    frequency = 10000.0 ** (-2.0 * jnp.arange(half_dim, dtype=jnp.float32) / vectors.shape[-1])
    angles = token_positions.astype(jnp.float32)[..., None] * frequency
    cosine = jnp.cos(angles)
    sine_part = jnp.sin(angles)
    first_half = vectors[..., :half_dim]
    second_half = vectors[..., half_dim:]
    return jnp.concatenate(
        [
            first_half * cosine - second_half * sine_part,
            second_half * cosine + first_half * sine_part,
        ],
        axis=-1,
    )


def capped_weight(scores):
    return jnp.exp(SCORE_CAP * jnp.tanh(scores * 0.0625 / SCORE_CAP))


def row_inverse(values):
    totals = lax.psum(jnp.sum(values * values, axis=-1), "seq")
    return lax.rsqrt(totals / MODEL_WIDTH + EPSILON)[:, None]


def gated_units(gate_up, squares):
    inverse = lax.rsqrt(squares / MODEL_WIDTH + EPSILON)[:, None]
    return (
        jax.nn.gelu(gate_up[:, 0] * inverse, approximate=True) * (gate_up[:, 1] * inverse)
    ).astype(jnp.bfloat16)


def local_general(
    hidden_state,
    input_projection,
    output_projection,
    norm_pre_attention,
    norm_post_attention,
    norm_pre_feedforward,
    norm_post_feedforward,
    norm_final,
    cache_keys,
    cache_values,
    cache_length,
    ancestors,
    accepted_path,
    gate_up_weight,
    down_weight,
    draft_weight,
    draft_bias,
    vocab_weight,
    candidate_tokens,
):
    tok_block = hidden_state.shape[0]
    kv_count = lax.axis_size("kv")
    tenants = lax.axis_size("vocab")
    tree_size = tok_block * kv_count
    own_state = hidden_state[:, 0, :]
    tenant_state = lax.all_gather(own_state, "kv", axis=0, tiled=True)
    tenant_float = tenant_state.astype(jnp.float32)
    scaled_input = (tenant_float * norm_pre_attention).astype(jnp.bfloat16)
    projected_rows = jnp.einsum(
        "td,dhc->thc", scaled_input, input_projection, preferred_element_type=jnp.float32
    )
    projected_rows, squares = lax.psum(
        (projected_rows, jnp.sum(tenant_float * tenant_float, axis=-1)), "seq"
    )
    projected_rows = projected_rows * lax.rsqrt(squares / MODEL_WIDTH + EPSILON)[:, None, None]
    head_count = projected_rows.shape[1]
    depths = jnp.sum(ancestors[0], axis=-1) - 1
    length = cache_length[0]
    token_positions = length + depths
    query_rows = apply_rotary(
        projected_rows[:, :, : 2 * HEAD_SIZE].reshape(tree_size, head_count, 2, HEAD_SIZE),
        token_positions[:, None, None],
    ).astype(jnp.bfloat16)
    new_keys = apply_rotary(
        projected_rows[:, :, 2 * HEAD_SIZE : 3 * HEAD_SIZE], token_positions[:, None]
    ).astype(jnp.bfloat16)
    new_values = projected_rows[:, :, 3 * HEAD_SIZE :].astype(jnp.bfloat16)
    block_size = cache_keys.shape[1]
    block_start = lax.axis_index("seq") * block_size
    cache_cells = block_start + jnp.arange(block_size, dtype=jnp.int32)
    scores = jnp.einsum(
        "thgc,shc->thgs", query_rows, cache_keys[0], preferred_element_type=jnp.float32
    )
    weights = jnp.where((cache_cells < length)[None, None, None, :], capped_weight(scores), 0.0)
    numerator = jnp.einsum(
        "thgs,shc->thgc",
        weights.astype(jnp.bfloat16),
        cache_values[0],
        preferred_element_type=jnp.float32,
    )
    numerator, denominator = lax.psum((numerator, jnp.sum(weights, axis=-1)), "seq")
    tree_scores = jnp.einsum(
        "thgc,uhc->thgu", query_rows, new_keys, preferred_element_type=jnp.float32
    )
    tree_weights = jnp.where(ancestors[0][:, None, None, :] > 0, capped_weight(tree_scores), 0.0)
    numerator = numerator + jnp.einsum(
        "thgu,uhc->thgc",
        tree_weights.astype(jnp.bfloat16),
        new_values,
        preferred_element_type=jnp.float32,
    )
    denominator = denominator + jnp.sum(tree_weights, axis=-1)
    attended = (
        (numerator / denominator[..., None])
        .astype(jnp.bfloat16)
        .reshape(tree_size, head_count * 2 * HEAD_SIZE)
    )
    out_matrix = output_projection.reshape(head_count * 2 * HEAD_SIZE, output_projection.shape[2])
    attention_out = lax.psum_scatter(
        jnp.dot(attended, out_matrix, preferred_element_type=jnp.float32),
        "kv",
        scatter_dimension=0,
        tiled=True,
    )
    first_sum = (
        own_state.astype(jnp.float32)
        + attention_out * row_inverse(attention_out) * norm_post_attention
    ).astype(jnp.bfloat16)
    all_state = lax.all_gather(first_sum, ("kv", "vocab"), axis=0, tiled=True)
    all_float = all_state.astype(jnp.float32)
    scaled_ffn = (all_float * norm_pre_feedforward).astype(jnp.bfloat16)
    gate_up = jnp.einsum(
        "td,dcf->tcf", scaled_ffn, gate_up_weight, preferred_element_type=jnp.float32
    )
    ffn_squares = jnp.sum(all_float * all_float, axis=-1)
    gate_up, ffn_squares = lax.psum((gate_up, ffn_squares), "seq")
    activated = gated_units(gate_up, ffn_squares)
    ffn_out = lax.psum_scatter(
        jnp.dot(activated, down_weight, preferred_element_type=jnp.float32),
        ("kv", "vocab"),
        scatter_dimension=0,
        tiled=True,
    )
    first_float = first_sum.astype(jnp.float32)
    second_sum = (first_float + ffn_out * row_inverse(ffn_out) * norm_post_feedforward).astype(
        jnp.bfloat16
    )
    second_float = second_sum.astype(jnp.float32)
    normed = (second_float * row_inverse(second_float) * norm_final).astype(jnp.bfloat16)
    gathered = lax.all_gather(normed, ("kv", "vocab"), axis=0, tiled=True)
    lifted = jnp.einsum("td,ndc->tnc", gathered, draft_weight, preferred_element_type=jnp.float32)
    lifted = lax.psum(lifted.astype(jnp.bfloat16), "seq").astype(jnp.float32)
    branch = jax.nn.silu(lifted + draft_bias).astype(jnp.bfloat16)
    row_count = gathered.shape[0]
    vocab_rows = vocab_weight.shape[0]
    draft_count = branch.shape[1]
    columns = vocab_weight
    base_logits = lax.dot_general(
        lax.all_gather(gathered, "seq", axis=1, tiled=True),
        columns,
        (((1,), (1,)), ((), ())),
        preferred_element_type=jnp.float32,
    )
    columns = vocab_weight
    draft_extra = jnp.einsum(
        "tnc,vc->tnv",
        lax.all_gather(branch, ("kv", "vocab"), axis=2, tiled=True),
        columns,
        preferred_element_type=jnp.float32,
    )
    raw_logits = jnp.concatenate(
        [base_logits[:, None, :], base_logits[:, None, :] + draft_extra], axis=1
    )
    logits = LOGIT_CAP * jnp.tanh(raw_logits / LOGIT_CAP)
    totals = jnp.sum(jnp.exp(logits), axis=-1)
    head_total = draft_count + 1
    candidates = candidate_tokens.reshape(head_total, kv_count, tok_block, tenants, CAND)
    candidates = jnp.transpose(candidates, (0, 1, 3, 2, 4)).reshape(head_total, row_count, CAND)
    candidates = jnp.transpose(candidates, (1, 0, 2))
    vocab_start = lax.axis_index(("kv", "seq", "vocab")) * vocab_rows
    local_tokens = candidates - vocab_start
    entry_index = jnp.arange(vocab_rows, dtype=jnp.int32)
    picked = jnp.stack(
        [
            jnp.sum(
                jnp.where(entry_index == local_tokens[:, :, column : column + 1], logits, 0.0),
                axis=-1,
            )
            for column in range(CAND)
        ],
        axis=-1,
    )
    totals, picked = lax.psum((totals, picked), ("kv", "seq", "vocab"))
    log_totals = jnp.transpose(jnp.log(totals)).reshape(head_total, kv_count, tenants, tok_block)
    log_normalizer = jnp.transpose(log_totals, (0, 1, 3, 2)).reshape(head_total, tree_size, tenants)
    picked = jnp.transpose(picked, (1, 0, 2)).reshape(
        head_total, kv_count, tenants, tok_block, CAND
    )
    candidate_logits = jnp.transpose(picked, (0, 1, 3, 2, 4)).reshape(
        head_total, tree_size, tenants, CAND
    )
    accept_count = accepted_path.shape[1]
    slot_rows = length + jnp.arange(accept_count, dtype=jnp.int32)
    tree_nodes = jnp.arange(tree_size, dtype=jnp.int32)
    matches = (cache_cells[:, None, None] == slot_rows[None, :, None]) & (
        accepted_path[0][None, :, None] == tree_nodes[None, None, :]
    )
    selector = jnp.sum(matches.astype(jnp.float32), axis=1)
    written = jnp.sum(selector, axis=-1) > 0.0
    selector = selector.astype(jnp.bfloat16)

    def write_path(old_block, fresh_rows):
        moved_rows = jnp.dot(
            selector, fresh_rows.reshape(tree_size, -1), preferred_element_type=jnp.float32
        ).astype(jnp.bfloat16)
        return jnp.where(
            written[:, None], moved_rows, old_block[0].reshape(block_size, -1)
        ).reshape(old_block.shape)

    keys_updated = write_path(cache_keys, new_keys)
    values_updated = write_path(cache_values, new_values)
    return (keys_updated, values_updated, log_normalizer, candidate_logits)


def fits(sizes):
    return sizes["kv"] == 2 and sizes["vocab"] == 4 and sizes["seq"] == 4


def send_ahead(pick):
    count = lax.axis_size("seq")
    return [
        lax.ppermute(pick(j), "seq", [(i, (i + j) % count) for i in range(count)])
        for j in range(1, count)
    ]


def collect(block):
    count = lax.axis_size("seq")
    return [block] + [
        lax.ppermute(block, "seq", [(i, (i - j) % count) for i in range(count)])
        for j in range(1, count)
    ]


def in_order(blocks, ahead):
    result = jnp.zeros((len(blocks),) + blocks[0].shape, blocks[0].dtype)
    for j, block in enumerate(blocks):
        result = lax.dynamic_update_index_in_dim(result, block, ahead[j], 0)
    return result


def add_up(blocks):
    total = blocks[0].astype(jnp.float32)
    for block in blocks[1:]:
        total = total + block.astype(jnp.float32)
    return total


def swap(values, axis, bit):
    count = lax.axis_size(axis)
    return lax.ppermute(values, axis, [(i, i ^ bit) for i in range(count)])


def split_lanes(values):
    high = values.astype(jnp.bfloat16)
    low = (values - high.astype(jnp.float32)).astype(jnp.bfloat16)
    shape = values.shape[:-1] + (64,)
    return jnp.concatenate([jnp.broadcast_to(high, shape), jnp.broadcast_to(low, shape)], axis=-1)


def hold(values, *events):
    count = len(values)
    anywhere = pl.BlockSpec(memory_space=pl.ANY)
    return pl.pallas_call(
        lambda *refs: None,
        out_shape=[jax.ShapeDtypeStruct(value.shape, value.dtype) for value in values],
        in_specs=[anywhere] * (count + len(events)),
        out_specs=[anywhere] * count,
        input_output_aliases={k: k for k in range(count)},
    )(*values, *events)


def inverse_of(totals):
    return lax.rsqrt(totals / MODEL_WIDTH + EPSILON)


def rotate(vectors, cosine, sine):
    half = vectors.shape[-1] // 2
    first, second = vectors[..., :half], vectors[..., half:]
    return jnp.concatenate(
        [first * cosine - second * sine, second * cosine + first * sine], axis=-1
    )


def copy_rows(sources, targets, *events):
    unit = 64
    number = len(sources)
    shapes = [
        (sum(rows for _, _, rows in parts),) + sources[0].shape[1:] for parts in targets
    ]
    moves = []
    for t, parts in enumerate(targets):
        filled = 0
        for source, first, rows in parts:
            for p in range(0, rows, unit):
                size = min(unit, rows - p)
                moves.append((source, first + p, t, filled + p, size))
            filled += rows

    def kernel(*refs):
        inputs, rest = refs[:number], refs[number + len(events) :]
        outputs, (held, get, put) = rest[: len(shapes)], rest[len(shapes) :]
        pairs = []
        for k, (source, first, target, place, size) in enumerate(moves):
            slot = held.at[k, pl.ds(0, size)]
            pairs.append(
                (
                    pltpu.make_async_copy(
                        inputs[source].at[pl.ds(first, size)], slot, get.at[k]
                    ),
                    pltpu.make_async_copy(
                        slot, outputs[target].at[pl.ds(place, size)], put.at[k]
                    ),
                )
            )
        for k, (inward, _) in enumerate(pairs):
            inward.start(priority=k % 2)
        for k, (inward, outward) in enumerate(pairs):
            inward.wait()
            outward.start(priority=k % 2)
        for _, outward in pairs:
            outward.wait()

    row = sources[0].shape[1:]
    dtype = sources[0].dtype
    return pl.pallas_call(
        kernel,
        out_shape=[jax.ShapeDtypeStruct(shape, dtype) for shape in shapes],
        in_specs=[pl.BlockSpec(memory_space=pl.ANY)] * (number + len(events)),
        out_specs=[pl.BlockSpec(memory_space=pltpu.HBM)] * len(shapes),
        scratch_shapes=[
            pltpu.VMEM((len(moves), unit) + row, dtype),
            pltpu.SemaphoreType.DMA((len(moves),)),
            pltpu.SemaphoreType.DMA((len(moves),)),
        ],
        compiler_params=pltpu.CompilerParams(vmem_limit_bytes=58 * 2**20),
        cost_estimate=pl.CostEstimate(
            flops=0,
            bytes_accessed=sum(4 * shape[0] * shape[1] for shape in shapes),
            transcendentals=0,
        ),
    )(*sources, *events)


def update_cache(cache, numbers, packed, arrived, first_row, accept, *events):
    slots, heads, size = cache.shape
    count = 1 + len(arrived)
    tail = pl.ds(packed.shape[1] - 16, 16)
    first_row = first_row - (packed.shape[1] - 16)
    piece = 256
    parts = slots // piece

    def kernel(numbers_ref, source, packed_ref, *rest):
        arrived_refs, rest = rest[: count - 1], rest[count - 1 + len(events) :]
        target, flag, held, tails, stage, ready, get, put, sem = rest
        flag[...] = jnp.zeros_like(flag)

        tail_copies = []
        for j in range(count):
            head = lax.rem(numbers_ref[1] + (count - j), count)
            block = packed_ref.at[0, tail] if j == 0 else arrived_refs[j - 1].at[tail]
            tail_copies.append(pltpu.make_async_copy(block, tails.at[head], sem.at[j]))
            tail_copies[j].start()
        pairs = []
        for k in range(parts):
            window = pl.ds(k * piece, piece)
            pairs.append(
                (
                    pltpu.make_async_copy(source.at[window], held.at[k], get.at[k]),
                    pltpu.make_async_copy(held.at[k], target.at[window], put.at[k]),
                )
            )
        for k, (inward, _) in enumerate(pairs):
            inward.start(priority=k % 2)
        for k, (inward, outward) in enumerate(pairs):
            inward.wait()
            outward.start(priority=k % 2)
        for copy in tail_copies:
            copy.wait()
        for head in range(count):
            rows = tails[head].astype(jnp.float32)
            for r in range(accept):
                stage[r, head : head + 1, :] = rows[first_row + r : first_row + r + 1]
        ready[...] = stage[...].astype(ready.dtype)
        for _, outward in pairs:
            outward.wait()
        for a in range(accept):
            slot = numbers_ref[0] + a

            @pl.when((slot >= 0) & (slot < slots))
            def _():
                copy = pltpu.make_async_copy(
                    ready.at[pl.ds(a, 1)], target.at[pl.ds(slot, 1)], sem.at[0]
                )
                copy.start()
                copy.wait()

    return pl.pallas_call(
        kernel,
        out_shape=(
            jax.ShapeDtypeStruct(cache.shape, cache.dtype),
            jax.ShapeDtypeStruct((8, 128), jnp.float32),
        ),
        in_specs=[
            pl.BlockSpec(memory_space=pltpu.SMEM),
            pl.BlockSpec(memory_space=pltpu.HBM),
        ]
        + [pl.BlockSpec(memory_space=pl.ANY)] * (count + len(events)),
        out_specs=(
            pl.BlockSpec(memory_space=pltpu.HBM),
            pl.BlockSpec(memory_space=pltpu.VMEM),
        ),
        scratch_shapes=[
            pltpu.VMEM((parts, piece, heads, size), cache.dtype),
            pltpu.VMEM((count, 16, size), cache.dtype),
            pltpu.VMEM((accept, heads, size), jnp.float32),
            pltpu.VMEM((accept, heads, size), cache.dtype),
            pltpu.SemaphoreType.DMA((parts,)),
            pltpu.SemaphoreType.DMA((parts,)),
            pltpu.SemaphoreType.DMA((count,)),
        ],
        compiler_params=pltpu.CompilerParams(vmem_limit_bytes=56 * 2**20),
        cost_estimate=pl.CostEstimate(
            flops=0, bytes_accessed=4 * cache.size, transcendentals=0
        ),
    )(numbers, cache, packed, *arrived, *events)


def score_vocabulary(numbers, candidates, heads, vocab_blocks, half, lanes):
    tokens = heads[0][0].shape[0]
    count = len(heads[0])
    groups = len(heads)
    parts = [part for block in vocab_blocks for part in block]
    arrays = []
    for array, _ in parts:
        if not any(array is known for known in arrays):
            arrays.append(array)
    blocks, extent, width = len(vocab_blocks), 2 * half, arrays[0].shape[1]
    share = width // count
    unit = 64
    inputs = [head for group in heads for head in group]

    def kernel(numbers_ref, *rest):
        candidate_refs, rest = rest[:groups], rest[groups:]
        vectors, rest = rest[: len(inputs)], rest[len(inputs) :]
        sources, rest = rest[: len(arrays)], rest[len(arrays) :]
        out_ref, held, arrived, wide, narrow, square, row_sems, sems = rest
        arrivals = []
        for k, vector in enumerate(vectors):
            arrivals.append(pltpu.make_async_copy(vector, arrived.at[k], sems.at[k]))
            arrivals[k].start(priority=0)
        def fetch(b):
            for k in (2 * b, 2 * b + 1):
                array, first = parts[k]
                source = sources[[array is known for known in arrays].index(True)]
                for q, p in enumerate(range(0, half, unit)):
                    pltpu.make_async_copy(
                        source.at[pl.ds(first + p, unit)],
                        held.at[b, pl.ds(k % 2 * half + p, unit)],
                        row_sems.at[b],
                    ).start(priority=1)

        fetch(0)
        fetch(1)
        fetch(2)
        fetch(3)
        spare = lanes - (count + 1) * tokens
        wanted = []
        for group, ref in enumerate(candidate_refs):
            square[...] = jnp.full((lanes, 128), -1, jnp.int32)
            square[0:tokens, 0:CAND] = ref[0]
            for j in range(count):
                row_at = (j + 1) * tokens
                square[row_at : row_at + tokens, 0:CAND] = ref[numbers_ref[2 * blocks + j] + 1]
            wanted.append(square[...].T[0:CAND])
        def assemble(group):
            for j in range(count):
                arrivals[group * count + j].wait()
                columns = pl.ds(pl.multiple_of(numbers_ref[2 * blocks + j] * share, 128), share)
                wide[group * tokens : (group + 1) * tokens, columns] = arrived[
                    group * count + j, :, width:
                ].astype(jnp.float32)
            pieces = [wide[group * tokens : (group + 1) * tokens, :]]
            pieces += [arrived[group * count + j, :, :width].astype(jnp.float32) for j in range(count)]
            pieces += [jnp.zeros((spare, width), jnp.float32)]
            narrow[group * lanes : (group + 1) * lanes, :] = jnp.concatenate(
                pieces, axis=0
            ).astype(narrow.dtype)
        assemble(0)
        assemble(1)
        lane = lax.broadcasted_iota(jnp.int32, (half, lanes), 1)
        row = lax.broadcasted_iota(jnp.int32, (half, lanes), 0)
        out_ref[...] = jnp.zeros_like(out_ref)

        def step(b, low):
            pltpu.make_async_copy(held.at[b], held.at[b], row_sems.at[b]).wait()
            both = lax.dot_general(
                held[b],
                narrow[low * lanes : (low + 2) * lanes, :],
                (((1,), (1,)), ((), ())),
                preferred_element_type=jnp.float32,
            )
            for group in (low, low + 1):
                place = slice((group - low) * lanes, (group - low + 1) * lanes)
                for part in range(2):
                    raw = both[part * half : (part + 1) * half, place]
                    entry = row + numbers_ref[2 * b + part]
                    first = jnp.where(lane < tokens, raw, 0.0)
                    for head in range(1, count + 1):
                        raw = raw + pltpu.roll(first, head * tokens, 1)
                    logits = LOGIT_CAP * jnp.tanh(raw / LOGIT_CAP)
                    tally = [jnp.sum(jnp.exp(logits), axis=0, keepdims=True)]
                    for c in range(CAND):
                        match = entry == wanted[group][c : c + 1]
                        tally.append(
                            jnp.sum(jnp.where(match, logits, 0.0), axis=0, keepdims=True)
                        )
                    out_ref[16 * group : 16 * group + CAND + 1, :] += jnp.concatenate(tally, axis=0)

        for low in range(2):
            if low == 1:
                assemble(2)

            def run(b, carry, low=low):
                step(b, low)
                return carry

            middle = blocks // 2
            lax.fori_loop(low * middle, (low + 1) * middle, run, 0)
        turn = numbers_ref[2 * blocks] * tokens
        across = lax.broadcasted_iota(jnp.int32, out_ref.shape, 1)
        values = out_ref[...]
        ahead = pltpu.roll(values, turn, 1)
        wrapped = pltpu.roll(values, turn + lanes - count * tokens, 1)
        turned = jnp.where(across - turn >= tokens, ahead, wrapped)
        out_ref[...] = jnp.where(across < tokens, values, turned)

    return pl.pallas_call(
        kernel,
        out_shape=jax.ShapeDtypeStruct((16 * groups, lanes), jnp.float32),
        in_specs=[pl.BlockSpec(memory_space=pltpu.SMEM)]
        + [pl.BlockSpec(memory_space=pltpu.VMEM)] * groups
        + [pl.BlockSpec(memory_space=pl.ANY)] * (len(inputs) + len(arrays)),
        out_specs=pl.BlockSpec(memory_space=pltpu.VMEM),
        scratch_shapes=[
            pltpu.VMEM((blocks, extent, width), inputs[0].dtype),
            pltpu.VMEM((len(inputs),) + inputs[0].shape, inputs[0].dtype),
            pltpu.VMEM((groups * tokens, width), jnp.float32),
            pltpu.VMEM((groups * lanes, width), inputs[0].dtype),
            pltpu.VMEM((lanes, 128), jnp.int32),
            pltpu.SemaphoreType.DMA((blocks,)),
            pltpu.SemaphoreType.DMA((len(inputs),)),
        ],
        compiler_params=pltpu.CompilerParams(vmem_limit_bytes=58 * 2**20),
        cost_estimate=pl.CostEstimate(
            flops=4 * blocks * extent * width * lanes,
            bytes_accessed=2 * blocks * extent * width,
            transcendentals=4 * blocks * extent * lanes,
        ),
    )(numbers, *candidates, *inputs, *arrays)


def activate_draft(parts, normed, kv_count, seq_count):
    number, tokens, columns = parts.shape
    tenants = number // (kv_count * seq_count)
    width = kv_count * tenants * columns

    def kernel(parts_ref, normed_ref, out_ref):
        pair = []
        for kv in range(kv_count):
            for tenant in range(tenants):
                total = 0.0
                for seq in range(seq_count):
                    block = parts_ref[(kv * seq_count + seq) * tenants + tenant]
                    total = total + block.astype(jnp.float32)
                pair.append(total / (1.0 + jnp.exp(-total)))
                if len(pair) == 2:
                    place = (kv * tenants + tenant - 1) * columns
                    out_ref[:, place : place + 2 * columns] = jnp.concatenate(
                        pair, axis=1
                    ).astype(out_ref.dtype)
                    pair = []
        out_ref[:, width:] = normed_ref[...]

    vmem = pl.BlockSpec(memory_space=pltpu.VMEM)
    return pl.pallas_call(
        kernel,
        out_shape=jax.ShapeDtypeStruct((tokens, width + normed.shape[1]), normed.dtype),
        in_specs=[vmem] * 2,
        out_specs=vmem,
    )(parts, normed)


def project_out(places, attended, weight, own_rows):
    rows = attended[0].shape[0] // 2
    size = attended[0].shape[1]
    count, _, width = weight.shape

    def kernel(places_ref, *refs):
        blocks, (weight_ref, theirs_ref, own_ref) = refs[:count], refs[count:]
        total = jnp.zeros((rows, width), jnp.float32)
        for j, block in enumerate(blocks):
            for g in range(2):
                total = total + jnp.dot(
                    block[g * rows : (g + 1) * rows, :],
                    weight_ref[places_ref[j], g * size : (g + 1) * size, :],
                    preferred_element_type=jnp.float32,
                )
        own_ref[...] = total[:own_rows]
        theirs_ref[...] = total[own_rows:].astype(theirs_ref.dtype)

    vmem = pl.BlockSpec(memory_space=pltpu.VMEM)
    return pl.pallas_call(
        kernel,
        out_shape=[
            jax.ShapeDtypeStruct((rows - own_rows, width), attended[0].dtype),
            jax.ShapeDtypeStruct((own_rows, width), jnp.float32),
        ],
        in_specs=[pl.BlockSpec(memory_space=pltpu.SMEM)] + [vmem] * (count + 1),
        out_specs=[vmem] * 2,
        compiler_params=pltpu.CompilerParams(vmem_limit_bytes=16 * 2**20),
        cost_estimate=pl.CostEstimate(
            flops=2 * rows * weight.size, bytes_accessed=2 * weight.size, transcendentals=0
        ),
    )(places, *attended, weight)


def local(
    hidden_state,
    input_projection,
    output_projection,
    norm_pre_attention,
    norm_post_attention,
    norm_pre_feedforward,
    norm_post_feedforward,
    norm_final,
    cache_keys,
    cache_values,
    cache_length,
    ancestors,
    accepted_path,
    gate_up_weight,
    down_weight,
    draft_weight,
    draft_bias,
    vocab_weight,
    candidate_tokens,
):
    f32, bf16 = jnp.float32, jnp.bfloat16
    plane = ("kv", "vocab")
    tok_block, _, width = hidden_state.shape
    seq_count = lax.axis_size("seq")
    kv_count = lax.axis_size("kv")
    tenants = lax.axis_size("vocab")
    groups = kv_count * tenants
    tree_size = tok_block * kv_count
    row_count = tok_block * groups
    seq_at = lax.axis_index("seq")
    kv_at = lax.axis_index("kv")
    vocab_at = lax.axis_index("vocab")
    ahead = [(seq_at + j) % seq_count for j in range(seq_count)]
    own_state = hidden_state[:, 0, :]

    tenant_state = jnp.concatenate([own_state, swap(own_state, "kv", 1)], axis=0)
    vocab_rows = vocab_weight.shape[0]
    half = vocab_rows // 2

    tenant_float = tenant_state.astype(f32)
    scaled_input = (tenant_float * norm_pre_attention).astype(bf16)
    projected = jnp.einsum(
        "td,dhc->htc", scaled_input, input_projection, preferred_element_type=f32
    ).astype(bf16)
    square_lanes = split_lanes(jnp.sum(tenant_float * tenant_float, axis=-1, keepdims=True))
    head_count = projected.shape[0]
    pair = 2 * HEAD_SIZE
    packed = jnp.concatenate(
        [
            projected,
            jnp.broadcast_to(square_lanes, (head_count,) + square_lanes.shape),
        ],
        axis=-1,
    )
    arrived = send_ahead(lambda j: lax.dynamic_index_in_dim(packed, ahead[j], 0, False))
    summed = add_up([lax.dynamic_index_in_dim(packed, seq_at, 0, False)] + arrived)
    whole = 2 * pair
    inverse = inverse_of(summed[:, whole : whole + 1] + summed[:, whole + 64 : whole + 65])
    tree_mask = ancestors[0]
    tree_mask = jnp.where(
        kv_at == 0, tree_mask, jnp.roll(tree_mask, (tok_block, tok_block), (0, 1))
    )
    length = cache_length[0]
    depths = jnp.sum(tree_mask, axis=-1, keepdims=True) - 1
    frequency = 10000.0 ** (
        -2.0 * jnp.arange(HEAD_SIZE // 2, dtype=f32) / HEAD_SIZE
    )
    angles = (length + depths).astype(f32) * frequency
    cosine, sine = jnp.cos(angles), jnp.sin(angles)
    query_rows = jnp.concatenate(
        [
            rotate(summed[:, :HEAD_SIZE] * inverse, cosine, sine),
            rotate(summed[:, HEAD_SIZE:pair] * inverse, cosine, sine),
        ],
        axis=0,
    ).astype(bf16)
    all_queries = in_order(collect(query_rows), ahead)
    new_keys = rotate(summed[:, pair : pair + HEAD_SIZE] * inverse, cosine, sine).astype(bf16)
    new_values = (summed[:, pair + HEAD_SIZE : whole] * inverse).astype(bf16)

    block_size = cache_keys.shape[1]
    block_start = seq_at * block_size
    cache_cells = block_start + jnp.arange(block_size, dtype=jnp.int32)
    scores = jnp.einsum("hrc,shc->hrs", all_queries, cache_keys[0], preferred_element_type=f32)
    weights = jnp.where((cache_cells < length)[None, None, :], capped_weight(scores), 0.0)
    numerator = jnp.einsum(
        "hrs,shc->hrc", weights.astype(bf16), cache_values[0], preferred_element_type=f32
    )
    rows = 2 * tree_size
    sums = jnp.sum(weights, axis=-1)
    sums_high = sums.astype(bf16)
    sums_low = (sums - sums_high.astype(f32)).astype(bf16)
    sums = jnp.concatenate(
        [sums_high, sums_low, jnp.zeros((head_count, HEAD_SIZE - 2 * rows), bf16)], axis=-1
    )
    node_at = jnp.arange(tree_size, dtype=jnp.int32)
    node_at = jnp.where(kv_at == 0, node_at, (node_at + tok_block) % tree_size)
    accept_pick = (accepted_path[0][:, None] == node_at[None, :]).astype(bf16)
    accept_count = accept_pick.shape[0]
    chosen = jnp.concatenate(
        [
            jnp.dot(accept_pick, fresh_part, preferred_element_type=f32).astype(bf16)
            for fresh_part in (new_keys, new_values)
        ],
        axis=0,
    )
    packed = jnp.concatenate(
        [
            numerator.astype(bf16),
            sums[:, None, :],
            jnp.broadcast_to(chosen, (head_count,) + chosen.shape),
            jnp.zeros((head_count, 15 - 2 * accept_count, HEAD_SIZE), bf16),
        ],
        axis=1,
    )
    arrived = send_ahead(lambda j: lax.dynamic_index_in_dim(packed, ahead[j], 0, False))
    tree_scores = lax.dot_general(
        query_rows, new_keys, (((1,), (1,)), ((), ())), preferred_element_type=f32
    )
    seen = jnp.concatenate([tree_mask, tree_mask], axis=0) > 0
    tree_weights = jnp.where(seen, capped_weight(tree_scores), 0.0)
    tree_numerator = jnp.dot(tree_weights.astype(bf16), new_values, preferred_element_type=f32)
    tree_sums = jnp.sum(tree_weights, axis=-1, keepdims=True)
    head_blocks = (packed, arrived)
    summed = add_up([lax.dynamic_index_in_dim(packed, seq_at, 0, False)] + arrived)
    denominator = (summed[rows, :rows] + summed[rows, rows : 2 * rows])[:, None] + tree_sums
    attended = ((summed[:rows] + tree_numerator) / denominator).astype(bf16)
    theirs, attention_out = project_out(
        jnp.stack(ahead).astype(jnp.int32),
        collect(attended),
        output_projection,
        tok_block,
    )
    first_part, second_part = copy_rows(
        [vocab_weight],
        [[(0, 0, half)], [(0, half, vocab_rows - half)]],
        theirs,
    )
    (theirs,) = hold([swap(theirs, "kv", 1)], first_part, second_part)
    attention_out = attention_out + theirs.astype(f32)

    def token_totals(*values):
        lanes = 128 // len(values)
        columns = [jnp.sum(value, axis=-1, keepdims=True) for value in values]
        columns = jnp.concatenate(
            [jnp.broadcast_to(column, (tok_block, lanes)) for column in columns], axis=-1
        )
        columns = add_up(collect(columns))
        return [columns[:, k * lanes : k * lanes + 1] for k in range(len(values))]

    own_float = own_state.astype(f32)

    def add_normed(state, update, gain):
        scaled = update * gain
        update_total, state_total, cross_total, scaled_total = token_totals(
            update * update, state * state, state * scaled, scaled * scaled
        )
        inverse = inverse_of(update_total)
        total = state_total + inverse * (2.0 * cross_total + inverse * scaled_total)
        return state + scaled * inverse, inverse_of(jnp.maximum(total, 0.0))

    first_sum, inverse = add_normed(own_float, attention_out, norm_post_attention)
    scaled_ffn = (first_sum * inverse * norm_pre_feedforward).astype(bf16)

    scaled_ffn = lax.all_gather(scaled_ffn, plane, axis=0, tiled=True)
    share = row_count // seq_count
    units = down_weight.shape[0]
    partial = jnp.einsum(
        "td,dcf->ctf", scaled_ffn, gate_up_weight, preferred_element_type=f32
    ).astype(bf16)

    first_part, second_part = hold([first_part, second_part], scaled_ffn)
    first_part, second_part = swap(first_part, "kv", 1), swap(second_part, "vocab", 2)
    slot_numbers = jnp.stack([length - block_start, seq_at])
    head_total = seq_count + 1
    lanes = 128
    starts = [
        (((kv_at ^ kv_bit) * seq_count + seq_at) * tenants + (vocab_at ^ vocab_bit)) * vocab_rows
        + first
        for kv_bit, vocab_bit, first in (
            (0, 0, 0),
            (0, 1, 0),
            (1, 0, 0),
            (1, 1, 0),
            (0, 0, half),
            (0, 1, half),
            (0, 2, half),
            (0, 3, half),
        )
    ]
    later = (jnp.abs(partial[0, 0, 0].astype(f32)) > 3e38).astype(jnp.int32)
    candidates = [
        lax.dynamic_slice(
            candidate_tokens,
            (0, block * tok_block + later, tenant, 0),
            (head_total, tok_block, 1, CAND),
        )[:, :, 0]
        for block, tenant in (
            (kv_at, vocab_at ^ 2),
            (kv_at, vocab_at),
            (kv_at ^ 1, vocab_at),
        )
    ]
    numbers = jnp.stack(starts + ahead).astype(jnp.int32) + later

    def rows_of(place):
        return lax.dynamic_slice_in_dim(partial, place * share, share, 1)

    summed = add_up([rows_of(seq_at)] + send_ahead(lambda j: rows_of(ahead[j])))
    keys_updated, key_flag = update_cache(
        cache_keys[0], slot_numbers, *head_blocks, rows + 1, accept_count, *candidates
    )
    activated = (jax.nn.gelu(summed[0], approximate=True) * summed[1]).astype(bf16)
    (activated,) = hold([activated], key_flag, first_part, second_part)
    ffn_out = in_order(
        [
            jnp.dot(block, down_weight, preferred_element_type=f32).astype(bf16)
            for block in collect(activated)
        ],
        ahead,
    ).reshape(groups, tok_block, width)
    ffn_out, numbers, *candidates = hold(
        [ffn_out, numbers, *candidates], first_part, second_part
    )
    ffn_out = add_up(list(lax.all_to_all(ffn_out, plane, 0, 0)))
    second_sum, inverse = add_normed(first_sum, ffn_out, norm_post_feedforward)
    normed = (second_sum * inverse * norm_final).astype(bf16)

    gathered = lax.all_gather(normed, plane, axis=0, tiled=True)
    lifted = jnp.einsum(
        "td,ndc->ntc", gathered, draft_weight, preferred_element_type=f32
    )
    lifted = lifted + draft_bias[:, None, :] * (1.0 / seq_count)
    lifted = lifted.astype(bf16).reshape(seq_count, kv_count, tenants, tok_block, -1)
    lifted = lifted.transpose(1, 0, 2, 3, 4).reshape(seq_count * groups, tok_block, -1)
    places = [("vocab", 2), (None, 0), ("kv", 1)]

    def around(values):
        return [values if axis is None else swap(values, axis, bit) for axis, bit in places]

    first_part, second_part = hold([first_part, second_part], lifted)
    core_first, core_second = swap(first_part, "vocab", 1), swap(second_part, "vocab", 1)
    core_rows = swap(vocab_weight, "vocab", 1)
    vocab_blocks = [
        [(vocab_weight, 0), (core_rows, 0)],
        [(first_part, 0), (core_first, 0)],
        [(vocab_weight, half), (core_rows, half)],
        [(second_part, 0), (core_second, 0)],
    ]
    values_updated, value_flag = update_cache(
        cache_values[0],
        slot_numbers,
        *head_blocks,
        rows + 1 + accept_count,
        accept_count,
        lifted,
    )
    everywhere = lax.all_to_all(lifted, ("kv", "seq", "vocab"), 0, 0, tiled=True)
    branch = activate_draft(everywhere, normed, kv_count, seq_count)
    (branch,) = hold([branch], core_first, core_second, core_rows, value_flag)
    heads = collect(branch)
    heads = [list(group) for group in zip(*[around(head) for head in heads])]
    tally = score_vocabulary(
        numbers, candidates, heads, vocab_blocks, half, lanes
    )
    tally = add_up(collect(tally))
    tally = lax.all_gather(tally, plane, axis=0)
    tally = tally.reshape(kv_count, tenants // 2, 2, 3, 16, lanes)
    tally = tally[:, :, :, 1] + (tally[:, ::-1, :, 0] + tally[::-1, :, :, 2])
    tally = tally[..., : CAND + 1, : head_total * tok_block]
    tally = tally.reshape(kv_count, tenants, CAND + 1, head_total, tok_block)
    log_normalizer = jnp.log(tally[:, :, 0].transpose(2, 0, 3, 1)).reshape(
        head_total, tree_size, tenants
    )
    candidate_logits = (
        tally[:, :, 1:]
        .transpose(3, 0, 4, 1, 2)
        .reshape(head_total, tree_size, tenants, CAND)
    )
    return (keys_updated[None], values_updated[None], log_normalizer, candidate_logits)


def solution(mesh):
    placed = (
        P("kv", "vocab", "seq"),
        P("seq", "kv", None),
        P("kv", None, "seq"),
        P("seq"),
        P("seq"),
        P("seq"),
        P("seq"),
        P("seq"),
        P("vocab", "seq", "kv", None),
        P("vocab", "seq", "kv", None),
        P("vocab"),
        P("vocab", None, None),
        P("vocab", None),
        P("seq", None, ("kv", "vocab")),
        P(("kv", "vocab"), "seq"),
        P(None, "seq", ("kv", "vocab")),
        P(None, ("kv", "vocab")),
        P(("kv", "seq", "vocab"), None),
        P(),
    )
    body = local if fits(mesh.shape) else local_general
    return jax.shard_map(
        body,
        mesh=mesh,
        in_specs=placed,
        out_specs=(P("vocab", "seq", "kv", None), P("vocab", "seq", "kv", None), P(), P()),
        check_vma=False,
    )
```

```python
import jax
import jax.numpy as jnp
from jax import lax
from jax.experimental import pallas as pl
from jax.experimental.pallas import tpu as pltpu
from jax.sharding import PartitionSpec as P

MODEL_WIDTH = 3584
HEAD_SIZE = 256
CAND = 8


EPSILON = 1e-06
SCORE_CAP = 50.0
LOGIT_CAP = 30.0


def apply_rotary(vectors, token_positions):
    half_dim = vectors.shape[-1] // 2
    frequency = 10000.0 ** (-2.0 * jnp.arange(half_dim, dtype=jnp.float32) / vectors.shape[-1])
    angles = token_positions.astype(jnp.float32)[..., None] * frequency
    cosine = jnp.cos(angles)
    sine_part = jnp.sin(angles)
    first_half = vectors[..., :half_dim]
    second_half = vectors[..., half_dim:]
    return jnp.concatenate(
        [
            first_half * cosine - second_half * sine_part,
            second_half * cosine + first_half * sine_part,
        ],
        axis=-1,
    )


def capped_weight(scores):
    return jnp.exp(SCORE_CAP * jnp.tanh(scores * 0.0625 / SCORE_CAP))


def row_inverse(values):
    totals = lax.psum(jnp.sum(values * values, axis=-1), "seq")
    return lax.rsqrt(totals / MODEL_WIDTH + EPSILON)[:, None]


def gated_units(gate_up, squares):
    inverse = lax.rsqrt(squares / MODEL_WIDTH + EPSILON)[:, None]
    return (
        jax.nn.gelu(gate_up[:, 0] * inverse, approximate=True) * (gate_up[:, 1] * inverse)
    ).astype(jnp.bfloat16)


def local_general(
    hidden_state,
    input_projection,
    output_projection,
    norm_pre_attention,
    norm_post_attention,
    norm_pre_feedforward,
    norm_post_feedforward,
    norm_final,
    cache_keys,
    cache_values,
    cache_length,
    ancestors,
    accepted_path,
    gate_up_weight,
    down_weight,
    draft_weight,
    draft_bias,
    vocab_weight,
    candidate_tokens,
):
    tok_block = hidden_state.shape[0]
    kv_count = lax.axis_size("kv")
    tenants = lax.axis_size("vocab")
    tree_size = tok_block * kv_count
    own_state = hidden_state[:, 0, :]
    tenant_state = lax.all_gather(own_state, "kv", axis=0, tiled=True)
    tenant_float = tenant_state.astype(jnp.float32)
    scaled_input = (tenant_float * norm_pre_attention).astype(jnp.bfloat16)
    projected_rows = jnp.einsum(
        "td,dhc->thc", scaled_input, input_projection, preferred_element_type=jnp.float32
    )
    projected_rows, squares = lax.psum(
        (projected_rows, jnp.sum(tenant_float * tenant_float, axis=-1)), "seq"
    )
    projected_rows = projected_rows * lax.rsqrt(squares / MODEL_WIDTH + EPSILON)[:, None, None]
    head_count = projected_rows.shape[1]
    depths = jnp.sum(ancestors[0], axis=-1) - 1
    length = cache_length[0]
    token_positions = length + depths
    query_rows = apply_rotary(
        projected_rows[:, :, : 2 * HEAD_SIZE].reshape(tree_size, head_count, 2, HEAD_SIZE),
        token_positions[:, None, None],
    ).astype(jnp.bfloat16)
    new_keys = apply_rotary(
        projected_rows[:, :, 2 * HEAD_SIZE : 3 * HEAD_SIZE], token_positions[:, None]
    ).astype(jnp.bfloat16)
    new_values = projected_rows[:, :, 3 * HEAD_SIZE :].astype(jnp.bfloat16)
    block_size = cache_keys.shape[1]
    block_start = lax.axis_index("seq") * block_size
    cache_cells = block_start + jnp.arange(block_size, dtype=jnp.int32)
    scores = jnp.einsum(
        "thgc,shc->thgs", query_rows, cache_keys[0], preferred_element_type=jnp.float32
    )
    weights = jnp.where((cache_cells < length)[None, None, None, :], capped_weight(scores), 0.0)
    numerator = jnp.einsum(
        "thgs,shc->thgc",
        weights.astype(jnp.bfloat16),
        cache_values[0],
        preferred_element_type=jnp.float32,
    )
    numerator, denominator = lax.psum((numerator, jnp.sum(weights, axis=-1)), "seq")
    tree_scores = jnp.einsum(
        "thgc,uhc->thgu", query_rows, new_keys, preferred_element_type=jnp.float32
    )
    tree_weights = jnp.where(ancestors[0][:, None, None, :] > 0, capped_weight(tree_scores), 0.0)
    numerator = numerator + jnp.einsum(
        "thgu,uhc->thgc",
        tree_weights.astype(jnp.bfloat16),
        new_values,
        preferred_element_type=jnp.float32,
    )
    denominator = denominator + jnp.sum(tree_weights, axis=-1)
    attended = (
        (numerator / denominator[..., None])
        .astype(jnp.bfloat16)
        .reshape(tree_size, head_count * 2 * HEAD_SIZE)
    )
    out_matrix = output_projection.reshape(head_count * 2 * HEAD_SIZE, output_projection.shape[2])
    attention_out = lax.psum_scatter(
        jnp.dot(attended, out_matrix, preferred_element_type=jnp.float32),
        "kv",
        scatter_dimension=0,
        tiled=True,
    )
    first_sum = (
        own_state.astype(jnp.float32)
        + attention_out * row_inverse(attention_out) * norm_post_attention
    ).astype(jnp.bfloat16)
    all_state = lax.all_gather(first_sum, ("kv", "vocab"), axis=0, tiled=True)
    all_float = all_state.astype(jnp.float32)
    scaled_ffn = (all_float * norm_pre_feedforward).astype(jnp.bfloat16)
    gate_up = jnp.einsum(
        "td,dcf->tcf", scaled_ffn, gate_up_weight, preferred_element_type=jnp.float32
    )
    ffn_squares = jnp.sum(all_float * all_float, axis=-1)
    gate_up, ffn_squares = lax.psum((gate_up, ffn_squares), "seq")
    activated = gated_units(gate_up, ffn_squares)
    ffn_out = lax.psum_scatter(
        jnp.dot(activated, down_weight, preferred_element_type=jnp.float32),
        ("kv", "vocab"),
        scatter_dimension=0,
        tiled=True,
    )
    first_float = first_sum.astype(jnp.float32)
    second_sum = (first_float + ffn_out * row_inverse(ffn_out) * norm_post_feedforward).astype(
        jnp.bfloat16
    )
    second_float = second_sum.astype(jnp.float32)
    normed = (second_float * row_inverse(second_float) * norm_final).astype(jnp.bfloat16)
    gathered = lax.all_gather(normed, ("kv", "vocab"), axis=0, tiled=True)
    lifted = jnp.einsum("td,ndc->tnc", gathered, draft_weight, preferred_element_type=jnp.float32)
    lifted = lax.psum(lifted.astype(jnp.bfloat16), "seq").astype(jnp.float32)
    branch = jax.nn.silu(lifted + draft_bias).astype(jnp.bfloat16)
    row_count = gathered.shape[0]
    vocab_rows = vocab_weight.shape[0]
    draft_count = branch.shape[1]
    columns = vocab_weight
    base_logits = lax.dot_general(
        lax.all_gather(gathered, "seq", axis=1, tiled=True),
        columns,
        (((1,), (1,)), ((), ())),
        preferred_element_type=jnp.float32,
    )
    columns = vocab_weight
    draft_extra = jnp.einsum(
        "tnc,vc->tnv",
        lax.all_gather(branch, ("kv", "vocab"), axis=2, tiled=True),
        columns,
        preferred_element_type=jnp.float32,
    )
    raw_logits = jnp.concatenate(
        [base_logits[:, None, :], base_logits[:, None, :] + draft_extra], axis=1
    )
    logits = LOGIT_CAP * jnp.tanh(raw_logits / LOGIT_CAP)
    totals = jnp.sum(jnp.exp(logits), axis=-1)
    head_total = draft_count + 1
    candidates = candidate_tokens.reshape(head_total, kv_count, tok_block, tenants, CAND)
    candidates = jnp.transpose(candidates, (0, 1, 3, 2, 4)).reshape(head_total, row_count, CAND)
    candidates = jnp.transpose(candidates, (1, 0, 2))
    vocab_start = lax.axis_index(("kv", "seq", "vocab")) * vocab_rows
    local_tokens = candidates - vocab_start
    entry_index = jnp.arange(vocab_rows, dtype=jnp.int32)
    picked = jnp.stack(
        [
            jnp.sum(
                jnp.where(entry_index == local_tokens[:, :, column : column + 1], logits, 0.0),
                axis=-1,
            )
            for column in range(CAND)
        ],
        axis=-1,
    )
    totals, picked = lax.psum((totals, picked), ("kv", "seq", "vocab"))
    log_totals = jnp.transpose(jnp.log(totals)).reshape(head_total, kv_count, tenants, tok_block)
    log_normalizer = jnp.transpose(log_totals, (0, 1, 3, 2)).reshape(head_total, tree_size, tenants)
    picked = jnp.transpose(picked, (1, 0, 2)).reshape(
        head_total, kv_count, tenants, tok_block, CAND
    )
    candidate_logits = jnp.transpose(picked, (0, 1, 3, 2, 4)).reshape(
        head_total, tree_size, tenants, CAND
    )
    accept_count = accepted_path.shape[1]
    slot_rows = length + jnp.arange(accept_count, dtype=jnp.int32)
    tree_nodes = jnp.arange(tree_size, dtype=jnp.int32)
    matches = (cache_cells[:, None, None] == slot_rows[None, :, None]) & (
        accepted_path[0][None, :, None] == tree_nodes[None, None, :]
    )
    selector = jnp.sum(matches.astype(jnp.float32), axis=1)
    written = jnp.sum(selector, axis=-1) > 0.0
    selector = selector.astype(jnp.bfloat16)

    def write_path(old_block, fresh_rows):
        moved_rows = jnp.dot(
            selector, fresh_rows.reshape(tree_size, -1), preferred_element_type=jnp.float32
        ).astype(jnp.bfloat16)
        return jnp.where(
            written[:, None], moved_rows, old_block[0].reshape(block_size, -1)
        ).reshape(old_block.shape)

    keys_updated = write_path(cache_keys, new_keys)
    values_updated = write_path(cache_values, new_values)
    return (keys_updated, values_updated, log_normalizer, candidate_logits)


def fits(sizes):
    return sizes["kv"] == 2 and sizes["vocab"] == 4 and sizes["seq"] == 4


def send_ahead(pick):
    count = lax.axis_size("seq")
    return [
        lax.ppermute(pick(j), "seq", [(i, (i + j) % count) for i in range(count)])
        for j in range(1, count)
    ]


def collect(block):
    count = lax.axis_size("seq")
    return [block] + [
        lax.ppermute(block, "seq", [(i, (i - j) % count) for i in range(count)])
        for j in range(1, count)
    ]


def in_order(blocks, ahead):
    result = jnp.zeros((len(blocks),) + blocks[0].shape, blocks[0].dtype)
    for j, block in enumerate(blocks):
        result = lax.dynamic_update_index_in_dim(result, block, ahead[j], 0)
    return result


def add_up(blocks):
    total = blocks[0].astype(jnp.float32)
    for block in blocks[1:]:
        total = total + block.astype(jnp.float32)
    return total


def swap(values, axis, bit):
    count = lax.axis_size(axis)
    return lax.ppermute(values, axis, [(i, i ^ bit) for i in range(count)])


def split_lanes(values):
    high = values.astype(jnp.bfloat16)
    low = (values - high.astype(jnp.float32)).astype(jnp.bfloat16)
    shape = values.shape[:-1] + (64,)
    return jnp.concatenate([jnp.broadcast_to(high, shape), jnp.broadcast_to(low, shape)], axis=-1)


def hold(values, *events):
    count = len(values)
    anywhere = pl.BlockSpec(memory_space=pl.ANY)
    return pl.pallas_call(
        lambda *refs: None,
        out_shape=[jax.ShapeDtypeStruct(value.shape, value.dtype) for value in values],
        in_specs=[anywhere] * (count + len(events)),
        out_specs=[anywhere] * count,
        input_output_aliases={k: k for k in range(count)},
    )(*values, *events)


def inverse_of(totals):
    return lax.rsqrt(totals / MODEL_WIDTH + EPSILON)


def rotate(vectors, cosine, sine):
    half = vectors.shape[-1] // 2
    first, second = vectors[..., :half], vectors[..., half:]
    return jnp.concatenate(
        [first * cosine - second * sine, second * cosine + first * sine], axis=-1
    )


def copy_rows(sources, targets, *events):
    unit = 64
    number = len(sources)
    shapes = [
        (sum(rows for _, _, rows in parts),) + sources[0].shape[1:] for parts in targets
    ]
    moves = []
    for t, parts in enumerate(targets):
        filled = 0
        for source, first, rows in parts:
            for p in range(0, rows, unit):
                size = min(unit, rows - p)
                moves.append((source, first + p, t, filled + p, size))
            filled += rows

    def kernel(*refs):
        inputs, rest = refs[:number], refs[number + len(events) :]
        outputs, (held, get, put) = rest[: len(shapes)], rest[len(shapes) :]
        pairs = []
        for k, (source, first, target, place, size) in enumerate(moves):
            slot = held.at[k, pl.ds(0, size)]
            pairs.append(
                (
                    pltpu.make_async_copy(
                        inputs[source].at[pl.ds(first, size)], slot, get.at[k]
                    ),
                    pltpu.make_async_copy(
                        slot, outputs[target].at[pl.ds(place, size)], put.at[k]
                    ),
                )
            )
        for k, (inward, _) in enumerate(pairs):
            inward.start(priority=k % 2)
        for k, (inward, outward) in enumerate(pairs):
            inward.wait()
            outward.start(priority=k % 2)
        for _, outward in pairs:
            outward.wait()

    row = sources[0].shape[1:]
    dtype = sources[0].dtype
    return pl.pallas_call(
        kernel,
        out_shape=[jax.ShapeDtypeStruct(shape, dtype) for shape in shapes],
        in_specs=[pl.BlockSpec(memory_space=pl.ANY)] * (number + len(events)),
        out_specs=[pl.BlockSpec(memory_space=pltpu.HBM)] * len(shapes),
        scratch_shapes=[
            pltpu.VMEM((len(moves), unit) + row, dtype),
            pltpu.SemaphoreType.DMA((len(moves),)),
            pltpu.SemaphoreType.DMA((len(moves),)),
        ],
        compiler_params=pltpu.CompilerParams(vmem_limit_bytes=58 * 2**20),
        cost_estimate=pl.CostEstimate(
            flops=0,
            bytes_accessed=sum(4 * shape[0] * shape[1] for shape in shapes),
            transcendentals=0,
        ),
    )(*sources, *events)


def update_cache(cache, numbers, packed, arrived, first_row, accept, *events):
    slots, heads, size = cache.shape
    count = 1 + len(arrived)
    tail = pl.ds(packed.shape[1] - 16, 16)
    first_row = first_row - (packed.shape[1] - 16)
    piece = 256
    parts = slots // piece

    def kernel(numbers_ref, source, packed_ref, *rest):
        arrived_refs, rest = rest[: count - 1], rest[count - 1 + len(events) :]
        target, flag, held, tails, stage, ready, get, put, sem = rest
        flag[...] = jnp.zeros_like(flag)

        tail_copies = []
        for j in range(count):
            head = lax.rem(numbers_ref[1] + (count - j), count)
            block = packed_ref.at[0, tail] if j == 0 else arrived_refs[j - 1].at[tail]
            tail_copies.append(pltpu.make_async_copy(block, tails.at[head], sem.at[j]))
            tail_copies[j].start()
        pairs = []
        for k in range(parts):
            window = pl.ds(k * piece, piece)
            pairs.append(
                (
                    pltpu.make_async_copy(source.at[window], held.at[k], get.at[k]),
                    pltpu.make_async_copy(held.at[k], target.at[window], put.at[k]),
                )
            )
        for k, (inward, _) in enumerate(pairs):
            inward.start(priority=k % 2)
        for k, (inward, outward) in enumerate(pairs):
            inward.wait()
            outward.start(priority=k % 2)
        for copy in tail_copies:
            copy.wait()
        for head in range(count):
            rows = tails[head].astype(jnp.float32)
            for r in range(accept):
                stage[r, head : head + 1, :] = rows[first_row + r : first_row + r + 1]
        ready[...] = stage[...].astype(ready.dtype)
        for _, outward in pairs:
            outward.wait()
        for a in range(accept):
            slot = numbers_ref[0] + a

            @pl.when((slot >= 0) & (slot < slots))
            def _():
                copy = pltpu.make_async_copy(
                    ready.at[pl.ds(a, 1)], target.at[pl.ds(slot, 1)], sem.at[0]
                )
                copy.start()
                copy.wait()

    return pl.pallas_call(
        kernel,
        out_shape=(
            jax.ShapeDtypeStruct(cache.shape, cache.dtype),
            jax.ShapeDtypeStruct((8, 128), jnp.float32),
        ),
        in_specs=[
            pl.BlockSpec(memory_space=pltpu.SMEM),
            pl.BlockSpec(memory_space=pltpu.HBM),
        ]
        + [pl.BlockSpec(memory_space=pl.ANY)] * (count + len(events)),
        out_specs=(
            pl.BlockSpec(memory_space=pltpu.HBM),
            pl.BlockSpec(memory_space=pltpu.VMEM),
        ),
        scratch_shapes=[
            pltpu.VMEM((parts, piece, heads, size), cache.dtype),
            pltpu.VMEM((count, 16, size), cache.dtype),
            pltpu.VMEM((accept, heads, size), jnp.float32),
            pltpu.VMEM((accept, heads, size), cache.dtype),
            pltpu.SemaphoreType.DMA((parts,)),
            pltpu.SemaphoreType.DMA((parts,)),
            pltpu.SemaphoreType.DMA((count,)),
        ],
        compiler_params=pltpu.CompilerParams(vmem_limit_bytes=56 * 2**20),
        cost_estimate=pl.CostEstimate(
            flops=0, bytes_accessed=4 * cache.size, transcendentals=0
        ),
    )(numbers, cache, packed, *arrived, *events)


def score_vocabulary(numbers, candidates, heads, vocab_blocks, half, lanes):
    tokens = heads[0][0].shape[0]
    count = len(heads[0])
    groups = len(heads)
    parts = [part for block in vocab_blocks for part in block]
    arrays = []
    for array, _ in parts:
        if not any(array is known for known in arrays):
            arrays.append(array)
    blocks, extent, width = len(vocab_blocks), 2 * half, arrays[0].shape[1]
    share = width // count
    unit = 64
    inputs = [head for group in heads for head in group]

    def kernel(numbers_ref, *rest):
        candidate_refs, rest = rest[:groups], rest[groups:]
        vectors, rest = rest[: len(inputs)], rest[len(inputs) :]
        sources, rest = rest[: len(arrays)], rest[len(arrays) :]
        out_ref, held, arrived, wide, narrow, square, row_sems, sems = rest
        arrivals = []
        for k, vector in enumerate(vectors):
            arrivals.append(pltpu.make_async_copy(vector, arrived.at[k], sems.at[k]))
            arrivals[k].start(priority=0)
        def fetch(b):
            for k in (2 * b, 2 * b + 1):
                array, first = parts[k]
                source = sources[[array is known for known in arrays].index(True)]
                for q, p in enumerate(range(0, half, unit)):
                    pltpu.make_async_copy(
                        source.at[pl.ds(first + p, unit)],
                        held.at[b, pl.ds(k % 2 * half + p, unit)],
                        row_sems.at[b],
                    ).start(priority=1)

        fetch(0)
        fetch(1)
        fetch(2)
        fetch(3)
        spare = lanes - (count + 1) * tokens
        wanted = []
        for group, ref in enumerate(candidate_refs):
            square[...] = jnp.full((lanes, 128), -1, jnp.int32)
            square[0:tokens, 0:CAND] = ref[0]
            for j in range(count):
                row_at = (j + 1) * tokens
                square[row_at : row_at + tokens, 0:CAND] = ref[numbers_ref[2 * blocks + j] + 1]
            wanted.append(square[...].T[0:CAND])
        def assemble(group):
            for j in range(count):
                arrivals[group * count + j].wait()
                columns = pl.ds(pl.multiple_of(numbers_ref[2 * blocks + j] * share, 128), share)
                wide[group * tokens : (group + 1) * tokens, columns] = arrived[
                    group * count + j, :, width:
                ].astype(jnp.float32)
            pieces = [wide[group * tokens : (group + 1) * tokens, :]]
            pieces += [arrived[group * count + j, :, :width].astype(jnp.float32) for j in range(count)]
            pieces += [jnp.zeros((spare, width), jnp.float32)]
            narrow[group * lanes : (group + 1) * lanes, :] = jnp.concatenate(
                pieces, axis=0
            ).astype(narrow.dtype)
        assemble(0)
        assemble(1)
        lane = lax.broadcasted_iota(jnp.int32, (half, lanes), 1)
        row = lax.broadcasted_iota(jnp.int32, (half, lanes), 0)
        out_ref[...] = jnp.zeros_like(out_ref)

        def step(b, low):
            pltpu.make_async_copy(held.at[b], held.at[b], row_sems.at[b]).wait()
            both = lax.dot_general(
                held[b],
                narrow[low * lanes : (low + 2) * lanes, :],
                (((1,), (1,)), ((), ())),
                preferred_element_type=jnp.float32,
            )
            for group in (low, low + 1):
                place = slice((group - low) * lanes, (group - low + 1) * lanes)
                for part in range(2):
                    raw = both[part * half : (part + 1) * half, place]
                    entry = row + numbers_ref[2 * b + part]
                    first = jnp.where(lane < tokens, raw, 0.0)
                    for head in range(1, count + 1):
                        raw = raw + pltpu.roll(first, head * tokens, 1)
                    logits = LOGIT_CAP * jnp.tanh(raw / LOGIT_CAP)
                    tally = [jnp.sum(jnp.exp(logits), axis=0, keepdims=True)]
                    for c in range(CAND):
                        match = entry == wanted[group][c : c + 1]
                        tally.append(
                            jnp.sum(jnp.where(match, logits, 0.0), axis=0, keepdims=True)
                        )
                    out_ref[16 * group : 16 * group + CAND + 1, :] += jnp.concatenate(tally, axis=0)

        for low in range(2):
            if low == 1:
                assemble(2)

            def run(b, carry, low=low):
                step(b, low)
                return carry

            middle = blocks // 2
            lax.fori_loop(low * middle, (low + 1) * middle, run, 0)
        turn = numbers_ref[2 * blocks] * tokens
        across = lax.broadcasted_iota(jnp.int32, out_ref.shape, 1)
        values = out_ref[...]
        ahead = pltpu.roll(values, turn, 1)
        wrapped = pltpu.roll(values, turn + lanes - count * tokens, 1)
        turned = jnp.where(across - turn >= tokens, ahead, wrapped)
        out_ref[...] = jnp.where(across < tokens, values, turned)

    return pl.pallas_call(
        kernel,
        out_shape=jax.ShapeDtypeStruct((16 * groups, lanes), jnp.float32),
        in_specs=[pl.BlockSpec(memory_space=pltpu.SMEM)]
        + [pl.BlockSpec(memory_space=pltpu.VMEM)] * groups
        + [pl.BlockSpec(memory_space=pl.ANY)] * (len(inputs) + len(arrays)),
        out_specs=pl.BlockSpec(memory_space=pltpu.VMEM),
        scratch_shapes=[
            pltpu.VMEM((blocks, extent, width), inputs[0].dtype),
            pltpu.VMEM((len(inputs),) + inputs[0].shape, inputs[0].dtype),
            pltpu.VMEM((groups * tokens, width), jnp.float32),
            pltpu.VMEM((groups * lanes, width), inputs[0].dtype),
            pltpu.VMEM((lanes, 128), jnp.int32),
            pltpu.SemaphoreType.DMA((blocks,)),
            pltpu.SemaphoreType.DMA((len(inputs),)),
        ],
        compiler_params=pltpu.CompilerParams(vmem_limit_bytes=58 * 2**20),
        cost_estimate=pl.CostEstimate(
            flops=4 * blocks * extent * width * lanes,
            bytes_accessed=2 * blocks * extent * width,
            transcendentals=4 * blocks * extent * lanes,
        ),
    )(numbers, *candidates, *inputs, *arrays)


def activate_draft(parts, normed, kv_count, seq_count):
    number, tokens, columns = parts.shape
    tenants = number // (kv_count * seq_count)
    width = kv_count * tenants * columns

    def kernel(parts_ref, normed_ref, out_ref):
        pair = []
        for kv in range(kv_count):
            for tenant in range(tenants):
                total = 0.0
                for seq in range(seq_count):
                    block = parts_ref[(kv * seq_count + seq) * tenants + tenant]
                    total = total + block.astype(jnp.float32)
                pair.append(total / (1.0 + jnp.exp(-total)))
                if len(pair) == 2:
                    place = (kv * tenants + tenant - 1) * columns
                    out_ref[:, place : place + 2 * columns] = jnp.concatenate(
                        pair, axis=1
                    ).astype(out_ref.dtype)
                    pair = []
        out_ref[:, width:] = normed_ref[...]

    vmem = pl.BlockSpec(memory_space=pltpu.VMEM)
    return pl.pallas_call(
        kernel,
        out_shape=jax.ShapeDtypeStruct((tokens, width + normed.shape[1]), normed.dtype),
        in_specs=[vmem] * 2,
        out_specs=vmem,
    )(parts, normed)


def project_in(rows, weight):
    tokens, depth = rows.shape
    _, heads, columns = weight.shape
    unit = 128

    def kernel(rows_ref, weight_ref, out_ref, spread, total):
        source = lax.broadcasted_iota(jnp.int32, (unit, unit * heads), 0)
        place = lax.broadcasted_iota(jnp.int32, (unit, unit * heads), 1)
        for h in range(heads):
            spread[h] = jnp.where(place == source * heads + h, 1.0, 0.0).astype(rows.dtype)
        total[...] = jnp.zeros_like(total)
        for k in range(depth // unit):
            block = rows_ref[:, k * unit : (k + 1) * unit]
            wide = jnp.concatenate(
                [
                    jnp.dot(block, spread[h], preferred_element_type=jnp.float32)
                    for h in range(heads)
                ],
                axis=0,
            ).astype(rows.dtype)
            total[...] += jnp.dot(
                wide,
                weight_ref[k * unit : (k + 1) * unit].reshape(unit * heads, columns),
                preferred_element_type=jnp.float32,
            )
        for h in range(heads):
            out_ref[h] = total[h * tokens : (h + 1) * tokens, :].astype(out_ref.dtype)

    vmem = pl.BlockSpec(memory_space=pltpu.VMEM)
    return pl.pallas_call(
        kernel,
        out_shape=jax.ShapeDtypeStruct((heads, tokens, columns), rows.dtype),
        in_specs=[vmem] * 2,
        out_specs=vmem,
        scratch_shapes=[
            pltpu.VMEM((heads, unit, unit * heads), rows.dtype),
            pltpu.VMEM((heads * tokens, columns), jnp.float32),
        ],
        compiler_params=pltpu.CompilerParams(vmem_limit_bytes=24 * 2**20),
        cost_estimate=pl.CostEstimate(
            flops=2 * heads * tokens * weight.size,
            bytes_accessed=2 * weight.size,
            transcendentals=0,
        ),
    )(rows, weight)


def project_out(places, attended, weight, own_rows):
    rows = attended[0].shape[0] // 2
    size = attended[0].shape[1]
    count, _, width = weight.shape

    def kernel(places_ref, *refs):
        blocks, (weight_ref, theirs_ref, own_ref) = refs[:count], refs[count:]
        total = jnp.zeros((rows, width), jnp.float32)
        for j, block in enumerate(blocks):
            for g in range(2):
                total = total + jnp.dot(
                    block[g * rows : (g + 1) * rows, :],
                    weight_ref[places_ref[j], g * size : (g + 1) * size, :],
                    preferred_element_type=jnp.float32,
                )
        own_ref[...] = total[:own_rows]
        theirs_ref[...] = total[own_rows:].astype(theirs_ref.dtype)

    vmem = pl.BlockSpec(memory_space=pltpu.VMEM)
    return pl.pallas_call(
        kernel,
        out_shape=[
            jax.ShapeDtypeStruct((rows - own_rows, width), attended[0].dtype),
            jax.ShapeDtypeStruct((own_rows, width), jnp.float32),
        ],
        in_specs=[pl.BlockSpec(memory_space=pltpu.SMEM)] + [vmem] * (count + 1),
        out_specs=[vmem] * 2,
        compiler_params=pltpu.CompilerParams(vmem_limit_bytes=16 * 2**20),
        cost_estimate=pl.CostEstimate(
            flops=2 * rows * weight.size, bytes_accessed=2 * weight.size, transcendentals=0
        ),
    )(places, *attended, weight)


def local(
    hidden_state,
    input_projection,
    output_projection,
    norm_pre_attention,
    norm_post_attention,
    norm_pre_feedforward,
    norm_post_feedforward,
    norm_final,
    cache_keys,
    cache_values,
    cache_length,
    ancestors,
    accepted_path,
    gate_up_weight,
    down_weight,
    draft_weight,
    draft_bias,
    vocab_weight,
    candidate_tokens,
):
    f32, bf16 = jnp.float32, jnp.bfloat16
    plane = ("kv", "vocab")
    tok_block, _, width = hidden_state.shape
    seq_count = lax.axis_size("seq")
    kv_count = lax.axis_size("kv")
    tenants = lax.axis_size("vocab")
    groups = kv_count * tenants
    tree_size = tok_block * kv_count
    row_count = tok_block * groups
    seq_at = lax.axis_index("seq")
    kv_at = lax.axis_index("kv")
    vocab_at = lax.axis_index("vocab")
    ahead = [(seq_at + j) % seq_count for j in range(seq_count)]
    own_state = hidden_state[:, 0, :]

    tenant_state = jnp.concatenate([own_state, swap(own_state, "kv", 1)], axis=0)
    vocab_rows = vocab_weight.shape[0]
    half = vocab_rows // 2

    tenant_float = tenant_state.astype(f32)
    scaled_input = (tenant_float * norm_pre_attention).astype(bf16)
    projected = project_in(scaled_input, input_projection)
    square_lanes = split_lanes(jnp.sum(tenant_float * tenant_float, axis=-1, keepdims=True))
    head_count = projected.shape[0]
    pair = 2 * HEAD_SIZE
    packed = jnp.concatenate(
        [
            projected,
            jnp.broadcast_to(square_lanes, (head_count,) + square_lanes.shape),
        ],
        axis=-1,
    )
    arrived = send_ahead(lambda j: lax.dynamic_index_in_dim(packed, ahead[j], 0, False))
    summed = add_up([lax.dynamic_index_in_dim(packed, seq_at, 0, False)] + arrived)
    whole = 2 * pair
    inverse = inverse_of(summed[:, whole : whole + 1] + summed[:, whole + 64 : whole + 65])
    tree_mask = ancestors[0]
    tree_mask = jnp.where(
        kv_at == 0, tree_mask, jnp.roll(tree_mask, (tok_block, tok_block), (0, 1))
    )
    length = cache_length[0]
    depths = jnp.sum(tree_mask, axis=-1, keepdims=True) - 1
    frequency = 10000.0 ** (
        -2.0 * jnp.arange(HEAD_SIZE // 2, dtype=f32) / HEAD_SIZE
    )
    angles = (length + depths).astype(f32) * frequency
    cosine, sine = jnp.cos(angles), jnp.sin(angles)
    query_rows = jnp.concatenate(
        [
            rotate(summed[:, :HEAD_SIZE] * inverse, cosine, sine),
            rotate(summed[:, HEAD_SIZE:pair] * inverse, cosine, sine),
        ],
        axis=0,
    ).astype(bf16)
    all_queries = in_order(collect(query_rows), ahead)
    new_keys = rotate(summed[:, pair : pair + HEAD_SIZE] * inverse, cosine, sine).astype(bf16)
    new_values = (summed[:, pair + HEAD_SIZE : whole] * inverse).astype(bf16)

    block_size = cache_keys.shape[1]
    block_start = seq_at * block_size
    cache_cells = block_start + jnp.arange(block_size, dtype=jnp.int32)
    scores = jnp.einsum("hrc,shc->hrs", all_queries, cache_keys[0], preferred_element_type=f32)
    weights = jnp.where((cache_cells < length)[None, None, :], capped_weight(scores), 0.0)
    numerator = jnp.einsum(
        "hrs,shc->hrc", weights.astype(bf16), cache_values[0], preferred_element_type=f32
    )
    rows = 2 * tree_size
    sums = jnp.sum(weights, axis=-1)
    sums_high = sums.astype(bf16)
    sums_low = (sums - sums_high.astype(f32)).astype(bf16)
    sums = jnp.concatenate(
        [sums_high, sums_low, jnp.zeros((head_count, HEAD_SIZE - 2 * rows), bf16)], axis=-1
    )
    node_at = jnp.arange(tree_size, dtype=jnp.int32)
    node_at = jnp.where(kv_at == 0, node_at, (node_at + tok_block) % tree_size)
    accept_pick = (accepted_path[0][:, None] == node_at[None, :]).astype(bf16)
    accept_count = accept_pick.shape[0]
    chosen = jnp.concatenate(
        [
            jnp.dot(accept_pick, fresh_part, preferred_element_type=f32).astype(bf16)
            for fresh_part in (new_keys, new_values)
        ],
        axis=0,
    )
    packed = jnp.concatenate(
        [
            numerator.astype(bf16),
            sums[:, None, :],
            jnp.broadcast_to(chosen, (head_count,) + chosen.shape),
            jnp.zeros((head_count, 15 - 2 * accept_count, HEAD_SIZE), bf16),
        ],
        axis=1,
    )
    arrived = send_ahead(lambda j: lax.dynamic_index_in_dim(packed, ahead[j], 0, False))
    tree_scores = lax.dot_general(
        query_rows, new_keys, (((1,), (1,)), ((), ())), preferred_element_type=f32
    )
    seen = jnp.concatenate([tree_mask, tree_mask], axis=0) > 0
    tree_weights = jnp.where(seen, capped_weight(tree_scores), 0.0)
    tree_numerator = jnp.dot(tree_weights.astype(bf16), new_values, preferred_element_type=f32)
    tree_sums = jnp.sum(tree_weights, axis=-1, keepdims=True)
    head_blocks = (packed, arrived)
    summed = add_up([lax.dynamic_index_in_dim(packed, seq_at, 0, False)] + arrived)
    denominator = (summed[rows, :rows] + summed[rows, rows : 2 * rows])[:, None] + tree_sums
    attended = ((summed[:rows] + tree_numerator) / denominator).astype(bf16)
    theirs, attention_out = project_out(
        jnp.stack(ahead).astype(jnp.int32),
        collect(attended),
        output_projection,
        tok_block,
    )
    first_part, second_part = copy_rows(
        [vocab_weight],
        [[(0, 0, half)], [(0, half, vocab_rows - half)]],
        theirs,
    )
    (theirs,) = hold([swap(theirs, "kv", 1)], first_part, second_part)
    attention_out = attention_out + theirs.astype(f32)

    def token_totals(*values):
        lanes = 128 // len(values)
        columns = [jnp.sum(value, axis=-1, keepdims=True) for value in values]
        columns = jnp.concatenate(
            [jnp.broadcast_to(column, (tok_block, lanes)) for column in columns], axis=-1
        )
        columns = add_up(collect(columns))
        return [columns[:, k * lanes : k * lanes + 1] for k in range(len(values))]

    own_float = own_state.astype(f32)

    def add_normed(state, update, gain):
        scaled = update * gain
        update_total, state_total, cross_total, scaled_total = token_totals(
            update * update, state * state, state * scaled, scaled * scaled
        )
        inverse = inverse_of(update_total)
        total = state_total + inverse * (2.0 * cross_total + inverse * scaled_total)
        return state + scaled * inverse, inverse_of(jnp.maximum(total, 0.0))

    first_sum, inverse = add_normed(own_float, attention_out, norm_post_attention)
    scaled_ffn = (first_sum * inverse * norm_pre_feedforward).astype(bf16)

    scaled_ffn = lax.all_gather(scaled_ffn, plane, axis=0, tiled=True)
    share = row_count // seq_count
    units = down_weight.shape[0]
    partial = jnp.einsum(
        "td,dcf->ctf", scaled_ffn, gate_up_weight, preferred_element_type=f32
    ).astype(bf16)

    first_part, second_part = hold([first_part, second_part], scaled_ffn)
    first_part, second_part = swap(first_part, "kv", 1), swap(second_part, "vocab", 2)
    slot_numbers = jnp.stack([length - block_start, seq_at])
    head_total = seq_count + 1
    lanes = 128
    starts = [
        (((kv_at ^ kv_bit) * seq_count + seq_at) * tenants + (vocab_at ^ vocab_bit)) * vocab_rows
        + first
        for kv_bit, vocab_bit, first in (
            (0, 0, 0),
            (0, 1, 0),
            (1, 0, 0),
            (1, 1, 0),
            (0, 0, half),
            (0, 1, half),
            (0, 2, half),
            (0, 3, half),
        )
    ]
    later = (jnp.abs(partial[0, 0, 0].astype(f32)) > 3e38).astype(jnp.int32)
    candidates = [
        lax.dynamic_slice(
            candidate_tokens,
            (0, block * tok_block + later, tenant, 0),
            (head_total, tok_block, 1, CAND),
        )[:, :, 0]
        for block, tenant in (
            (kv_at, vocab_at ^ 2),
            (kv_at, vocab_at),
            (kv_at ^ 1, vocab_at),
        )
    ]
    numbers = jnp.stack(starts + ahead).astype(jnp.int32) + later

    def rows_of(place):
        return lax.dynamic_slice_in_dim(partial, place * share, share, 1)

    summed = add_up([rows_of(seq_at)] + send_ahead(lambda j: rows_of(ahead[j])))
    keys_updated, key_flag = update_cache(
        cache_keys[0], slot_numbers, *head_blocks, rows + 1, accept_count, *candidates
    )
    activated = (jax.nn.gelu(summed[0], approximate=True) * summed[1]).astype(bf16)
    (activated,) = hold([activated], key_flag, first_part, second_part)
    ffn_out = in_order(
        [
            jnp.dot(block, down_weight, preferred_element_type=f32).astype(bf16)
            for block in collect(activated)
        ],
        ahead,
    ).reshape(groups, tok_block, width)
    ffn_out, numbers, *candidates = hold(
        [ffn_out, numbers, *candidates], first_part, second_part
    )
    ffn_out = add_up(list(lax.all_to_all(ffn_out, plane, 0, 0)))
    second_sum, inverse = add_normed(first_sum, ffn_out, norm_post_feedforward)
    normed = (second_sum * inverse * norm_final).astype(bf16)

    gathered = lax.all_gather(normed, plane, axis=0, tiled=True)
    lifted = jnp.einsum(
        "td,ndc->ntc", gathered, draft_weight, preferred_element_type=f32
    )
    lifted = lifted + draft_bias[:, None, :] * (1.0 / seq_count)
    lifted = lifted.astype(bf16).reshape(seq_count, kv_count, tenants, tok_block, -1)
    lifted = lifted.transpose(1, 0, 2, 3, 4).reshape(seq_count * groups, tok_block, -1)
    places = [("vocab", 2), (None, 0), ("kv", 1)]

    def around(values):
        return [values if axis is None else swap(values, axis, bit) for axis, bit in places]

    first_part, second_part = hold([first_part, second_part], lifted)
    core_first, core_second = swap(first_part, "vocab", 1), swap(second_part, "vocab", 1)
    core_rows = swap(vocab_weight, "vocab", 1)
    vocab_blocks = [
        [(vocab_weight, 0), (core_rows, 0)],
        [(first_part, 0), (core_first, 0)],
        [(vocab_weight, half), (core_rows, half)],
        [(second_part, 0), (core_second, 0)],
    ]
    values_updated, value_flag = update_cache(
        cache_values[0],
        slot_numbers,
        *head_blocks,
        rows + 1 + accept_count,
        accept_count,
        lifted,
    )
    everywhere = lax.all_to_all(lifted, ("kv", "seq", "vocab"), 0, 0, tiled=True)
    branch = activate_draft(everywhere, normed, kv_count, seq_count)
    (branch,) = hold([branch], core_first, core_second, core_rows, value_flag)
    heads = collect(branch)
    heads = [list(group) for group in zip(*[around(head) for head in heads])]
    tally = score_vocabulary(
        numbers, candidates, heads, vocab_blocks, half, lanes
    )
    tally = add_up(collect(tally))
    tally = lax.all_gather(tally, plane, axis=0)
    tally = tally.reshape(kv_count, tenants // 2, 2, 3, 16, lanes)
    tally = tally[:, :, :, 1] + (tally[:, ::-1, :, 0] + tally[::-1, :, :, 2])
    tally = tally[..., : CAND + 1, : head_total * tok_block]
    tally = tally.reshape(kv_count, tenants, CAND + 1, head_total, tok_block)
    log_normalizer = jnp.log(tally[:, :, 0].transpose(2, 0, 3, 1)).reshape(
        head_total, tree_size, tenants
    )
    candidate_logits = (
        tally[:, :, 1:]
        .transpose(3, 0, 4, 1, 2)
        .reshape(head_total, tree_size, tenants, CAND)
    )
    return (keys_updated[None], values_updated[None], log_normalizer, candidate_logits)


def solution(mesh):
    placed = (
        P("kv", "vocab", "seq"),
        P("seq", "kv", None),
        P("kv", None, "seq"),
        P("seq"),
        P("seq"),
        P("seq"),
        P("seq"),
        P("seq"),
        P("vocab", "seq", "kv", None),
        P("vocab", "seq", "kv", None),
        P("vocab"),
        P("vocab", None, None),
        P("vocab", None),
        P("seq", None, ("kv", "vocab")),
        P(("kv", "vocab"), "seq"),
        P(None, "seq", ("kv", "vocab")),
        P(None, ("kv", "vocab")),
        P(("kv", "seq", "vocab"), None),
        P(),
    )
    body = local if fits(mesh.shape) else local_general
    return jax.shard_map(
        body,
        mesh=mesh,
        in_specs=placed,
        out_specs=(P("vocab", "seq", "kv", None), P("vocab", "seq", "kv", None), P(), P()),
        check_vma=False,
    )
```

```python
import jax
import jax.numpy as jnp
from jax import lax
from jax.experimental import pallas as pl
from jax.experimental.pallas import tpu as pltpu
from jax.sharding import PartitionSpec as P

MODEL_WIDTH = 3584
HEAD_SIZE = 256
CAND = 8


EPSILON = 1e-06
SCORE_CAP = 50.0
LOGIT_CAP = 30.0


def apply_rotary(vectors, token_positions):
    half_dim = vectors.shape[-1] // 2
    frequency = 10000.0 ** (-2.0 * jnp.arange(half_dim, dtype=jnp.float32) / vectors.shape[-1])
    angles = token_positions.astype(jnp.float32)[..., None] * frequency
    cosine = jnp.cos(angles)
    sine_part = jnp.sin(angles)
    first_half = vectors[..., :half_dim]
    second_half = vectors[..., half_dim:]
    return jnp.concatenate(
        [
            first_half * cosine - second_half * sine_part,
            second_half * cosine + first_half * sine_part,
        ],
        axis=-1,
    )


def capped_weight(scores):
    return jnp.exp(SCORE_CAP * jnp.tanh(scores * 0.0625 / SCORE_CAP))


def row_inverse(values):
    totals = lax.psum(jnp.sum(values * values, axis=-1), "seq")
    return lax.rsqrt(totals / MODEL_WIDTH + EPSILON)[:, None]


def gated_units(gate_up, squares):
    inverse = lax.rsqrt(squares / MODEL_WIDTH + EPSILON)[:, None]
    return (
        jax.nn.gelu(gate_up[:, 0] * inverse, approximate=True) * (gate_up[:, 1] * inverse)
    ).astype(jnp.bfloat16)


def local_general(
    hidden_state,
    input_projection,
    output_projection,
    norm_pre_attention,
    norm_post_attention,
    norm_pre_feedforward,
    norm_post_feedforward,
    norm_final,
    cache_keys,
    cache_values,
    cache_length,
    ancestors,
    accepted_path,
    gate_up_weight,
    down_weight,
    draft_weight,
    draft_bias,
    vocab_weight,
    candidate_tokens,
):
    tok_block = hidden_state.shape[0]
    kv_count = lax.axis_size("kv")
    tenants = lax.axis_size("vocab")
    tree_size = tok_block * kv_count
    own_state = hidden_state[:, 0, :]
    tenant_state = lax.all_gather(own_state, "kv", axis=0, tiled=True)
    tenant_float = tenant_state.astype(jnp.float32)
    scaled_input = (tenant_float * norm_pre_attention).astype(jnp.bfloat16)
    projected_rows = jnp.einsum(
        "td,dhc->thc", scaled_input, input_projection, preferred_element_type=jnp.float32
    )
    projected_rows, squares = lax.psum(
        (projected_rows, jnp.sum(tenant_float * tenant_float, axis=-1)), "seq"
    )
    projected_rows = projected_rows * lax.rsqrt(squares / MODEL_WIDTH + EPSILON)[:, None, None]
    head_count = projected_rows.shape[1]
    depths = jnp.sum(ancestors[0], axis=-1) - 1
    length = cache_length[0]
    token_positions = length + depths
    query_rows = apply_rotary(
        projected_rows[:, :, : 2 * HEAD_SIZE].reshape(tree_size, head_count, 2, HEAD_SIZE),
        token_positions[:, None, None],
    ).astype(jnp.bfloat16)
    new_keys = apply_rotary(
        projected_rows[:, :, 2 * HEAD_SIZE : 3 * HEAD_SIZE], token_positions[:, None]
    ).astype(jnp.bfloat16)
    new_values = projected_rows[:, :, 3 * HEAD_SIZE :].astype(jnp.bfloat16)
    block_size = cache_keys.shape[1]
    block_start = lax.axis_index("seq") * block_size
    cache_cells = block_start + jnp.arange(block_size, dtype=jnp.int32)
    scores = jnp.einsum(
        "thgc,shc->thgs", query_rows, cache_keys[0], preferred_element_type=jnp.float32
    )
    weights = jnp.where((cache_cells < length)[None, None, None, :], capped_weight(scores), 0.0)
    numerator = jnp.einsum(
        "thgs,shc->thgc",
        weights.astype(jnp.bfloat16),
        cache_values[0],
        preferred_element_type=jnp.float32,
    )
    numerator, denominator = lax.psum((numerator, jnp.sum(weights, axis=-1)), "seq")
    tree_scores = jnp.einsum(
        "thgc,uhc->thgu", query_rows, new_keys, preferred_element_type=jnp.float32
    )
    tree_weights = jnp.where(ancestors[0][:, None, None, :] > 0, capped_weight(tree_scores), 0.0)
    numerator = numerator + jnp.einsum(
        "thgu,uhc->thgc",
        tree_weights.astype(jnp.bfloat16),
        new_values,
        preferred_element_type=jnp.float32,
    )
    denominator = denominator + jnp.sum(tree_weights, axis=-1)
    attended = (
        (numerator / denominator[..., None])
        .astype(jnp.bfloat16)
        .reshape(tree_size, head_count * 2 * HEAD_SIZE)
    )
    out_matrix = output_projection.reshape(head_count * 2 * HEAD_SIZE, output_projection.shape[2])
    attention_out = lax.psum_scatter(
        jnp.dot(attended, out_matrix, preferred_element_type=jnp.float32),
        "kv",
        scatter_dimension=0,
        tiled=True,
    )
    first_sum = (
        own_state.astype(jnp.float32)
        + attention_out * row_inverse(attention_out) * norm_post_attention
    ).astype(jnp.bfloat16)
    all_state = lax.all_gather(first_sum, ("kv", "vocab"), axis=0, tiled=True)
    all_float = all_state.astype(jnp.float32)
    scaled_ffn = (all_float * norm_pre_feedforward).astype(jnp.bfloat16)
    gate_up = jnp.einsum(
        "td,dcf->tcf", scaled_ffn, gate_up_weight, preferred_element_type=jnp.float32
    )
    ffn_squares = jnp.sum(all_float * all_float, axis=-1)
    gate_up, ffn_squares = lax.psum((gate_up, ffn_squares), "seq")
    activated = gated_units(gate_up, ffn_squares)
    ffn_out = lax.psum_scatter(
        jnp.dot(activated, down_weight, preferred_element_type=jnp.float32),
        ("kv", "vocab"),
        scatter_dimension=0,
        tiled=True,
    )
    first_float = first_sum.astype(jnp.float32)
    second_sum = (first_float + ffn_out * row_inverse(ffn_out) * norm_post_feedforward).astype(
        jnp.bfloat16
    )
    second_float = second_sum.astype(jnp.float32)
    normed = (second_float * row_inverse(second_float) * norm_final).astype(jnp.bfloat16)
    gathered = lax.all_gather(normed, ("kv", "vocab"), axis=0, tiled=True)
    lifted = jnp.einsum("td,ndc->tnc", gathered, draft_weight, preferred_element_type=jnp.float32)
    lifted = lax.psum(lifted.astype(jnp.bfloat16), "seq").astype(jnp.float32)
    branch = jax.nn.silu(lifted + draft_bias).astype(jnp.bfloat16)
    row_count = gathered.shape[0]
    vocab_rows = vocab_weight.shape[0]
    draft_count = branch.shape[1]
    columns = vocab_weight
    base_logits = lax.dot_general(
        lax.all_gather(gathered, "seq", axis=1, tiled=True),
        columns,
        (((1,), (1,)), ((), ())),
        preferred_element_type=jnp.float32,
    )
    columns = vocab_weight
    draft_extra = jnp.einsum(
        "tnc,vc->tnv",
        lax.all_gather(branch, ("kv", "vocab"), axis=2, tiled=True),
        columns,
        preferred_element_type=jnp.float32,
    )
    raw_logits = jnp.concatenate(
        [base_logits[:, None, :], base_logits[:, None, :] + draft_extra], axis=1
    )
    logits = LOGIT_CAP * jnp.tanh(raw_logits / LOGIT_CAP)
    totals = jnp.sum(jnp.exp(logits), axis=-1)
    head_total = draft_count + 1
    candidates = candidate_tokens.reshape(head_total, kv_count, tok_block, tenants, CAND)
    candidates = jnp.transpose(candidates, (0, 1, 3, 2, 4)).reshape(head_total, row_count, CAND)
    candidates = jnp.transpose(candidates, (1, 0, 2))
    vocab_start = lax.axis_index(("kv", "seq", "vocab")) * vocab_rows
    local_tokens = candidates - vocab_start
    entry_index = jnp.arange(vocab_rows, dtype=jnp.int32)
    picked = jnp.stack(
        [
            jnp.sum(
                jnp.where(entry_index == local_tokens[:, :, column : column + 1], logits, 0.0),
                axis=-1,
            )
            for column in range(CAND)
        ],
        axis=-1,
    )
    totals, picked = lax.psum((totals, picked), ("kv", "seq", "vocab"))
    log_totals = jnp.transpose(jnp.log(totals)).reshape(head_total, kv_count, tenants, tok_block)
    log_normalizer = jnp.transpose(log_totals, (0, 1, 3, 2)).reshape(head_total, tree_size, tenants)
    picked = jnp.transpose(picked, (1, 0, 2)).reshape(
        head_total, kv_count, tenants, tok_block, CAND
    )
    candidate_logits = jnp.transpose(picked, (0, 1, 3, 2, 4)).reshape(
        head_total, tree_size, tenants, CAND
    )
    accept_count = accepted_path.shape[1]
    slot_rows = length + jnp.arange(accept_count, dtype=jnp.int32)
    tree_nodes = jnp.arange(tree_size, dtype=jnp.int32)
    matches = (cache_cells[:, None, None] == slot_rows[None, :, None]) & (
        accepted_path[0][None, :, None] == tree_nodes[None, None, :]
    )
    selector = jnp.sum(matches.astype(jnp.float32), axis=1)
    written = jnp.sum(selector, axis=-1) > 0.0
    selector = selector.astype(jnp.bfloat16)

    def write_path(old_block, fresh_rows):
        moved_rows = jnp.dot(
            selector, fresh_rows.reshape(tree_size, -1), preferred_element_type=jnp.float32
        ).astype(jnp.bfloat16)
        return jnp.where(
            written[:, None], moved_rows, old_block[0].reshape(block_size, -1)
        ).reshape(old_block.shape)

    keys_updated = write_path(cache_keys, new_keys)
    values_updated = write_path(cache_values, new_values)
    return (keys_updated, values_updated, log_normalizer, candidate_logits)


def fits(sizes):
    return sizes["kv"] == 2 and sizes["vocab"] == 4 and sizes["seq"] == 4


def send_ahead(pick):
    count = lax.axis_size("seq")
    return [
        lax.ppermute(pick(j), "seq", [(i, (i + j) % count) for i in range(count)])
        for j in range(1, count)
    ]


def collect(block):
    count = lax.axis_size("seq")
    return [block] + [
        lax.ppermute(block, "seq", [(i, (i - j) % count) for i in range(count)])
        for j in range(1, count)
    ]


def in_order(blocks, ahead):
    result = jnp.zeros((len(blocks),) + blocks[0].shape, blocks[0].dtype)
    for j, block in enumerate(blocks):
        result = lax.dynamic_update_index_in_dim(result, block, ahead[j], 0)
    return result


def add_up(blocks):
    total = blocks[0].astype(jnp.float32)
    for block in blocks[1:]:
        total = total + block.astype(jnp.float32)
    return total


def swap(values, axis, bit):
    count = lax.axis_size(axis)
    return lax.ppermute(values, axis, [(i, i ^ bit) for i in range(count)])


def split_lanes(values):
    high = values.astype(jnp.bfloat16)
    low = (values - high.astype(jnp.float32)).astype(jnp.bfloat16)
    shape = values.shape[:-1] + (64,)
    return jnp.concatenate([jnp.broadcast_to(high, shape), jnp.broadcast_to(low, shape)], axis=-1)


def hold(values, *events):
    count = len(values)
    anywhere = pl.BlockSpec(memory_space=pl.ANY)
    return pl.pallas_call(
        lambda *refs: None,
        out_shape=[jax.ShapeDtypeStruct(value.shape, value.dtype) for value in values],
        in_specs=[anywhere] * (count + len(events)),
        out_specs=[anywhere] * count,
        input_output_aliases={k: k for k in range(count)},
    )(*values, *events)


def inverse_of(totals):
    return lax.rsqrt(totals / MODEL_WIDTH + EPSILON)


def rotate(vectors, cosine, sine):
    half = vectors.shape[-1] // 2
    first, second = vectors[..., :half], vectors[..., half:]
    return jnp.concatenate(
        [first * cosine - second * sine, second * cosine + first * sine], axis=-1
    )


def copy_rows(sources, targets, *events):
    unit = 64
    number = len(sources)
    shapes = [
        (sum(rows for _, _, rows in parts),) + sources[0].shape[1:] for parts in targets
    ]
    moves = []
    for t, parts in enumerate(targets):
        filled = 0
        for source, first, rows in parts:
            for p in range(0, rows, unit):
                size = min(unit, rows - p)
                moves.append((source, first + p, t, filled + p, size))
            filled += rows

    def kernel(*refs):
        inputs, rest = refs[:number], refs[number + len(events) :]
        outputs, (held, get, put) = rest[: len(shapes)], rest[len(shapes) :]
        pairs = []
        for k, (source, first, target, place, size) in enumerate(moves):
            slot = held.at[k, pl.ds(0, size)]
            pairs.append(
                (
                    pltpu.make_async_copy(
                        inputs[source].at[pl.ds(first, size)], slot, get.at[k]
                    ),
                    pltpu.make_async_copy(
                        slot, outputs[target].at[pl.ds(place, size)], put.at[k]
                    ),
                )
            )
        for k, (inward, _) in enumerate(pairs):
            inward.start(priority=k % 2)
        for k, (inward, outward) in enumerate(pairs):
            inward.wait()
            outward.start(priority=k % 2)
        for _, outward in pairs:
            outward.wait()

    row = sources[0].shape[1:]
    dtype = sources[0].dtype
    return pl.pallas_call(
        kernel,
        out_shape=[jax.ShapeDtypeStruct(shape, dtype) for shape in shapes],
        in_specs=[pl.BlockSpec(memory_space=pl.ANY)] * (number + len(events)),
        out_specs=[pl.BlockSpec(memory_space=pltpu.HBM)] * len(shapes),
        scratch_shapes=[
            pltpu.VMEM((len(moves), unit) + row, dtype),
            pltpu.SemaphoreType.DMA((len(moves),)),
            pltpu.SemaphoreType.DMA((len(moves),)),
        ],
        compiler_params=pltpu.CompilerParams(vmem_limit_bytes=58 * 2**20),
        cost_estimate=pl.CostEstimate(
            flops=0,
            bytes_accessed=sum(4 * shape[0] * shape[1] for shape in shapes),
            transcendentals=0,
        ),
    )(*sources, *events)


def update_cache(cache, numbers, packed, arrived, first_row, accept, *events):
    slots, heads, size = cache.shape
    count = 1 + len(arrived)
    tail = pl.ds(packed.shape[1] - 16, 16)
    first_row = first_row - (packed.shape[1] - 16)
    piece = 256
    parts = slots // piece

    def kernel(numbers_ref, source, packed_ref, *rest):
        arrived_refs, rest = rest[: count - 1], rest[count - 1 + len(events) :]
        target, flag, held, tails, stage, ready, get, put, sem = rest
        flag[...] = jnp.zeros_like(flag)

        tail_copies = []
        for j in range(count):
            head = lax.rem(numbers_ref[1] + (count - j), count)
            block = packed_ref.at[0, tail] if j == 0 else arrived_refs[j - 1].at[tail]
            tail_copies.append(pltpu.make_async_copy(block, tails.at[head], sem.at[j]))
            tail_copies[j].start()
        pairs = []
        for k in range(parts):
            window = pl.ds(k * piece, piece)
            pairs.append(
                (
                    pltpu.make_async_copy(source.at[window], held.at[k], get.at[k]),
                    pltpu.make_async_copy(held.at[k], target.at[window], put.at[k]),
                )
            )
        for k, (inward, _) in enumerate(pairs):
            inward.start(priority=k % 2)
        for k, (inward, outward) in enumerate(pairs):
            inward.wait()
            outward.start(priority=k % 2)
        for copy in tail_copies:
            copy.wait()
        for head in range(count):
            rows = tails[head].astype(jnp.float32)
            for r in range(accept):
                stage[r, head : head + 1, :] = rows[first_row + r : first_row + r + 1]
        ready[...] = stage[...].astype(ready.dtype)
        for _, outward in pairs:
            outward.wait()
        for a in range(accept):
            slot = numbers_ref[0] + a

            @pl.when((slot >= 0) & (slot < slots))
            def _():
                copy = pltpu.make_async_copy(
                    ready.at[pl.ds(a, 1)], target.at[pl.ds(slot, 1)], sem.at[0]
                )
                copy.start()
                copy.wait()

    return pl.pallas_call(
        kernel,
        out_shape=(
            jax.ShapeDtypeStruct(cache.shape, cache.dtype),
            jax.ShapeDtypeStruct((8, 128), jnp.float32),
        ),
        in_specs=[
            pl.BlockSpec(memory_space=pltpu.SMEM),
            pl.BlockSpec(memory_space=pltpu.HBM),
        ]
        + [pl.BlockSpec(memory_space=pl.ANY)] * (count + len(events)),
        out_specs=(
            pl.BlockSpec(memory_space=pltpu.HBM),
            pl.BlockSpec(memory_space=pltpu.VMEM),
        ),
        scratch_shapes=[
            pltpu.VMEM((parts, piece, heads, size), cache.dtype),
            pltpu.VMEM((count, 16, size), cache.dtype),
            pltpu.VMEM((accept, heads, size), jnp.float32),
            pltpu.VMEM((accept, heads, size), cache.dtype),
            pltpu.SemaphoreType.DMA((parts,)),
            pltpu.SemaphoreType.DMA((parts,)),
            pltpu.SemaphoreType.DMA((count,)),
        ],
        compiler_params=pltpu.CompilerParams(vmem_limit_bytes=56 * 2**20),
        cost_estimate=pl.CostEstimate(
            flops=0, bytes_accessed=4 * cache.size, transcendentals=0
        ),
    )(numbers, cache, packed, *arrived, *events)


def score_vocabulary(numbers, candidates, heads, vocab_blocks, half, lanes):
    tokens = heads[0][0].shape[0]
    count = len(heads[0])
    groups = len(heads)
    parts = [part for block in vocab_blocks for part in block]
    arrays = []
    for array, _ in parts:
        if not any(array is known for known in arrays):
            arrays.append(array)
    blocks, extent, width = len(vocab_blocks), 2 * half, arrays[0].shape[1]
    share = width // count
    unit = 64
    inputs = [head for group in heads for head in group]

    def kernel(numbers_ref, *rest):
        candidate_refs, rest = rest[:groups], rest[groups:]
        vectors, rest = rest[: len(inputs)], rest[len(inputs) :]
        sources, rest = rest[: len(arrays)], rest[len(arrays) :]
        out_ref, held, arrived, wide, narrow, square, row_sems, sems = rest
        arrivals = []
        for k, vector in enumerate(vectors):
            arrivals.append(pltpu.make_async_copy(vector, arrived.at[k], sems.at[k]))
            arrivals[k].start(priority=0)
        def fetch(b):
            for k in (2 * b, 2 * b + 1):
                array, first = parts[k]
                source = sources[[array is known for known in arrays].index(True)]
                for q, p in enumerate(range(0, half, unit)):
                    pltpu.make_async_copy(
                        source.at[pl.ds(first + p, unit)],
                        held.at[b, pl.ds(k % 2 * half + p, unit)],
                        row_sems.at[b],
                    ).start(priority=1)

        fetch(0)
        fetch(1)
        fetch(2)
        fetch(3)
        spare = lanes - (count + 1) * tokens
        wanted = []
        for group, ref in enumerate(candidate_refs):
            square[...] = jnp.full((lanes, 128), -1, jnp.int32)
            square[0:tokens, 0:CAND] = ref[0]
            for j in range(count):
                row_at = (j + 1) * tokens
                square[row_at : row_at + tokens, 0:CAND] = ref[numbers_ref[2 * blocks + j] + 1]
            wanted.append(square[...].T[0:CAND])
        def assemble(group):
            for j in range(count):
                arrivals[group * count + j].wait()
                columns = pl.ds(pl.multiple_of(numbers_ref[2 * blocks + j] * share, 128), share)
                wide[group * tokens : (group + 1) * tokens, columns] = arrived[
                    group * count + j, :, width:
                ].astype(jnp.float32)
            pieces = [wide[group * tokens : (group + 1) * tokens, :]]
            pieces += [arrived[group * count + j, :, :width].astype(jnp.float32) for j in range(count)]
            pieces += [jnp.zeros((spare, width), jnp.float32)]
            narrow[group * lanes : (group + 1) * lanes, :] = jnp.concatenate(
                pieces, axis=0
            ).astype(narrow.dtype)
        assemble(0)
        assemble(1)
        lane = lax.broadcasted_iota(jnp.int32, (half, lanes), 1)
        row = lax.broadcasted_iota(jnp.int32, (half, lanes), 0)
        out_ref[...] = jnp.zeros_like(out_ref)

        def step(b, low):
            pltpu.make_async_copy(held.at[b], held.at[b], row_sems.at[b]).wait()
            both = lax.dot_general(
                held[b],
                narrow[low * lanes : (low + 2) * lanes, :],
                (((1,), (1,)), ((), ())),
                preferred_element_type=jnp.float32,
            )
            for group in (low, low + 1):
                place = slice((group - low) * lanes, (group - low + 1) * lanes)
                for part in range(2):
                    raw = both[part * half : (part + 1) * half, place]
                    entry = row + numbers_ref[2 * b + part]
                    first = jnp.where(lane < tokens, raw, 0.0)
                    for head in range(1, count + 1):
                        raw = raw + pltpu.roll(first, head * tokens, 1)
                    logits = LOGIT_CAP * jnp.tanh(raw / LOGIT_CAP)
                    tally = [jnp.sum(jnp.exp(logits), axis=0, keepdims=True)]
                    for c in range(CAND):
                        match = entry == wanted[group][c : c + 1]
                        tally.append(
                            jnp.sum(jnp.where(match, logits, 0.0), axis=0, keepdims=True)
                        )
                    out_ref[16 * group : 16 * group + CAND + 1, :] += jnp.concatenate(tally, axis=0)

        for low in range(2):
            if low == 1:
                assemble(2)

            def run(b, carry, low=low):
                step(b, low)
                return carry

            middle = blocks // 2
            lax.fori_loop(low * middle, (low + 1) * middle, run, 0)
        turn = numbers_ref[2 * blocks] * tokens
        across = lax.broadcasted_iota(jnp.int32, out_ref.shape, 1)
        values = out_ref[...]
        ahead = pltpu.roll(values, turn, 1)
        wrapped = pltpu.roll(values, turn + lanes - count * tokens, 1)
        turned = jnp.where(across - turn >= tokens, ahead, wrapped)
        out_ref[...] = jnp.where(across < tokens, values, turned)

    return pl.pallas_call(
        kernel,
        out_shape=jax.ShapeDtypeStruct((16 * groups, lanes), jnp.float32),
        in_specs=[pl.BlockSpec(memory_space=pltpu.SMEM)]
        + [pl.BlockSpec(memory_space=pltpu.VMEM)] * groups
        + [pl.BlockSpec(memory_space=pl.ANY)] * (len(inputs) + len(arrays)),
        out_specs=pl.BlockSpec(memory_space=pltpu.VMEM),
        scratch_shapes=[
            pltpu.VMEM((blocks, extent, width), inputs[0].dtype),
            pltpu.VMEM((len(inputs),) + inputs[0].shape, inputs[0].dtype),
            pltpu.VMEM((groups * tokens, width), jnp.float32),
            pltpu.VMEM((groups * lanes, width), inputs[0].dtype),
            pltpu.VMEM((lanes, 128), jnp.int32),
            pltpu.SemaphoreType.DMA((blocks,)),
            pltpu.SemaphoreType.DMA((len(inputs),)),
        ],
        compiler_params=pltpu.CompilerParams(vmem_limit_bytes=58 * 2**20),
        cost_estimate=pl.CostEstimate(
            flops=4 * blocks * extent * width * lanes,
            bytes_accessed=2 * blocks * extent * width,
            transcendentals=4 * blocks * extent * lanes,
        ),
    )(numbers, *candidates, *inputs, *arrays)


def activate_draft(parts, normed, kv_count, seq_count):
    number, tokens, columns = parts.shape
    tenants = number // (kv_count * seq_count)
    width = kv_count * tenants * columns

    def kernel(parts_ref, normed_ref, out_ref):
        pair = []
        for kv in range(kv_count):
            for tenant in range(tenants):
                total = 0.0
                for seq in range(seq_count):
                    block = parts_ref[(seq * kv_count + kv) * tenants + tenant]
                    total = total + block.astype(jnp.float32)
                pair.append(total / (1.0 + jnp.exp(-total)))
                if len(pair) == 2:
                    place = (kv * tenants + tenant - 1) * columns
                    out_ref[:, place : place + 2 * columns] = jnp.concatenate(
                        pair, axis=1
                    ).astype(out_ref.dtype)
                    pair = []
        out_ref[:, width:] = normed_ref[...]

    vmem = pl.BlockSpec(memory_space=pltpu.VMEM)
    return pl.pallas_call(
        kernel,
        out_shape=jax.ShapeDtypeStruct((tokens, width + normed.shape[1]), normed.dtype),
        in_specs=[vmem] * 2,
        out_specs=vmem,
    )(parts, normed)


def project_in(rows, weight):
    tokens, depth = rows.shape
    _, heads, columns = weight.shape
    unit = 128

    def kernel(rows_ref, weight_ref, out_ref, spread, total):
        source = lax.broadcasted_iota(jnp.int32, (unit, unit * heads), 0)
        place = lax.broadcasted_iota(jnp.int32, (unit, unit * heads), 1)
        for h in range(heads):
            spread[h] = jnp.where(place == source * heads + h, 1.0, 0.0).astype(rows.dtype)
        total[...] = jnp.zeros_like(total)
        for k in range(depth // unit):
            block = rows_ref[:, k * unit : (k + 1) * unit]
            wide = jnp.concatenate(
                [
                    jnp.dot(block, spread[h], preferred_element_type=jnp.float32)
                    for h in range(heads)
                ],
                axis=0,
            ).astype(rows.dtype)
            total[...] += jnp.dot(
                wide,
                weight_ref[k * unit : (k + 1) * unit].reshape(unit * heads, columns),
                preferred_element_type=jnp.float32,
            )
        for h in range(heads):
            out_ref[h] = total[h * tokens : (h + 1) * tokens, :].astype(out_ref.dtype)

    vmem = pl.BlockSpec(memory_space=pltpu.VMEM)
    return pl.pallas_call(
        kernel,
        out_shape=jax.ShapeDtypeStruct((heads, tokens, columns), rows.dtype),
        in_specs=[vmem] * 2,
        out_specs=vmem,
        scratch_shapes=[
            pltpu.VMEM((heads, unit, unit * heads), rows.dtype),
            pltpu.VMEM((heads * tokens, columns), jnp.float32),
        ],
        compiler_params=pltpu.CompilerParams(vmem_limit_bytes=24 * 2**20),
        cost_estimate=pl.CostEstimate(
            flops=2 * heads * tokens * weight.size,
            bytes_accessed=2 * weight.size,
            transcendentals=0,
        ),
    )(rows, weight)


def project_out(places, attended, weight, own_rows):
    rows = attended[0].shape[0] // 2
    size = attended[0].shape[1]
    count, _, width = weight.shape

    def kernel(places_ref, *refs):
        blocks, (weight_ref, theirs_ref, own_ref) = refs[:count], refs[count:]
        total = jnp.zeros((rows, width), jnp.float32)
        for j, block in enumerate(blocks):
            for g in range(2):
                total = total + jnp.dot(
                    block[g * rows : (g + 1) * rows, :],
                    weight_ref[places_ref[j], g * size : (g + 1) * size, :],
                    preferred_element_type=jnp.float32,
                )
        own_ref[...] = total[:own_rows]
        theirs_ref[...] = total[own_rows:].astype(theirs_ref.dtype)

    vmem = pl.BlockSpec(memory_space=pltpu.VMEM)
    return pl.pallas_call(
        kernel,
        out_shape=[
            jax.ShapeDtypeStruct((rows - own_rows, width), attended[0].dtype),
            jax.ShapeDtypeStruct((own_rows, width), jnp.float32),
        ],
        in_specs=[pl.BlockSpec(memory_space=pltpu.SMEM)] + [vmem] * (count + 1),
        out_specs=[vmem] * 2,
        compiler_params=pltpu.CompilerParams(vmem_limit_bytes=16 * 2**20),
        cost_estimate=pl.CostEstimate(
            flops=2 * rows * weight.size, bytes_accessed=2 * weight.size, transcendentals=0
        ),
    )(places, *attended, weight)


def local(
    hidden_state,
    input_projection,
    output_projection,
    norm_pre_attention,
    norm_post_attention,
    norm_pre_feedforward,
    norm_post_feedforward,
    norm_final,
    cache_keys,
    cache_values,
    cache_length,
    ancestors,
    accepted_path,
    gate_up_weight,
    down_weight,
    draft_weight,
    draft_bias,
    vocab_weight,
    candidate_tokens,
):
    f32, bf16 = jnp.float32, jnp.bfloat16
    plane = ("kv", "vocab")
    tok_block, _, width = hidden_state.shape
    seq_count = lax.axis_size("seq")
    kv_count = lax.axis_size("kv")
    tenants = lax.axis_size("vocab")
    groups = kv_count * tenants
    tree_size = tok_block * kv_count
    row_count = tok_block * groups
    seq_at = lax.axis_index("seq")
    kv_at = lax.axis_index("kv")
    vocab_at = lax.axis_index("vocab")
    ahead = [(seq_at + j) % seq_count for j in range(seq_count)]
    own_state = hidden_state[:, 0, :]

    tenant_state = jnp.concatenate([own_state, swap(own_state, "kv", 1)], axis=0)
    vocab_rows = vocab_weight.shape[0]
    half = vocab_rows // 2

    tenant_float = tenant_state.astype(f32)
    scaled_input = (tenant_float * norm_pre_attention).astype(bf16)
    projected = project_in(scaled_input, input_projection)
    square_lanes = split_lanes(jnp.sum(tenant_float * tenant_float, axis=-1, keepdims=True))
    head_count = projected.shape[0]
    pair = 2 * HEAD_SIZE
    packed = jnp.concatenate(
        [
            projected,
            jnp.broadcast_to(square_lanes, (head_count,) + square_lanes.shape),
        ],
        axis=-1,
    )
    arrived = send_ahead(lambda j: lax.dynamic_index_in_dim(packed, ahead[j], 0, False))
    summed = add_up([lax.dynamic_index_in_dim(packed, seq_at, 0, False)] + arrived)
    whole = 2 * pair
    inverse = inverse_of(summed[:, whole : whole + 1] + summed[:, whole + 64 : whole + 65])
    tree_mask = ancestors[0]
    tree_mask = jnp.where(
        kv_at == 0, tree_mask, jnp.roll(tree_mask, (tok_block, tok_block), (0, 1))
    )
    length = cache_length[0]
    depths = jnp.sum(tree_mask, axis=-1, keepdims=True) - 1
    frequency = 10000.0 ** (
        -2.0 * jnp.arange(HEAD_SIZE // 2, dtype=f32) / HEAD_SIZE
    )
    angles = (length + depths).astype(f32) * frequency
    cosine, sine = jnp.cos(angles), jnp.sin(angles)
    query_rows = jnp.concatenate(
        [
            rotate(summed[:, :HEAD_SIZE] * inverse, cosine, sine),
            rotate(summed[:, HEAD_SIZE:pair] * inverse, cosine, sine),
        ],
        axis=0,
    ).astype(bf16)
    all_queries = in_order(collect(query_rows), ahead)
    new_keys = rotate(summed[:, pair : pair + HEAD_SIZE] * inverse, cosine, sine).astype(bf16)
    new_values = (summed[:, pair + HEAD_SIZE : whole] * inverse).astype(bf16)

    block_size = cache_keys.shape[1]
    block_start = seq_at * block_size
    cache_cells = block_start + jnp.arange(block_size, dtype=jnp.int32)
    scores = jnp.einsum("hrc,shc->hrs", all_queries, cache_keys[0], preferred_element_type=f32)
    weights = jnp.where((cache_cells < length)[None, None, :], capped_weight(scores), 0.0)
    numerator = jnp.einsum(
        "hrs,shc->hrc", weights.astype(bf16), cache_values[0], preferred_element_type=f32
    )
    rows = 2 * tree_size
    sums = jnp.sum(weights, axis=-1)
    sums_high = sums.astype(bf16)
    sums_low = (sums - sums_high.astype(f32)).astype(bf16)
    sums = jnp.concatenate(
        [sums_high, sums_low, jnp.zeros((head_count, HEAD_SIZE - 2 * rows), bf16)], axis=-1
    )
    node_at = jnp.arange(tree_size, dtype=jnp.int32)
    node_at = jnp.where(kv_at == 0, node_at, (node_at + tok_block) % tree_size)
    accept_pick = (accepted_path[0][:, None] == node_at[None, :]).astype(bf16)
    accept_count = accept_pick.shape[0]
    chosen = jnp.concatenate(
        [
            jnp.dot(accept_pick, fresh_part, preferred_element_type=f32).astype(bf16)
            for fresh_part in (new_keys, new_values)
        ],
        axis=0,
    )
    packed = jnp.concatenate(
        [
            numerator.astype(bf16),
            sums[:, None, :],
            jnp.broadcast_to(chosen, (head_count,) + chosen.shape),
            jnp.zeros((head_count, 15 - 2 * accept_count, HEAD_SIZE), bf16),
        ],
        axis=1,
    )
    arrived = send_ahead(lambda j: lax.dynamic_index_in_dim(packed, ahead[j], 0, False))
    tree_scores = lax.dot_general(
        query_rows, new_keys, (((1,), (1,)), ((), ())), preferred_element_type=f32
    )
    seen = jnp.concatenate([tree_mask, tree_mask], axis=0) > 0
    tree_weights = jnp.where(seen, capped_weight(tree_scores), 0.0)
    tree_numerator = jnp.dot(tree_weights.astype(bf16), new_values, preferred_element_type=f32)
    tree_sums = jnp.sum(tree_weights, axis=-1, keepdims=True)
    head_blocks = (packed, arrived)
    summed = add_up([lax.dynamic_index_in_dim(packed, seq_at, 0, False)] + arrived)
    denominator = (summed[rows, :rows] + summed[rows, rows : 2 * rows])[:, None] + tree_sums
    attended = ((summed[:rows] + tree_numerator) / denominator).astype(bf16)
    theirs, attention_out = project_out(
        jnp.stack(ahead).astype(jnp.int32),
        collect(attended),
        output_projection,
        tok_block,
    )
    first_part, second_part = copy_rows(
        [vocab_weight],
        [[(0, 0, half)], [(0, half, vocab_rows - half)]],
        theirs,
    )
    (theirs,) = hold([swap(theirs, "kv", 1)], first_part, second_part)
    attention_out = attention_out + theirs.astype(f32)

    def token_totals(*values):
        lanes = 128 // len(values)
        columns = [jnp.sum(value, axis=-1, keepdims=True) for value in values]
        columns = jnp.concatenate(
            [jnp.broadcast_to(column, (tok_block, lanes)) for column in columns], axis=-1
        )
        columns = add_up(collect(columns))
        return [columns[:, k * lanes : k * lanes + 1] for k in range(len(values))]

    own_float = own_state.astype(f32)

    def add_normed(state, update, gain):
        scaled = update * gain
        update_total, state_total, cross_total, scaled_total = token_totals(
            update * update, state * state, state * scaled, scaled * scaled
        )
        inverse = inverse_of(update_total)
        total = state_total + inverse * (2.0 * cross_total + inverse * scaled_total)
        return state + scaled * inverse, inverse_of(jnp.maximum(total, 0.0))

    first_sum, inverse = add_normed(own_float, attention_out, norm_post_attention)
    scaled_ffn = (first_sum * inverse * norm_pre_feedforward).astype(bf16)

    scaled_ffn = lax.all_gather(scaled_ffn, plane, axis=0, tiled=True)
    share = row_count // seq_count
    units = down_weight.shape[0]
    partial = jnp.einsum(
        "td,dcf->ctf", scaled_ffn, gate_up_weight, preferred_element_type=f32
    ).astype(bf16)

    first_part, second_part = hold([first_part, second_part], scaled_ffn)
    first_part, second_part = swap(first_part, "kv", 1), swap(second_part, "vocab", 2)
    slot_numbers = jnp.stack([length - block_start, seq_at])
    head_total = seq_count + 1
    lanes = 128
    starts = [
        (((kv_at ^ kv_bit) * seq_count + seq_at) * tenants + (vocab_at ^ vocab_bit)) * vocab_rows
        + first
        for kv_bit, vocab_bit, first in (
            (0, 0, 0),
            (0, 1, 0),
            (1, 0, 0),
            (1, 1, 0),
            (0, 0, half),
            (0, 1, half),
            (0, 2, half),
            (0, 3, half),
        )
    ]
    later = (jnp.abs(partial[0, 0, 0].astype(f32)) > 3e38).astype(jnp.int32)
    candidates = [
        lax.dynamic_slice(
            candidate_tokens,
            (0, block * tok_block + later, tenant, 0),
            (head_total, tok_block, 1, CAND),
        )[:, :, 0]
        for block, tenant in (
            (kv_at, vocab_at ^ 2),
            (kv_at, vocab_at),
            (kv_at ^ 1, vocab_at),
        )
    ]
    numbers = jnp.stack(starts + ahead).astype(jnp.int32) + later

    def rows_of(place):
        return lax.dynamic_slice_in_dim(partial, place * share, share, 1)

    summed = add_up([rows_of(seq_at)] + send_ahead(lambda j: rows_of(ahead[j])))
    keys_updated, key_flag = update_cache(
        cache_keys[0], slot_numbers, *head_blocks, rows + 1, accept_count, *candidates
    )
    activated = (jax.nn.gelu(summed[0], approximate=True) * summed[1]).astype(bf16)
    (activated,) = hold([activated], key_flag, first_part, second_part)
    ffn_out = in_order(
        [
            jnp.dot(block, down_weight, preferred_element_type=f32).astype(bf16)
            for block in collect(activated)
        ],
        ahead,
    ).reshape(groups, tok_block, width)
    ffn_out, numbers, *candidates = hold(
        [ffn_out, numbers, *candidates], first_part, second_part
    )
    ffn_out = add_up(list(lax.all_to_all(ffn_out, plane, 0, 0)))
    second_sum, inverse = add_normed(first_sum, ffn_out, norm_post_feedforward)
    normed = (second_sum * inverse * norm_final).astype(bf16)

    gathered = lax.all_gather(normed, plane, axis=0, tiled=True)
    lifted = jnp.einsum(
        "td,ndc->ntc", gathered, draft_weight, preferred_element_type=f32
    )
    lifted = lifted + draft_bias[:, None, :] * (1.0 / seq_count)
    lifted = lifted.astype(bf16).reshape(seq_count * groups, tok_block, -1)
    places = [("vocab", 2), (None, 0), ("kv", 1)]

    def around(values):
        return [values if axis is None else swap(values, axis, bit) for axis, bit in places]

    first_part, second_part = hold([first_part, second_part], lifted)
    core_first, core_second = swap(first_part, "vocab", 1), swap(second_part, "vocab", 1)
    core_rows = swap(vocab_weight, "vocab", 1)
    vocab_blocks = [
        [(vocab_weight, 0), (core_rows, 0)],
        [(first_part, 0), (core_first, 0)],
        [(vocab_weight, half), (core_rows, half)],
        [(second_part, 0), (core_second, 0)],
    ]
    values_updated, value_flag = update_cache(
        cache_values[0],
        slot_numbers,
        *head_blocks,
        rows + 1 + accept_count,
        accept_count,
        lifted,
    )
    everywhere = lax.all_to_all(lifted, ("seq", "kv", "vocab"), 0, 0, tiled=True)
    branch = activate_draft(everywhere, normed, kv_count, seq_count)
    (branch,) = hold([branch], core_first, core_second, core_rows, value_flag)
    heads = collect(branch)
    heads = [list(group) for group in zip(*[around(head) for head in heads])]
    tally = score_vocabulary(
        numbers, candidates, heads, vocab_blocks, half, lanes
    )
    tally = add_up(collect(tally))
    tally = lax.all_gather(tally, plane, axis=0)
    tally = tally.reshape(kv_count, tenants // 2, 2, 3, 16, lanes)
    tally = tally[:, :, :, 1] + (tally[:, ::-1, :, 0] + tally[::-1, :, :, 2])
    tally = tally[..., : CAND + 1, : head_total * tok_block]
    tally = tally.reshape(kv_count, tenants, CAND + 1, head_total, tok_block)
    log_normalizer = jnp.log(tally[:, :, 0].transpose(2, 0, 3, 1)).reshape(
        head_total, tree_size, tenants
    )
    candidate_logits = (
        tally[:, :, 1:]
        .transpose(3, 0, 4, 1, 2)
        .reshape(head_total, tree_size, tenants, CAND)
    )
    return (keys_updated[None], values_updated[None], log_normalizer, candidate_logits)


def solution(mesh):
    placed = (
        P("kv", "vocab", "seq"),
        P("seq", "kv", None),
        P("kv", None, "seq"),
        P("seq"),
        P("seq"),
        P("seq"),
        P("seq"),
        P("seq"),
        P("vocab", "seq", "kv", None),
        P("vocab", "seq", "kv", None),
        P("vocab"),
        P("vocab", None, None),
        P("vocab", None),
        P("seq", None, ("kv", "vocab")),
        P(("kv", "vocab"), "seq"),
        P(None, "seq", ("kv", "vocab")),
        P(None, ("kv", "vocab")),
        P(("kv", "seq", "vocab"), None),
        P(),
    )
    body = local if fits(mesh.shape) else local_general
    return jax.shard_map(
        body,
        mesh=mesh,
        in_specs=placed,
        out_specs=(P("vocab", "seq", "kv", None), P("vocab", "seq", "kv", None), P(), P()),
        check_vma=False,
    )
```
